32 devices in a mesh: ctx: 8 (over z, x), ch: 4 (over y, core).
Axes of the slice: x: 2, y: 2, z: 4, core: 2. Of those that a mesh axis runs over, the one named last changes fastest.
Arguments:
- queries: bfloat16 [1024, 8192], P('ctx', 'ch'), may hold values from -6 to 6
- keys: bfloat16 [1024, 8192], P('ctx', 'ch'), may hold values from -6 to 6
- values: bfloat16 [1024, 8192], P('ctx', 'ch'), may hold values from -6 to 6
- short_taps: float32 [3, 7, 8192], P(None, None, 'ch'), may hold values from -2 to 2
- residues: float32 [512, 16], P('ch'), may hold values from -1.5 to 1.5
- decay_rate: float32 [512, 16], P('ch'), may hold values from 0.0001953125 to 0.03125
- out_gain: float32 [8192], P('ch'), may hold values from 0.5 to 1.5
- doc_lengths: int32 [16], replicated, may hold values from 1 to 512, 1024 in all
- upstream: bfloat16 [1024, 8192], P('ctx', 'ch'), may hold values from -6 to 6
Outputs:
- mixed_out: bfloat16 [1024, 8192], P('ctx', 'ch')
- d_queries: bfloat16 [1024, 8192], P('ctx', 'ch')
- d_keys: bfloat16 [1024, 8192], P('ctx', 'ch')
- d_values: bfloat16 [1024, 8192], P('ctx', 'ch')
- d_taps: float32 [3, 7, 8192], P(None, None, 'ch')
- d_residues: float32 [512, 16], P('ch')
- d_rate: float32 [512, 16], P('ch')
- d_gain: float32 [8192], P('ch')
The draws below stay inside these ranges and needn't reach their ends.
Inputs may be any that keep to these rules, and one draw needn't show every extreme that they name: `doc_lengths`: the lengths sum to 1024, and one document is exactly 512 positions long.
All inputs are finite; a program needn't handle non-finite values.
Results may differ from the reference program's by a relative error of at most 0.01.
Values may be sent and summed in bfloat16 or wider, within the bound.
No kernel may reach another device: no remote copies, remote signals or barrier semaphores. Data moves between devices by JAX's collectives and lax.ppermute only.
A program may use at most 192 MiB of HBM per device.

```python
import math
import jax
import jax.numpy as jnp
import numpy as np
from jax import lax

D = 8192
GROUP = 16
MODES = 16
TAPS = 7
NDOC = 16
TOK_DEV = 128
TOKENS = 1024
NGROUPS = 512


def levels(rng, dims, shards, low, top_value):
    loudness, own = 1.0, jax.random.fold_in(rng, 6)
    for dim, parts in shards:
        heights = jnp.exp(jax.random.uniform(jax.random.fold_in(own, dim), (parts,), jnp.float32, low / len(shards), top_value / len(shards)))
        loudness = loudness * jnp.repeat(heights, dims[dim] // parts).reshape([-1 if axis == dim else 1 for axis in range(len(dims))])
    return loudness


def profile(number_of, total, bound, slope):
    weights = [(1 << 20) // math.isqrt(rank ** slope) + 1 for rank in range(2, number_of + 1)]
    rest, counts = total - bound - (number_of - 1), [1] * (number_of - 1)
    while rest > 0:
        movable = [i for i in range(number_of - 1) if counts[i] < bound]
        mass, left = sum([weights[i] for i in movable]), rest
        for i in movable:
            addition = min(bound - counts[i], max(1, left * weights[i] // mass), rest)
            counts[i] = counts[i] + addition
            rest = rest - addition
    return np.array([bound] + counts)


def ragged_sizes(rng, number_of, total, reach, lean):
    if number_of == 2:
        one = jax.random.randint(rng, (), max(1, total - reach), min(reach, total - 1) + 1)
        return jnp.stack([one, total - one])
    sizes = jnp.asarray(profile(number_of, total, reach, lean), jnp.int32)
    pairs = (number_of - 1) // 2
    giver, receiver = sizes[1:1 + 2 * pairs:2], sizes[2:2 + 2 * pairs:2]
    margin = jnp.minimum(giver - 1, reach - receiver)
    moved = jax.random.randint(jax.random.fold_in(rng, 1), (pairs,), 0, 1 << 20) % (margin + 1)
    sizes = sizes.at[1:1 + 2 * pairs:2].set(giver - moved).at[2:2 + 2 * pairs:2].set(receiver + moved)
    return sizes[jax.random.permutation(jax.random.fold_in(rng, 2), number_of)]


def scatter_about(stream_key, extent, width, limit, cuts=(), held_as=jnp.bfloat16):
    entries = width * jax.random.normal(stream_key, extent, jnp.float32)
    if cuts:
        entries = entries * levels(stream_key, extent, cuts, -0.22, 0.18)
    return jnp.clip(entries, -limit, limit).astype(held_as)


def setup_inputs(seed: int = 0) -> dict:
    streams_of = jax.random.split(jax.random.key(seed), 10)
    queries = scatter_about(streams_of[0], (TOKENS, D), 1.0, 6.0, ((0, 8), (1, 4)))
    keys = scatter_about(streams_of[1], (TOKENS, D), 1.0, 6.0, ((0, 8), (1, 4)))
    values = scatter_about(streams_of[2], (TOKENS, D), 1.0, 6.0, ((0, 8), (1, 4)))
    short_taps = scatter_about(streams_of[3], (3, TAPS, D), TAPS ** -0.5, 2.0, ((2, 4),), jnp.float32)
    residues = scatter_about(streams_of[4], (NGROUPS, MODES), MODES ** -0.5, 1.5, ((0, 4),), jnp.float32)
    decay_rate = jnp.clip(jnp.exp(math.log(0.03125) - 5.075174 * jax.random.uniform(streams_of[5], (NGROUPS, MODES), jnp.float32) ** levels(streams_of[5], (NGROUPS, MODES), ((0, 4),), -0.2, 0.2)), 0.0001953125, 0.03125)
    out_gain = jnp.clip(1.0 + 0.1 * jax.random.normal(streams_of[6], (D,), jnp.float32), 0.5, 1.5)
    doc_lengths = ragged_sizes(streams_of[7], NDOC, TOKENS, TOKENS // 2, 2).astype(jnp.int32)
    upstream = scatter_about(streams_of[8], (TOKENS, D), 1.0, 6.0, ((0, 8), (1, 4)))
    return dict(queries=queries, keys=keys, values=values, short_taps=short_taps, residues=residues, decay_rate=decay_rate, out_gain=out_gain, doc_lengths=doc_lengths, upstream=upstream)


epsilon = 1e-06
highest = lax.Precision.HIGHEST
entry_limit = 2097152

def doc_index(doc_lengths, positions):
    starts = jnp.cumsum(doc_lengths) - doc_lengths
    return lax.optimization_barrier(jnp.sum((starts[None, :] <= positions[:, None]).astype(jnp.int32), axis=1)) - 1

def spread_groups(per_group):
    return jnp.repeat(per_group.T, GROUP, axis=1)

def mode_gain(decay_rate):
    return jnp.sqrt(-jnp.expm1(-2.0 * decay_rate))

def local_part(mixed, doc_ids, prev_doc, residues, decay_rate):
    row_count, channels = mixed.shape
    group_count = channels // GROUP
    mode_count = decay_rate.shape[1]
    lag_steps = jnp.arange(row_count, dtype=jnp.float32)
    weighted = residues * mode_gain(decay_rate)
    filter_rows = jnp.einsum('gn,gnd->gd', weighted, jnp.exp(-decay_rate[:, :, None] * lag_steps[None, None, :]), precision=highest)
    row_index = jnp.arange(row_count, dtype=jnp.int32)
    lag_table = row_index[:, None] - row_index[None, :]
    causal_mask = (lag_table >= 0) & (doc_ids[:, None] == doc_ids[None, :])
    safe_lags = jnp.maximum(lag_table, 0)
    per_step = group_count
    while per_step % 2 == 0 and per_step * row_count * row_count > entry_limit:
        per_step = per_step // 2
    step_count = group_count // per_step
    mixed_cols = mixed.T.reshape(group_count, GROUP, row_count)
    table_steps = filter_rows.reshape(step_count, per_step, row_count)
    mixed_steps = mixed_cols.reshape(step_count, per_step, GROUP, row_count)

    def toeplitz_block(pieces):
        table_part, mixed_part = pieces
        toeplitz = jnp.where(causal_mask[None, :, :], table_part[:, safe_lags], 0.0)
        return jnp.einsum('gts,gis->git', toeplitz, mixed_part, precision=highest)
    outputs = lax.map(jax.checkpoint(toeplitz_block), (table_steps, mixed_steps))
    within = outputs.reshape(channels, row_count).T
    same_last = (doc_ids == doc_ids[row_count - 1]).astype(jnp.float32)
    backward_decay = jnp.exp(-decay_rate[:, :, None] * (row_count - 1.0 - lag_steps)[None, None, :]) * same_last[None, None, :]
    end_state = jnp.einsum('gns,gis->ngi', backward_decay, mixed_cols, precision=highest).reshape(mode_count, channels)
    through = (doc_ids[row_count - 1] == prev_doc).astype(jnp.float32)
    pass_decay = spread_groups(jnp.exp(-decay_rate * row_count) * through)
    return (within, pass_decay, end_state)

def tail_part(doc_ids, prev_doc, residues, decay_rate, state):
    row_count = doc_ids.shape[0]
    mode_count, channels = state.shape
    group_count = channels // GROUP
    lag_steps = jnp.arange(row_count, dtype=jnp.float32)
    weighted = residues * mode_gain(decay_rate)
    carried_mask = (doc_ids == prev_doc).astype(jnp.float32)
    decays = weighted[:, :, None] * jnp.exp(-decay_rate[:, :, None] * (lag_steps + 1.0)[None, None, :]) * carried_mask[None, None, :]
    state_cols = state.reshape(mode_count, group_count, GROUP).transpose(1, 2, 0)
    carried_cols = jnp.einsum('gnt,gin->git', decays, state_cols, precision=highest)
    return carried_cols.reshape(channels, row_count).T

def full_conv(mixed, doc_ids, residues, decay_rate, block):
    row_count, channels = mixed.shape
    step_count = row_count // block
    mode_count = decay_rate.shape[1]
    block_ends = doc_ids[block - 1::block][:-1]
    prev_docs = jnp.concatenate([jnp.full((1,), -1, jnp.int32), block_ends.astype(jnp.int32)])

    def advance(state, pieces):
        mixed_part, doc_part, prev_doc = pieces
        within, pass_decay, end_state = local_part(mixed_part, doc_part, prev_doc, residues, decay_rate)
        carried_part = tail_part(doc_part, prev_doc, residues, decay_rate, state)
        return (pass_decay * state + end_state, within + carried_part)
    start_state = jnp.zeros((mode_count, channels), jnp.float32)
    _, outputs = lax.scan(jax.checkpoint(advance), start_state, (mixed.reshape(step_count, block, channels), doc_ids.reshape(step_count, block), prev_docs))
    return outputs.reshape(row_count, channels)

def short_forward(extended, ext_docs, taps):
    row_count = extended.shape[0] - (TAPS - 1)
    doc_here = ext_docs[TAPS - 1:]
    summed = jnp.zeros((row_count, extended.shape[1]), jnp.float32)
    for lag in range(TAPS):
        begin = TAPS - 1 - lag
        same_doc = (ext_docs[begin:begin + row_count] == doc_here).astype(jnp.float32)
        summed = summed + taps[lag][None, :] * extended[begin:begin + row_count] * same_doc[:, None]
    return summed

def reference(queries, keys, values, short_taps, residues, decay_rate, out_gain, doc_lengths, upstream):
    doc_ids = doc_index(doc_lengths, jnp.arange(TOKENS, dtype=jnp.int32))
    pad_docs = jnp.concatenate([jnp.full((TAPS - 1,), -1, jnp.int32), doc_ids.astype(jnp.int32)])
    padding = jnp.zeros((TAPS - 1, D), jnp.float32)

    def forward(query_in, key_in, value_in, taps, resid_in, rate_in, gain_in):
        qs = short_forward(jnp.concatenate([padding, query_in]), pad_docs, taps[0])
        ks = short_forward(jnp.concatenate([padding, key_in]), pad_docs, taps[1])
        vs = short_forward(jnp.concatenate([padding, value_in]), pad_docs, taps[2])
        conv = full_conv(ks * vs, doc_ids, resid_in, rate_in, TOK_DEV)
        gated = qs * conv
        inverse = lax.rsqrt(lax.optimization_barrier(jnp.sum(gated * gated, axis=1)) / D + epsilon)
        return gated * inverse[:, None] * gain_in
    out_full, backward = jax.vjp(forward, queries.astype(jnp.float32), keys.astype(jnp.float32), values.astype(jnp.float32), short_taps, residues, decay_rate, out_gain)
    grads = backward(upstream.astype(jnp.float32))
    return (out_full.astype(jnp.bfloat16), grads[0].astype(jnp.bfloat16), grads[1].astype(jnp.bfloat16), grads[2].astype(jnp.bfloat16), grads[3], grads[4], grads[5], grads[6])
```

```python
import functools

import jax
import jax.numpy as jnp
from jax import lax
from jax.experimental import pallas as pl
from jax.experimental.pallas import tpu as pltpu
from jax.sharding import PartitionSpec as P

GROUP = 16
TAPS = 7
HALO = 8
LANES = 128
PER_TILE = LANES // GROUP
epsilon = 1e-06
f32, bf16 = jnp.float32, jnp.bfloat16
highest = lax.Precision.HIGHEST
NN = (((1,), (0,)), ((), ()))
NT = (((1,), (1,)), ((), ()))


def dot(a, b, dims=NN, precision=None):
    return lax.dot_general(a, b, dims, precision=precision, preferred_element_type=f32)


def iota(shape, dim):
    return lax.broadcasted_iota(jnp.int32, shape, dim)


def docs_at(lens, positions):
    start = jnp.int32(0)
    count = jnp.zeros_like(positions)
    for k in range(lens.shape[0]):
        count = count + jnp.where(positions >= start, 1, 0)
        start = start + lens[k]
    return count - 1


def one_minus_exp(x):
    series = x * (1 - x / 2 * (1 - x / 3 * (1 - x / 4 * (1 - x / 5 * (1 - x / 6 * (1 - x / 7))))))
    return jnp.where(x < 0.125, series, 1 - jnp.exp(-x))


def own_group(rows=LANES):
    return [iota((rows, LANES), 1) // GROUP == k for k in range(PER_TILE)]


def spread_rows(per_mode, masks):
    return jnp.concatenate([jnp.where(m, per_mode, 0.0) for m in masks], axis=0)


def pick_rows(full, masks):
    modes = full.shape[0] // PER_TILE
    total = jnp.where(masks[0], full[:modes], 0.0)
    for k in range(1, PER_TILE):
        total = jnp.where(masks[k], full[k * modes : (k + 1) * modes], total)
    return total


def column_of(ref, tile, modes):
    rows = [
        jnp.broadcast_to(ref[pl.ds(tile * PER_TILE + k, 1), :], (modes, modes))
        for k in range(PER_TILE)
    ]
    stacked = jnp.concatenate(rows, axis=0)
    own = iota(stacked.shape, 0) % modes == iota(stacked.shape, 1)
    return jnp.sum(jnp.where(own, stacked, 0.0), axis=1, keepdims=True)


def tile_slice(tile):
    return pl.ds(pl.multiple_of(tile * LANES, LANES), LANES)


def vmem(shape, dtype):
    return jax.ShapeDtypeStruct(shape, dtype)


def call(body, outs, *args, smem=0, scratch=(), flops=0, name=None, limit=32):
    moved = sum(a.size * a.dtype.itemsize for a in args) + sum(
        o.size * o.dtype.itemsize for o in outs
    )
    return pl.pallas_call(
        body,
        out_shape=tuple(outs),
        in_specs=[pl.BlockSpec(memory_space=pltpu.SMEM)] * smem
        + [pl.BlockSpec(memory_space=pltpu.VMEM)] * (len(args) - smem),
        out_specs=tuple([pl.BlockSpec(memory_space=pltpu.VMEM)] * len(outs)),
        scratch_shapes=list(scratch),
        compiler_params=pltpu.CompilerParams(vmem_limit_bytes=limit << 20),
        cost_estimate=pl.CostEstimate(flops=flops, bytes_accessed=moved, transcendentals=0),
        name=name,
    )(*args)


def pack_last(k, v, q, out):
    for slot, ref in enumerate((k, v, q)):
        tail = ref[...].astype(f32)[HALO:]
        out[slot * HALO : (slot + 1) * HALO, :] = tail.astype(bf16)


def mode_tables(levels, lens, res, rate, e_tab, e_tab_t, c_tab, c_tab_t, w_out, own_pass, *passes):
    groups, modes = rate.shape
    rows = LANES
    first = lax.axis_index("ctx") * rows
    lane = iota((LANES, LANES), 1)
    last = first + rows - 1
    docs_lane = docs_at(lens, first + lane)
    doc_last, doc_prev = docs_at(lens, last), docs_at(lens, first - 1)
    in_last = jnp.where(docs_lane == doc_last, 1.0, 0.0)
    in_prev = jnp.where(docs_lane == doc_prev, 1.0, 0.0)
    lag_e = (rows - 1 - lane).astype(f32)
    lag_c = (lane + 1).astype(f32)
    masks = own_group(modes)
    whole = jnp.where(doc_last == doc_prev, 1.0, 0.0)
    through = []
    for level in range(levels):
        reach = rows << level
        through.append(jnp.where(docs_at(lens, first - 1 - reach) == doc_prev, 1.0, 0.0))
        through.append(jnp.where(docs_at(lens, last + reach) == doc_last, 1.0, 0.0))

    def step(tile, carry):
        at = tile_slice(tile)
        r_col = jnp.broadcast_to(column_of(rate, tile, modes), (LANES, LANES))
        w_col = column_of(res, tile, modes) * jnp.sqrt(one_minus_exp(2.0 * r_col))
        e = jnp.exp(-r_col * lag_e) * in_last
        c = jnp.exp(-r_col * lag_c) * in_prev
        e_tab[at, :] = e.astype(bf16)
        c_tab_t[at, :] = c.astype(bf16)
        e_tab_t[at, :] = e.T.astype(bf16)
        c_tab[at, :] = c.T.astype(bf16)
        w_out[:, at] = pick_rows(w_col, masks)
        r_tile = pick_rows(r_col, masks)
        own_pass[:, at] = jnp.exp(-r_tile * float(rows)) * whole
        for level in range(levels):
            decay = jnp.exp(-r_tile * float(rows << level))
            passes[2 * level][:, at] = decay * through[2 * level]
            passes[2 * level + 1][:, at] = decay * through[2 * level + 1]
        return carry

    lax.fori_loop(0, groups // PER_TILE, step, 0)


def toeplitz_tables(transposed, lens, res, rate, out, base):
    groups, modes = rate.shape
    first = lax.axis_index("ctx") * LANES
    row, lane = iota((LANES, LANES), 0), iota((LANES, LANES), 1)
    same = docs_at(lens, first + row) == docs_at(lens, first + lane)
    if transposed:
        keep, lag = same & (lane >= row), lane
    else:
        keep, lag = same & (lane <= row), (LANES - lane) % LANES
    keep = jnp.where(keep, 1.0, 0.0)
    lag = lag.astype(f32)
    r = rate[...]
    w = res[...] * jnp.sqrt(one_minus_exp(2.0 * r))
    total = jnp.zeros((groups, LANES), f32)
    for n in range(modes):
        total = total + w[:, n : n + 1] * jnp.exp(-r[:, n : n + 1] * lag)
    base[...] = total

    def step(tile, carry):
        at = tile_slice(tile)
        for k in range(PER_TILE):
            line = jnp.broadcast_to(base[pl.ds(tile * PER_TILE + k, 1), :], (LANES, LANES))
            rolled = pltpu.roll(line, 0, 1, stride=1, stride_axis=0)
            out[at, k * LANES : (k + 1) * LANES] = (rolled * keep).astype(bf16)
        return carry

    lax.fori_loop(0, groups // PER_TILE, step, 0)


def same_doc_masks(lens, first, sign, masks):
    pos = first + iota((LANES, LANES), 0)
    here = docs_at(lens, pos)
    for lag in range(1, TAPS):
        masks[lag] = jnp.where(docs_at(lens, pos + sign * lag) == here, 1.0, 0.0)


def short_conv(ext, taps, index, masks, at, sign):
    base = HALO if sign < 0 else 0
    total = taps[index, 0:1, at] * ext[base : base + LANES, at]
    for lag in range(1, TAPS):
        begin = base + sign * lag
        total = total + taps[index, lag : lag + 1, at] * (ext[begin : begin + LANES, at] * masks[lag])
    return total


def fill_before(ext, halo, slot, own):
    ext[:HALO, :] = halo[...].astype(f32)[slot * HALO : (slot + 1) * HALO]
    ext[HALO:, :] = own[...].astype(f32)


def keys_values(lens, k, v, halo, taps, e_tab, mixed, ks_out, vs_out, s_out, s_msg, k_ext, v_ext, masks):
    channels = k.shape[1]
    modes = s_out.shape[0]
    first = lax.axis_index("ctx") * LANES
    same_doc_masks(lens, first, -1, masks)
    fill_before(k_ext, halo, 0, k)
    fill_before(v_ext, halo, 1, v)
    own = own_group(modes)

    def step(tile, carry):
        at = tile_slice(tile)
        ks = short_conv(k_ext, taps, 1, masks, at, -1)
        vs = short_conv(v_ext, taps, 2, masks, at, -1)
        ks_out[:, at] = ks
        vs_out[:, at] = vs
        m = (ks * vs).astype(bf16)
        mixed[:, at] = m
        state = pick_rows(dot(e_tab[at, :], m), own)
        s_out[:, at] = state
        s_msg[:, at] = state.astype(bf16)
        return carry

    lax.fori_loop(0, channels // LANES, step, 0)


def queries_short(lens, q, halo, taps, qs_out, q_ext, masks):
    first = lax.axis_index("ctx") * LANES
    same_doc_masks(lens, first, -1, masks)
    fill_before(q_ext, halo, 2, q)

    def step(tile, carry):
        at = tile_slice(tile)
        qs_out[:, at] = short_conv(q_ext, taps, 0, masks, at, -1)
        return carry

    lax.fori_loop(0, q.shape[1] // LANES, step, 0)


def lane_masks_bf16():
    return [jnp.where(m, 1.0, 0.0).astype(bf16) for m in own_group()]


def toeplitz_apply(table, x, out):
    own = lane_masks_bf16()

    def step(tile, carry):
        at = tile_slice(tile)
        part = x[:, at]
        stacked = jnp.concatenate([part * m for m in own], axis=0)
        out[:, at] = dot(table[at, :], stacked)
        return carry

    lax.fori_loop(0, x.shape[1] // LANES, step, 0)


def gate(within, state, w, c_tab, qs, up, gain, conv_out, sums):
    modes = state.shape[0]
    own = own_group(modes)
    zero = jnp.zeros((LANES, LANES), f32)

    def step(tile, carry):
        squares, dots = carry
        at = tile_slice(tile)
        carried = spread_rows(state[:, at] * w[:, at], own).astype(bf16)
        conv = within[:, at] + dot(c_tab[at, :], carried)
        conv_out[:, at] = conv
        gated = qs[:, at] * conv
        scaled = up[:, at].astype(f32) * gain[:, at]
        return squares + gated * gated, dots + scaled * gated

    squares, dots = lax.fori_loop(0, qs.shape[1] // LANES, step, (zero, zero))
    ones = jnp.ones((HALO, LANES), f32)
    first = dot(ones, squares, NT, highest)
    second = dot(ones, dots, NT, highest)
    sums[...] = jnp.where(iota((HALO, LANES), 0) < 4, first, second)


def norm_columns(sums, width):
    both = sums[...]
    inverse = lax.rsqrt(both[0:1] / width + epsilon)
    slope = inverse * inverse * inverse * both[4:5] / width
    wide = lambda line: jnp.broadcast_to(line, (LANES, LANES)).T
    return wide(inverse), wide(slope)


def grad_conv(width, sums, conv, qs, up, gain, w, c_tab_t, dconv, u_out, g_out, g_msg):
    modes = u_out.shape[0]
    own = own_group(modes)
    inverse, slope = norm_columns(sums, width)

    def step(tile, carry):
        at = tile_slice(tile)
        q = qs[:, at]
        scaled = up[:, at].astype(f32) * gain[:, at]
        d_gated = inverse * scaled - (q * conv[:, at]) * slope
        d = (d_gated * q).astype(bf16)
        dconv[:, at] = d
        u = pick_rows(dot(c_tab_t[at, :], d), own)
        u_out[:, at] = u
        g = u * w[:, at]
        g_out[:, at] = g
        g_msg[:, at] = g.astype(bf16)
        return carry

    lax.fori_loop(0, qs.shape[1] // LANES, step, 0)


def tap_rows(rows_out, slot, d, ext, masks, at):
    for lag in range(TAPS):
        begin = HALO - lag
        prod = d * ext[begin : begin + LANES, at]
        if lag:
            prod = prod * masks[lag]
        rows_out[slot + lag : slot + lag + 1, at] = jnp.sum(prod, axis=0, keepdims=True)


def query_side(width, lens, sums, conv, qs, up, gain, q, halo, out, dqs_out, rows_out, q_ext, masks):
    first = lax.axis_index("ctx") * LANES
    same_doc_masks(lens, first, -1, masks)
    fill_before(q_ext, halo, 2, q)
    inverse, slope = norm_columns(sums, width)

    def step(tile, carry):
        at = tile_slice(tile)
        c = conv[:, at]
        gated = qs[:, at] * c
        upstream = up[:, at].astype(f32)
        d_gated = inverse * (upstream * gain[:, at]) - gated * slope
        normed = gated * inverse
        out[:, at] = (normed * gain[:, at]).astype(bf16)
        dqs = d_gated * c
        dqs_out[:, at] = dqs
        tap_rows(rows_out, 0, dqs, q_ext, masks, at)
        rows_out[TAPS : TAPS + 1, at] = jnp.sum(upstream * normed, axis=0, keepdims=True)
        return carry

    lax.fori_loop(0, q.shape[1] // LANES, step, 0)


def filter_grads(lens, rate, dconv, mixed, state, u, passed, e_tab, c_tab_t, q0_out, q1_out, x_out):
    groups, modes = rate.shape
    first = lax.axis_index("ctx") * LANES
    row, lane = iota((LANES, LANES), 0), iota((LANES, LANES), 1)
    turned = LANES - 1 - row
    same = docs_at(lens, first + turned) == docs_at(lens, first + lane)
    keep = jnp.where(same & (lane <= turned), 1.0, 0.0)
    turn = jnp.where(lane == turned, 1.0, 0.0).astype(bf16)
    lag = ((LANES - lane) % LANES).astype(f32)
    lag_c = (lane + 1).astype(f32)
    lag_e = (LANES - 1 - lane).astype(f32)
    own_b = lane_masks_bf16()
    own = own_group(modes)
    ones = jnp.ones((HALO, LANES), f32)
    mine = iota((PER_TILE, LANES), 1) // modes == iota((PER_TILE, LANES), 0)

    def step(tile, carry):
        at = tile_slice(tile)
        d, m = dconv[:, at], mixed[:, at]
        stacked = jnp.concatenate([m * o for o in own_b], axis=0)
        outer = dot(dot(turn, d).astype(bf16), stacked, NT)
        lines = []
        for k in range(PER_TILE):
            block = outer[:, k * LANES : (k + 1) * LANES] * keep
            block = pltpu.roll(block, 1, 1, stride=1, stride_axis=0)
            lines.append(jnp.sum(block, axis=0, keepdims=True))
        dh = jnp.concatenate(lines, axis=0)
        r_col = jnp.broadcast_to(column_of(rate, tile, modes), (LANES, LANES))
        powers = jnp.exp(-r_col * lag)
        both = dot(jnp.concatenate([dh, dh * lag[:PER_TILE]], axis=0), powers, NT, highest)
        s = state[:, at]
        c_t = c_tab_t[at, :].astype(f32)
        v = pick_rows(dot((c_t * lag_c).astype(bf16), d), own)
        x = pick_rows(dot((e_tab[at, :].astype(f32) * lag_e).astype(bf16), m), own)
        x_out[:, at] = x + float(LANES) * passed[:, at] * s
        in0 = dot(ones, spread_rows(s * u[:, at], own), NT, highest)
        in1 = dot(ones, spread_rows(s * v, own), NT, highest)
        q0 = jnp.where(mine, both[:PER_TILE], 0.0)
        q1 = jnp.where(mine, both[PER_TILE:], 0.0)
        q0_out[:, at] = jnp.sum(q0, axis=0, keepdims=True) + in0[0:1]
        q1_out[:, at] = jnp.sum(q1, axis=0, keepdims=True) + in1[0:1]
        return carry

    lax.fori_loop(0, groups // PER_TILE, step, 0)


def grad_keys_values(
    lens, res, rate, later, local, e_tab_t, ks, vs, k, v, halo, dqs, q0, q1, x,
    dks_out, dvs_out, rows_out, halo_out, k_ext, v_ext, masks,
):
    modes = later.shape[0]
    first = lax.axis_index("ctx") * LANES
    same_doc_masks(lens, first, -1, masks)
    fill_before(k_ext, halo, 0, k)
    fill_before(v_ext, halo, 1, v)
    own = own_group(modes)
    ones = jnp.ones((HALO, LANES), f32)

    def step(tile, carry):
        at = tile_slice(tile)
        g = later[:, at]
        d_mixed = local[:, at] + dot(e_tab_t[at, :], spread_rows(g, own).astype(bf16))
        dks = d_mixed * vs[:, at]
        dvs = d_mixed * ks[:, at]
        dks_out[:, at] = dks
        dvs_out[:, at] = dvs
        halo_out[0:HALO, at] = dks[:HALO].astype(bf16)
        halo_out[HALO : 2 * HALO, at] = dvs[:HALO].astype(bf16)
        halo_out[2 * HALO : 3 * HALO, at] = dqs[:HALO, at].astype(bf16)
        tap_rows(rows_out, 0, dks, k_ext, masks, at)
        tap_rows(rows_out, TAPS, dvs, v_ext, masks, at)
        after = dot(ones, spread_rows(g * x[:, at], own), NT, highest)[0:1]
        r_row = jnp.broadcast_to(column_of(rate, tile, modes), (LANES, LANES)).T[0:1]
        res_row = jnp.broadcast_to(column_of(res, tile, modes), (LANES, LANES)).T[0:1]
        gain = jnp.sqrt(one_minus_exp(2.0 * r_row))
        slope = jnp.exp(-2.0 * r_row) / gain
        q0_row, q1_row = q0[:, at], q1[:, at]
        rows_out[2 * TAPS : 2 * TAPS + 1, at] = gain * q0_row
        rows_out[2 * TAPS + 1 : 2 * TAPS + 2, at] = (
            res_row * slope * q0_row - res_row * gain * q1_row - after
        )
        return carry

    lax.fori_loop(0, k.shape[1] // LANES, step, 0)


def grad_inputs(lens, taps, dq, dk, dv, after, q_out, k_out, v_out, q_ext, k_ext, v_ext, masks):
    first = lax.axis_index("ctx") * LANES
    same_doc_masks(lens, first, 1, masks)
    for slot, own, ext in ((2, dq, q_ext), (0, dk, k_ext), (1, dv, v_ext)):
        ext[:LANES, :] = own[...]
        ext[LANES:, :] = after[...].astype(f32)[slot * HALO : (slot + 1) * HALO]

    def step(tile, carry):
        at = tile_slice(tile)
        q_out[:, at] = short_conv(q_ext, taps, 0, masks, at, 1).astype(bf16)
        k_out[:, at] = short_conv(k_ext, taps, 1, masks, at, 1).astype(bf16)
        v_out[:, at] = short_conv(v_ext, taps, 2, masks, at, 1).astype(bf16)
        return carry

    lax.fori_loop(0, dq.shape[1] // LANES, step, 0)


def unpack(rows_q, rows_kv, taps_out, res_out, rate_out, gain_out):
    groups, modes = res_out.shape
    taps_out[0] = rows_q[0:TAPS, :]
    taps_out[1] = rows_kv[0:TAPS, :]
    taps_out[2] = rows_kv[TAPS : 2 * TAPS, :]
    gain_out[...] = rows_q[TAPS : TAPS + 1, :]
    pick = jnp.where(iota((LANES, modes), 0) % modes == iota((LANES, modes), 1), 1.0, 0.0)
    mine = iota((PER_TILE, LANES), 1) // modes == iota((PER_TILE, LANES), 0)
    for slot, out in ((2 * TAPS, res_out), (2 * TAPS + 1, rate_out)):
        parts = []
        for tile in range(groups // PER_TILE):
            line = rows_kv[slot : slot + 1, tile * LANES : (tile + 1) * LANES]
            parts.append(jnp.where(mine, jnp.broadcast_to(line, (PER_TILE, LANES)), 0.0))
        out[...] = dot(jnp.concatenate(parts, axis=0), pick, NN, highest)


def moved(value, axis, steps):
    count = lax.axis_size(axis)
    first, last = max(0, -steps), min(count, count - steps)
    return lax.ppermute(value, axis, [(i, i + steps) for i in range(first, last)])


def swapped(value, axis, bit):
    return lax.ppermute(value, axis, [(i, i ^ bit) for i in range(lax.axis_size(axis))])


def window(message, own, passes, direction):
    count = lax.axis_size("ctx")
    near = moved(message, "ctx", direction)
    far = moved(message, "ctx", 2 * direction)
    total = near.astype(f32) + passes[0] * far.astype(f32)
    reach, level = 2, 1
    while reach < count // 2:
        other = moved(total.astype(bf16), "ctx", reach * direction)
        total = total + passes[level] * other.astype(f32)
        reach, level = 2 * reach, level + 1
    return total


def on_device(q, k, v, taps, res, rate, gain, lens, up):
    rows, channels = q.shape
    groups, modes = rate.shape
    count = lax.axis_size("ctx")
    width = channels * lax.axis_size("ch")
    tiles = channels // LANES
    levels = max(1, (count // 2).bit_length() - 1)
    gain = gain.reshape(1, channels)
    wide = lambda dtype: vmem((rows, channels), dtype)
    state_shape = vmem((modes, channels), f32)
    msg_shape = vmem((modes, channels), bf16)
    table = vmem((channels, LANES), bf16)
    ext = pltpu.VMEM((rows + HALO, channels), f32)
    mask_scratch = pltpu.VMEM((TAPS, rows, LANES), f32)

    tail = pl.BlockSpec((2 * HALO, channels), lambda i: (rows // (2 * HALO) - 1, 0))
    last = pl.pallas_call(
        pack_last,
        out_shape=vmem((3 * HALO, channels), bf16),
        grid=(1,),
        in_specs=[tail] * 3,
        out_specs=pl.BlockSpec((3 * HALO, channels), lambda i: (0, 0)),
        name="halo_rows",
    )(k, v, q)
    halo = moved(last, "ctx", 1)

    e_tab, e_tab_t, c_tab, c_tab_t, w, own_pass, *passes = call(
        functools.partial(mode_tables, levels),
        [table] * 4 + [state_shape] * (2 + 2 * levels),
        lens, res, rate, smem=1, flops=4 << 20, name="mode_tables",
    )
    big = vmem((channels, PER_TILE * LANES), bf16)
    base = pltpu.VMEM((groups, LANES), f32)
    toep = call(
        functools.partial(toeplitz_tables, False), [big],
        lens, res, rate, smem=1, scratch=[base], flops=8 << 20, name="toeplitz",
    )[0]
    toep_t = call(
        functools.partial(toeplitz_tables, True), [big],
        lens, res, rate, smem=1, scratch=[base], flops=8 << 20, name="toeplitz_t",
    )[0]

    mixed, ks, vs, own_state, state_msg = call(
        keys_values, [wide(bf16), wide(f32), wide(f32), state_shape, msg_shape],
        lens, k, v, halo, taps, e_tab, smem=1, scratch=[ext, ext, mask_scratch],
        flops=64 << 20, name="keys_values",
    )
    state = window(state_msg, own_state, passes[0::2], 1)
    qs = call(
        queries_short, [wide(f32)], lens, q, halo, taps, smem=1, scratch=[ext, mask_scratch],
        flops=8 << 20, name="queries_short",
    )[0]
    within = call(
        toeplitz_apply, [wide(f32)], toep, mixed, flops=512 << 20, name="within"
    )[0]
    conv, sums = call(
        gate, [wide(f32), vmem((HALO, LANES), f32)],
        within, state, w, c_tab, qs, up, gain, flops=64 << 20, name="gate",
    )
    bit = 1
    while bit < lax.axis_size("ch"):
        sums = sums + swapped(sums, "ch", bit)
        bit *= 2
    dconv, u, own_grad, grad_msg = call(
        functools.partial(grad_conv, width), [wide(bf16), state_shape, state_shape, msg_shape],
        sums, conv, qs, up, gain, w, c_tab_t, flops=64 << 20, name="grad_conv",
    )
    later = window(grad_msg, own_grad, passes[1::2], -1)
    out, dqs, rows_q = call(
        functools.partial(query_side, width),
        [wide(bf16), wide(f32), vmem((HALO, channels), f32)],
        lens, sums, conv, qs, up, gain, q, halo, smem=1, scratch=[ext, mask_scratch],
        flops=16 << 20, name="query_side",
    )
    local = call(
        toeplitz_apply, [wide(f32)], toep_t, dconv, flops=512 << 20, name="local_grad"
    )[0]
    row = vmem((1, channels), f32)
    q0, q1, x = call(
        filter_grads, [row, row, state_shape],
        lens, rate, dconv, mixed, state, u, own_pass, e_tab, c_tab_t,
        smem=1, flops=512 << 20, name="filter_grads",
    )
    dks, dvs, rows_kv, first_rows = call(
        grad_keys_values,
        [wide(f32), wide(f32), vmem((2 * HALO, channels), f32), vmem((3 * HALO, channels), bf16)],
        lens, res, rate, later, local, e_tab_t, ks, vs, k, v, halo, dqs, q0, q1, x,
        smem=1, scratch=[ext, ext, mask_scratch], flops=64 << 20, name="grad_keys_values",
    )
    after = moved(first_rows, "ctx", -1)
    bit = 1
    while bit < count:
        rows_q, rows_kv = rows_q.astype(bf16), rows_kv.astype(bf16)
        both = jnp.concatenate([rows_q, rows_kv])
        both = both.astype(f32) + swapped(both, "ctx", bit).astype(f32)
        rows_q, rows_kv = both[:HALO], both[HALO:]
        bit *= 2
    d_q, d_k, d_v = call(
        grad_inputs, [wide(bf16)] * 3, lens, taps, dqs, dks, dvs, after,
        smem=1, scratch=[ext, ext, ext, mask_scratch], flops=24 << 20, name="grad_inputs",
    )
    d_taps, d_res, d_rate, d_gain = call(
        unpack,
        [vmem(taps.shape, f32), vmem(res.shape, f32), vmem(rate.shape, f32), vmem((1, channels), f32)],
        rows_q, rows_kv, name="unpack",
    )
    return out, d_q, d_k, d_v, d_taps, d_res, d_rate, d_gain.reshape(channels)


def solution(mesh):
    wide = P("ctx", "ch")
    third, table, line = P(None, None, "ch"), P("ch", None), P("ch")
    return jax.shard_map(
        on_device,
        mesh=mesh,
        in_specs=(wide, wide, wide, third, table, table, line, P(), wide),
        out_specs=(wide, wide, wide, wide, third, table, table, line),
        check_vma=False,
    )
```

```python
import functools
import math

import jax
import jax.numpy as jnp
from jax import lax
from jax.experimental import pallas as pl
from jax.experimental.pallas import tpu as pltpu
from jax.sharding import PartitionSpec as P

GROUP = 16
TAPS = 7
HALO = 8
LANES = 128
PER_TILE = LANES // GROUP
epsilon = 1e-06
f32, bf16 = jnp.float32, jnp.bfloat16
highest = lax.Precision.HIGHEST
NN = (((1,), (0,)), ((), ()))
NT = (((1,), (1,)), ((), ()))


def dot(a, b, dims=NN, precision=None):
    return lax.dot_general(a, b, dims, precision=precision, preferred_element_type=f32)


def iota(shape, dim):
    return lax.broadcasted_iota(jnp.int32, shape, dim)


def docs_at(lens, positions):
    start = jnp.int32(0)
    count = jnp.zeros_like(positions)
    for k in range(lens.shape[0]):
        count = count + jnp.where(positions >= start, 1, 0)
        start = start + lens[k]
    return count - 1


def starts_at(lens):
    out = [jnp.int32(0)]
    for k in range(lens.shape[0] - 1):
        out.append(out[-1] + lens[k])
    return out


def doc_start(lens, positions):
    start = jnp.full_like(positions, 0)
    for s in starts_at(lens)[1:]:
        start = jnp.where(positions >= s, s, start)
    return start


def next_start(lens, positions):
    after = jnp.full_like(positions, jnp.iinfo(jnp.int32).max)
    for s in starts_at(lens)[:0:-1]:
        after = jnp.where(positions < s, s, after)
    return after


def one_minus_exp(x):
    series = x * (1 - x / 2 * (1 - x / 3 * (1 - x / 4 * (1 - x / 5 * (1 - x / 6 * (1 - x / 7))))))
    return jnp.where(x < 0.125, series, 1 - jnp.exp(-x))


def own_group(rows=LANES):
    return [iota((rows, LANES), 1) // GROUP == k for k in range(PER_TILE)]


def spread_rows(per_mode, masks):
    return jnp.concatenate([jnp.where(m, per_mode, 0.0) for m in masks], axis=0)


def pick_rows(full, masks):
    modes = full.shape[0] // PER_TILE
    total = jnp.where(masks[0], full[:modes], 0.0)
    for k in range(1, PER_TILE):
        total = jnp.where(masks[k], full[k * modes : (k + 1) * modes], total)
    return total


def column_of(ref, tile):
    modes = ref.shape[0]
    part = [ref[:, tile * PER_TILE + k : tile * PER_TILE + k + 1] for k in range(PER_TILE)]
    return jnp.concatenate([jnp.broadcast_to(p, (modes, LANES)) for p in part], axis=0)


def mode_gain(rate):
    return jnp.sqrt(one_minus_exp(2.0 * rate))


def each_tile(channels, width=LANES):
    return [slice(i, i + width) for i in range(0, channels, width)]


def vmem(shape, dtype):
    return jax.ShapeDtypeStruct(shape, dtype)


def call(body, outs, *args, smem=0, hbm=0, scratch=(), flops=0, name=None, limit=32):
    moved = sum(a.size * a.dtype.itemsize for a in args) + sum(
        math.prod(o.shape) * o.dtype.itemsize for o in outs
    )
    if hbm:
        args = (*args[:-hbm], *[pltpu.with_memory_space_constraint(a, pltpu.HBM) for a in args[-hbm:]])
        outs = [pltpu.VMEM(o.shape, o.dtype) for o in outs]
    return pl.pallas_call(
        body,
        out_shape=tuple(outs),
        in_specs=[pl.BlockSpec(memory_space=pltpu.SMEM)] * smem
        + [pl.BlockSpec(memory_space=pltpu.VMEM)] * (len(args) - smem - hbm)
        + [pl.BlockSpec(memory_space=pltpu.HBM)] * hbm,
        out_specs=tuple([pl.BlockSpec(memory_space=pltpu.VMEM)] * len(outs)),
        scratch_shapes=list(scratch),
        compiler_params=pltpu.CompilerParams(vmem_limit_bytes=limit << 20),
        cost_estimate=pl.CostEstimate(flops=flops, bytes_accessed=moved, transcendentals=0),
        name=name,
    )(*args)


def bring_in(arrays, *refs):
    sources, out, targets, sems = refs[:arrays], refs[arrays], refs[arrays + 1 : -1], refs[-1]
    copies = [pltpu.make_async_copy(a, b, sems.at[i]) for i, (a, b) in enumerate(zip(sources, targets))]
    for copy in copies:
        copy.start()
    for slot, (copy, ref) in enumerate(zip(copies, targets[:3])):
        copy.wait()
        rows = ref.shape[0]
        tail = ref[rows - 2 * HALO :, :].astype(f32)[HALO:]
        out[slot * HALO : (slot + 1) * HALO, :] = tail.astype(bf16)
    for copy in copies[3:]:
        copy.wait()


def shift_rows(table, lens, first, sign):
    shape = table.shape[1:]
    pos = first + iota((LANES, LANES), 0)
    limit = doc_start(lens, pos) if sign < 0 else next_start(lens, pos)
    limit = jnp.concatenate([limit, limit], axis=1)[:, : shape[1]]
    row, col = iota(shape, 0), iota(shape, 1)
    source = first + col - (2 * HALO if sign < 0 else 0)
    apart = col - row - (2 * HALO if sign < 0 else 0)
    apart = jnp.where(source >= limit if sign < 0 else source < limit, apart * sign, 0)
    for lag in range(1, TAPS):
        table[lag - 1] = jnp.where(apart == lag, 1.0, 0.0).astype(bf16)


def rounds_of(count):
    out, below = [], 0
    while count >> below > 1:
        meet = min(4, count >> below)
        out.append((below, meet))
        below += meet.bit_length() - 1
    return out


def pass_count(count):
    rounds = rounds_of(count)
    return sum(meet - 1 for _, meet in rounds) + sum(meet for _, meet in rounds[:-1])


def pass_factors(lens, me, count, forward):
    ends = lambda device: docs_at(lens, device * LANES + LANES - 1)
    out = []
    rounds = rounds_of(count)
    for place, (below, meet) in enumerate(rounds):
        size, mine = 1 << below, me >> below
        wide = size * meet
        start = (me // wide) * wide
        for m in range(1, meet):
            other = mine ^ m
            if forward:
                edge = other * size + size - 1
                lag, meets, valid = me - 1 - edge, ends(edge) == ends(me - 1), other < mine
            else:
                edge = other * size - 1
                lag, meets, valid = edge - me, ends(edge) == ends(me), other > mine
            out.append((lag, jnp.where(meets & valid, 1.0, 0.0)))
        if place + 1 == len(rounds):
            continue
        for m in range(meet):
            other = mine ^ m
            if forward:
                edge, far = other * size + size - 1, start + wide - 1
                lag = far - edge
            else:
                edge, far = other * size - 1, start - 1
                lag = edge - far
            out.append((lag, jnp.where(ends(edge) == ends(far), 1.0, 0.0)))
    return out


def first_tables(count, lens, rate, e_tab, before, after, start_row, start_col, edges, in_prev, factors):
    me = lax.axis_index("ctx")
    first = me * LANES
    shift_rows(before, lens, first, -1)
    lane = iota((LANES, LANES), 1)
    last = first + LANES - 1
    in_last = jnp.where(docs_at(lens, first + lane) == docs_at(lens, last), 1.0, 0.0)
    lag = (LANES - 1 - lane).astype(f32)
    for tile in range(rate.shape[1] // PER_TILE):
        e = jnp.exp(-column_of(rate, tile) * lag) * in_last
        e_tab[tile * LANES : (tile + 1) * LANES, :] = e.astype(bf16)
    shift_rows(after, lens, first, 1)
    row = first + iota((LANES, LANES), 0)
    start_row[...] = doc_start(lens, row)
    start_col[...] = doc_start(lens, first + lane)
    for lag, mask in enumerate(edge_masks(lens, first)):
        if lag:
            edges[lag] = mask
    doc_prev = docs_at(lens, first - 1)
    in_prev[...] = jnp.where(docs_at(lens, first + lane) == doc_prev, 1.0, 0.0)
    pairs = [(jnp.int32(1), jnp.where(docs_at(lens, last) == doc_prev, float(LANES), 0.0))]
    pairs += pass_factors(lens, me, count, True) + pass_factors(lens, me, count, False)
    for place, (steps, mask) in enumerate(pairs):
        scale = -(jnp.maximum(steps, 0) * LANES).astype(f32)
        factors[2 * place : 2 * place + 1, :] = jnp.full((1, LANES), scale, f32)
        factors[2 * place + 1 : 2 * place + 2, :] = jnp.full((1, LANES), mask, f32)


def mode_tables(res, rate, e_tab, in_prev, factors, c_tab, c_tab_t, e_tab_t, w_out, *passes):
    modes = rate.shape[0]
    lag = (iota((LANES, LANES), 1) + 1).astype(f32)
    masks = own_group(modes)
    mask = in_prev[...]
    for tile in range(rate.shape[1] // PER_TILE):
        at = slice(tile * LANES, (tile + 1) * LANES)
        r_col = column_of(rate, tile)
        c = jnp.exp(-r_col * lag) * mask
        c_tab_t[at, :] = c.astype(bf16)
        c_tab[at, :] = c.T.astype(bf16)
        e_tab_t[at, :] = e_tab[at, :].astype(f32).T.astype(bf16)
        r_tile = pick_rows(r_col, masks)
        w_out[:, at] = pick_rows(column_of(res, tile), masks) * mode_gain(r_tile)
        for place, out in enumerate(passes):
            scale, keep = factors[2 * place : 2 * place + 1, :], factors[2 * place + 1 : 2 * place + 2, :]
            out[:, at] = jnp.exp(r_tile * scale) * keep


def split(x):
    high = x.astype(bf16)
    return high, (x - high.astype(f32)).astype(bf16)


def toeplitz_tables(transposed, res, rate, start_row, start_col, out, base):
    modes, groups = rate.shape
    row, lane = iota((LANES, LANES), 0), iota((LANES, LANES), 1)
    same = start_row[...] == start_col[...]
    keep = jnp.where(same & ((lane >= row) if transposed else (lane <= row)), 1.0, 0.0)
    lag = (lane if transposed else (LANES - lane) % LANES).astype(f32)
    over = jnp.where(iota((PER_TILE, LANES), 1) // modes == iota((PER_TILE, LANES), 0), 1.0, 0.0).astype(bf16)

    def store(tile, k, table):
        to = k * LANES
        out[tile * LANES : (tile + 1) * LANES, to : to + LANES] = (table * keep).astype(bf16)

    def prepare(tile):
        r = column_of(rate, tile)
        high, low = split(column_of(res, tile) * mode_gain(r) * jnp.exp(-r * lag))
        rows = slice(tile * PER_TILE, (tile + 1) * PER_TILE)
        base[rows, :] = dot(over, high) + dot(over, low)

    def by_roll(tile):
        for k in range(PER_TILE):
            line = jnp.broadcast_to(base[tile * PER_TILE + k : tile * PER_TILE + k + 1, :], (LANES, LANES))
            store(tile, k, pltpu.roll(line, 0, 1, stride=1, stride_axis=0))

    for tile in range(groups // PER_TILE):
        prepare(tile)
    for tile in range(groups // PER_TILE):
        by_roll(tile)


def with_before(halo, slot, own, at):
    rows = halo[:, at].astype(f32)[slot * HALO : (slot + 1) * HALO]
    return jnp.concatenate([jnp.concatenate([jnp.zeros_like(rows), rows]).astype(bf16), own[:, at]])


def shifted(table, x):
    return dot(table[...].reshape(-1, table.shape[2])[:, : x.shape[0]], x)


def short_conv(moved_rows, here, taps, index, at):
    total = taps[index, 0:1, at] * here
    for lag in range(1, TAPS):
        total = total + taps[index, lag : lag + 1, at] * moved_rows[(lag - 1) * LANES : lag * LANES]
    return total


def keys_values(k, v, halo, taps, before, e_tab, mixed, ks_out, vs_out, s_out, s_msg):
    modes = s_out.shape[0]
    own = own_group(modes)
    for at in each_tile(k.shape[1], 2 * LANES):
        ks = short_conv(shifted(before, with_before(halo, 0, k, at)), k[:, at].astype(f32), taps, 1, at)
        vs = short_conv(shifted(before, with_before(halo, 1, v, at)), v[:, at].astype(f32), taps, 2, at)
        ks_out[:, at] = ks
        vs_out[:, at] = vs
        mixed[:, at] = (ks * vs).astype(bf16)
        for half in (slice(at.start, at.start + LANES), slice(at.start + LANES, at.stop)):
            state = pick_rows(dot(e_tab[half, :], mixed[:, half]), own)
            s_out[:, half] = state
            s_msg[:, half] = state.astype(bf16)


def queries_short(q, halo, taps, before, qs_out):
    for at in each_tile(q.shape[1], 2 * LANES):
        qs_out[:, at] = short_conv(shifted(before, with_before(halo, 2, q, at)), q[:, at].astype(f32), taps, 0, at)


def lane_masks_bf16():
    return [jnp.where(m, 1.0, 0.0).astype(bf16) for m in own_group()]


def toeplitz_apply(table, x, out):
    own = lane_masks_bf16()
    for at in each_tile(x.shape[1]):
        part = x[:, at]
        stacked = jnp.concatenate([part * m for m in own], axis=0)
        out[:, at] = dot(table[at, :], stacked)


def joined(near, parts, at):
    total = near[:, at]
    for factor, message in zip(parts[0::2], parts[1::2]):
        total = total + factor[:, at] * message[:, at].astype(f32)
    return total


def gate(parts, within, near, *refs):
    links, (w, c_tab, qs, up, gain, conv_out, state_out, sums) = refs[:parts], refs[parts:]
    modes = near.shape[0]
    own = own_group(modes)
    squares = dots = jnp.zeros((LANES, LANES), f32)
    for at in each_tile(qs.shape[1]):
        state = joined(near, links, at)
        state_out[:, at] = state
        carried = spread_rows(state * w[:, at], own).astype(bf16)
        conv = within[:, at] + dot(c_tab[at, :], carried)
        conv_out[:, at] = conv
        gated = qs[:, at] * conv
        scaled = up[:, at].astype(f32) * gain[:, at]
        squares = squares + gated * gated
        dots = dots + scaled * gated
    line = lambda total: jnp.sum(total.T, axis=0, keepdims=True)
    sums[...] = jnp.where(iota((HALO, LANES), 0) < 4, line(squares), line(dots))


def norm_columns(sums, width):
    both = sums[...]
    inverse = lax.rsqrt(both[0:1] / width + epsilon)
    slope = inverse * inverse * inverse * both[4:5] / width
    wide = lambda line: jnp.broadcast_to(line, (LANES, LANES)).T
    return wide(inverse), wide(slope)


def grad_conv(width, sums, conv, qs, up, gain, w, c_tab_t, dconv, g_out, g_msg):
    modes = g_out.shape[0]
    own = own_group(modes)
    inverse, slope = norm_columns(sums, width)
    for at in each_tile(qs.shape[1]):
        q = qs[:, at]
        scaled = up[:, at].astype(f32) * gain[:, at]
        d_gated = inverse * scaled - (q * conv[:, at]) * slope
        d = (d_gated * q).astype(bf16)
        dconv[:, at] = d
        u = pick_rows(dot(c_tab_t[at, :], d), own)
        g = u * w[:, at]
        g_out[:, at] = g
        g_msg[:, at] = g.astype(bf16)


def edge_masks(lens, first):
    row = iota((HALO, LANES), 0)
    start = doc_start(lens, first + row)
    out = [None]
    for lag in range(1, TAPS):
        out.append(jnp.where((first + row - lag >= start) & (row < lag), 1.0, 0.0))
    return out


def tap_rows(rows_out, slot, d, x, edge, after, masks, at):
    back = shifted(after, d)
    head = d[:HALO].astype(f32) if d.dtype == f32 else d.astype(f32)[:HALO]
    rows_out[slot : slot + 1, at] = jnp.sum(d.astype(f32) * x, axis=0, keepdims=True)
    for lag in range(1, TAPS):
        prod = back[(lag - 1) * LANES : lag * LANES] * x
        total = prod[:HALO]
        for i in range(HALO, LANES, HALO):
            total = total + prod[i : i + HALO]
        mask = jnp.concatenate([masks[lag]] * (total.shape[1] // LANES), axis=1)
        total = total + head * (pltpu.roll(edge, lag, 0) * mask)
        rows_out[slot + lag : slot + lag + 1, at] = jnp.sum(total, axis=0, keepdims=True)


def query_side(width, sums, conv, qs, up, gain, q, halo, after, edges, out, dqs_out, rows_out):
    masks = edges
    inverse, slope = norm_columns(sums, width)
    for pair in each_tile(q.shape[1], 2 * LANES):
        for at in (slice(pair.start, pair.start + LANES), slice(pair.start + LANES, pair.stop)):
            c = conv[:, at]
            gated = qs[:, at] * c
            upstream = up[:, at].astype(f32)
            d_gated = inverse * (upstream * gain[:, at]) - gated * slope
            normed = gated * inverse
            out[:, at] = (normed * gain[:, at]).astype(bf16)
            dqs_out[:, at] = (d_gated * c).astype(bf16)
            rows_out[TAPS : TAPS + 1, at] = jnp.sum(upstream * normed, axis=0, keepdims=True)
        edge = halo[:, pair].astype(f32)[2 * HALO : 3 * HALO]
        d = dqs_out[:, pair]
        tap_rows(rows_out, 0, d, q[:, pair].astype(f32), edge, after, masks, pair)


def group_sums(parts):
    channels = parts.shape[1]
    high, low = split(parts)
    shape = (channels, channels // GROUP)
    belongs = jnp.where(iota(shape, 0) // GROUP == iota(shape, 1), 1.0, 0.0).astype(bf16)
    return dot(high, belongs) + dot(low, belongs)


def filter_grads(start_row, start_col, rate, dconv, mixed, state, own_pass, e_tab, c_tab, q0_out, q1_out, x_out, lines):
    modes, groups = rate.shape
    row, lane = iota((LANES, LANES), 0), iota((LANES, LANES), 1)
    keep = jnp.where((start_row[...] == start_col[...]) & (lane <= row), 1.0, 0.0)
    centred = (lane - LANES // 2).astype(f32)
    centred_row = (row - LANES // 2).astype(f32)
    later = (row + 1).astype(f32)
    lag_e = (LANES - 1 - lane).astype(f32)
    own_b = lane_masks_bf16()
    own = own_group(modes)
    for tile, at in enumerate(each_tile(dconv.shape[1])):
        d, m = dconv[:, at], mixed[:, at]
        stacked = jnp.concatenate([m * o for o in own_b], axis=0)
        outer = dot(d, stacked, NT)
        blocks = [outer[:, k * LANES : (k + 1) * LANES] * keep for k in range(PER_TILE)]
        outer = jnp.concatenate([b.astype(bf16) for b in blocks], axis=1)
        r = column_of(rate, tile)
        early = jnp.exp(r * centred)
        late = jnp.exp(-r * centred).T
        both = jnp.concatenate([early.T, (early * centred).T], axis=1).astype(bf16)
        wide = [jnp.concatenate([o, o], axis=1) for o in own_b]
        met = dot(outer, jnp.concatenate([both * o for o in wide], axis=0))
        near, near_lag = met[:, :LANES] * late, met[:, LANES:] * late
        s = state[:, at]
        far = dot(d, spread_rows(s, own).astype(bf16), NT) * c_tab[at, :].astype(f32)
        q0 = jnp.sum(near + far, axis=0, keepdims=True)
        q1 = jnp.sum(near * centred_row - near_lag + far * later, axis=0, keepdims=True)
        lines[tile : tile + 1, :] = q0
        lines[groups // PER_TILE + tile : groups // PER_TILE + tile + 1, :] = q1
        x = pick_rows(dot((e_tab[at, :].astype(f32) * lag_e).astype(bf16), m), own)
        x_out[:, at] = x + own_pass[:, at] * s
    pick = jnp.where(iota((modes, LANES), 1) % modes == iota((modes, LANES), 0), 1.0, 0.0).astype(bf16)
    mine = iota((PER_TILE, LANES), 1) // modes == iota((PER_TILE, LANES), 0)
    for begin, out in ((0, q0_out), (groups // PER_TILE, q1_out)):
        parts = [
            jnp.where(mine, jnp.broadcast_to(lines[begin + i : begin + i + 1, :], mine.shape), 0.0)
            for i in range(groups // PER_TILE)
        ]
        high, low = split(jnp.concatenate(parts, axis=0))
        out[...] = dot(pick, high, NT) + dot(pick, low, NT)


def first_grads(parts, near, *refs):
    links, (local, e_tab_t, ks, vs, dqs, later, rows_out) = refs[:parts], refs[parts:]
    own = own_group(near.shape[0])
    rows = 2 * HALO
    for tile, at in enumerate(each_tile(ks.shape[1])):
        g = joined(near, links, at)
        later[:, at] = g
        head = slice(tile * LANES, tile * LANES + rows)
        d_mixed = local[:rows, at] + dot(e_tab_t[head, :], spread_rows(g, own).astype(bf16))
        rows_out[:rows, at] = dqs[:rows, at]
        rows_out[rows : 2 * rows, at] = (d_mixed * vs[:rows, at]).astype(bf16)
        rows_out[2 * rows :, at] = (d_mixed * ks[:rows, at]).astype(bf16)


def grad_keys_values(
    res, rate, later, local, e_tab_t, ks, vs, k, v, halo, q0, q1, x, after, masks, dks_out, dvs_out, rows_out, flows
):
    modes = later.shape[0]
    own = own_group(modes)
    for pair in each_tile(k.shape[1], 2 * LANES):
        for at in (slice(pair.start, pair.start + LANES), slice(pair.start + LANES, pair.stop)):
            g = later[:, at]
            flows[:, at] = g * x[:, at]
            d_mixed = local[:, at] + dot(e_tab_t[at, :], spread_rows(g, own).astype(bf16))
            dks_out[:, at] = (d_mixed * vs[:, at]).astype(bf16)
            dvs_out[:, at] = (d_mixed * ks[:, at]).astype(bf16)
        edges = halo[:, pair].astype(f32)
        for slot, x_in, d_out in ((0, k, dks_out), (1, v, dvs_out)):
            edge = edges[slot * HALO : (slot + 1) * HALO]
            tap_rows(rows_out, slot * TAPS, d_out[:, pair], x_in[:, pair].astype(f32), edge, after, masks, pair)
    r = rate[...]
    gain = mode_gain(r)
    slope = jnp.exp(-2.0 * r) / gain
    q0_all = q0[...]
    d_res = gain * q0_all
    d_rate = res[...] * (slope * q0_all - gain * q1[...]) - group_sums(flows[...])
    groups = r.shape[1]
    for n in range(modes):
        at = slice(n * groups, (n + 1) * groups)
        rows_out[2 * TAPS : 2 * TAPS + 1, at] = d_res[n : n + 1]
        rows_out[2 * TAPS + 1 : 2 * TAPS + 2, at] = d_rate[n : n + 1]


def grad_inputs(filters, taps, after, edges, *refs):
    owns, outs = refs[: len(filters)], refs[len(filters) :]
    for index, own, out in zip(filters, owns, outs):
        begin = index * 2 * HALO
        for at in each_tile(own.shape[1], 2 * LANES):
            d = own[:, at]
            moved_rows = shifted(after, jnp.concatenate([d, edges[begin : begin + 2 * HALO, at]]))
            out[:, at] = short_conv(moved_rows, d.astype(f32), taps, index, at).astype(bf16)


def unpack(rows, *refs):
    others, (taps_out, res_out, rate_out, gain_out) = refs[:-4], refs[-4:]
    modes, groups = res_out.shape
    everything = rows[...].astype(f32) + others[0][...].astype(f32)
    if len(others) > 1:
        everything = everything + (others[1][...].astype(f32) + others[2][...].astype(f32))
    total_q, total = everything[:HALO], everything[HALO:]
    taps_out[0] = total_q[0:TAPS]
    taps_out[1] = total[0:TAPS]
    taps_out[2] = total[TAPS : 2 * TAPS]
    gain_out[...] = total_q[TAPS : TAPS + 1]
    for slot, out in ((2 * TAPS, res_out), (2 * TAPS + 1, rate_out)):
        for n in range(modes):
            out[n : n + 1, :] = total[slot : slot + 1, n * groups : (n + 1) * groups]


def moved(value, axis, steps):
    count = lax.axis_size(axis)
    first, last = max(0, -steps), min(count, count - steps)
    return lax.ppermute(value, axis, [(i, i + steps) for i in range(first, last)])


def swapped(value, axis, bits):
    return lax.ppermute(value, axis, [(i, i ^ bits) for i in range(lax.axis_size(axis))])


def after_all(value, *others):
    return lax.optimization_barrier((value, *others))[0]


def scanned(message, own, passes, beside=()):
    rounds = rounds_of(lax.axis_size("ctx"))
    near, at = None, 0
    for place, (below, meet) in enumerate(rounds):
        got = [swapped(message, "ctx", m << below) for m in range(1, meet)]
        factors, at = passes[at : at + meet - 1], at + meet - 1
        if place + 1 == len(rounds):
            links = [part for pair in zip(factors, got) for part in pair]
            return (jnp.zeros_like(own) if near is None else near), links
        for factor, other in zip(factors, got):
            part = factor * other.astype(f32)
            near = part if near is None else near + part
        own = passes[at] * own
        for factor, other in zip(passes[at + 1 : at + meet], got):
            own = own + factor * other.astype(f32)
        at += meet
        message = after_all(own.astype(bf16), *beside) if beside and not place else own.astype(bf16)


def on_device(q, k, v, taps, res, rate, gain, lens, up):
    rows, channels = q.shape
    groups, modes = rate.shape
    count = lax.axis_size("ctx")
    width = channels * lax.axis_size("ch")
    res, rate = res.T, rate.T
    gain = gain.reshape(1, channels)
    wide = lambda dtype: vmem((rows, channels), dtype)
    state_shape = vmem((modes, channels), f32)
    msg_shape = vmem((modes, channels), bf16)
    table = vmem((channels, LANES), bf16)
    shifts = (TAPS - 1, LANES, LANES + 2 * HALO)

    brought = [k, v, q, up, taps, res, rate, gain]
    last, k, v, q, up, taps, res, rate, gain = call(
        functools.partial(bring_in, len(brought)),
        [vmem((3 * HALO, channels), bf16)] + [vmem(a.shape, a.dtype) for a in brought],
        *brought, hbm=len(brought), name="bring_in",
        scratch=[pltpu.SemaphoreType.DMA((len(brought),))],
    )
    halo = moved(last, "ctx", 1)
    passes_each = pass_count(count)
    square = lambda dtype: vmem((LANES, LANES), dtype)
    e_tab, before, after, start_row, start_col, edges, in_prev, factors = call(
        functools.partial(first_tables, count),
        [table, vmem(shifts, bf16), vmem(shifts, bf16), square(jnp.int32), square(jnp.int32)]
        + [vmem((TAPS, HALO, LANES), f32), square(f32), vmem((2 + 4 * passes_each, LANES), f32)],
        lens, rate, smem=1, flops=4 << 20, name="first_tables",
    )
    mixed, ks, vs, own_state, state_msg = call(
        keys_values, [wide(bf16), wide(f32), wide(f32), state_shape, msg_shape],
        k, v, halo, taps, before, e_tab, flops=64 << 20, name="keys_values",
    )
    c_tab, c_tab_t, e_tab_t, w, own_pass, *passes = call(
        mode_tables, [table] * 3 + [state_shape] * (2 + 2 * passes_each),
        res, rate, e_tab, in_prev, factors, flops=4 << 20, name="mode_tables",
    )
    qs = call(queries_short, [wide(f32)], q, halo, taps, before, flops=8 << 20, name="queries_short")[0]
    near, links = scanned(state_msg, own_state, passes[:passes_each], (qs,))
    base = pltpu.VMEM((groups, LANES), f32)
    big = vmem((channels, PER_TILE * LANES), bf16)
    toep = call(
        functools.partial(toeplitz_tables, False), [big], res, rate, start_row, start_col, scratch=[base], flops=8 << 20, name="toeplitz",
    )[0]
    within = call(toeplitz_apply, [wide(f32)], toep, mixed, flops=512 << 20, name="within")[0]
    conv, state, sums = call(
        functools.partial(gate, len(links)), [wide(f32), state_shape, vmem((HALO, LANES), f32)],
        within, near, *links, w, c_tab, qs, up, gain, flops=64 << 20, name="gate",
    )
    toep_t = call(
        functools.partial(toeplitz_tables, True), [big], res, rate, start_row, start_col, scratch=[base], flops=8 << 20, name="toeplitz_t",
    )[0]
    bit = 1
    while bit < lax.axis_size("ch"):
        sums = sums + swapped(sums, "ch", bit)
        bit *= 2
    sums, toep_t = lax.optimization_barrier((sums, toep_t))
    dconv, own_grad, grad_msg = call(
        functools.partial(grad_conv, width), [wide(bf16), state_shape, msg_shape],
        sums, conv, qs, up, gain, w, c_tab_t, flops=64 << 20, name="grad_conv",
    )
    out, dqs, rows_q = call(
        functools.partial(query_side, width), [wide(bf16), wide(bf16), vmem((HALO, channels), f32)],
        sums, conv, qs, up, gain, q, halo, after, edges, flops=16 << 20, name="query_side",
    )
    local = call(toeplitz_apply, [wide(f32)], toep_t, dconv, flops=512 << 20, name="local_grad")[0]
    near, links = scanned(grad_msg, own_grad, passes[passes_each:], (local, rows_q))
    q0, q1, x = call(
        filter_grads, [vmem((modes, groups), f32)] * 2 + [state_shape],
        start_row, start_col, rate, dconv, mixed, state, own_pass, e_tab, c_tab,
        scratch=[pltpu.VMEM((2 * groups // PER_TILE, LANES), f32)], flops=512 << 20, name="filter_grads",
    )
    near, x = lax.optimization_barrier((near, x))
    later, first_rows = call(
        functools.partial(first_grads, len(links)), [state_shape, vmem((6 * HALO, channels), bf16)],
        near, *links, local, e_tab_t, ks, vs, dqs, flops=8 << 20, name="first_grads",
    )
    next_rows = moved(first_rows, "ctx", -1)
    dks, dvs, rows_kv = call(
        grad_keys_values, [wide(bf16), wide(bf16), vmem((2 * HALO, channels), f32)],
        res, rate, later, local, e_tab_t, ks, vs, k, v, halo, q0, q1, x, after, edges,
        scratch=[pltpu.VMEM((modes, channels), f32)], flops=64 << 20, name="grad_keys_values",
    )
    both = jnp.concatenate([rows_q, rows_kv]).astype(bf16)
    d_q = call(
        functools.partial(grad_inputs, (0,)), [wide(bf16)], taps, after, next_rows, dqs,
        flops=24 << 20, name="grad_queries",
    )[0]
    d_k, d_v = call(
        functools.partial(grad_inputs, (1, 2)), [wide(bf16)] * 2, taps, after, next_rows, dks, dvs,
        flops=24 << 20, name="grad_inputs",
    )
    rounds = rounds_of(count)
    for place, (below, meet) in enumerate(rounds):
        got = [swapped(both, "ctx", m << below) for m in range(1, meet)]
        if place + 1 < len(rounds):
            if place == 0:
                got[0], d_q = lax.optimization_barrier((got[0], d_q))
            both, got = both.astype(f32), [part.astype(f32) for part in got]
            both = ((both + got[0]) + (got[1] + got[2]) if meet == 4 else both + got[0]).astype(bf16)
    d_taps, d_res, d_rate, d_gain = call(
        unpack,
        [vmem(taps.shape, f32), vmem(res.shape, f32), vmem(rate.shape, f32), vmem((1, channels), f32)],
        both, *got, name="unpack",
    )
    return out, d_q, d_k, d_v, d_taps, d_res.T, d_rate.T, d_gain.reshape(channels)


def solution(mesh):
    wide = P("ctx", "ch")
    third, table, line = P(None, None, "ch"), P("ch", None), P("ch")
    return jax.shard_map(
        on_device,
        mesh=mesh,
        in_specs=(wide, wide, wide, third, table, table, line, P(), wide),
        out_specs=(wide, wide, wide, wide, third, table, table, line),
        check_vma=False,
    )
```

```python
import functools
import math

import jax
import jax.numpy as jnp
from jax import lax
from jax.experimental import pallas as pl
from jax.experimental.pallas import tpu as pltpu
from jax.sharding import PartitionSpec as P

GROUP = 16
TAPS = 7
HALO = 8
LANES = 128
PER_TILE = LANES // GROUP
SUB = 32
ROLLED = 1
BLOCKS = LANES // SUB
PER_LINE = LANES // SUB
epsilon = 1e-06
f32, bf16 = jnp.float32, jnp.bfloat16
highest = lax.Precision.HIGHEST
NN = (((1,), (0,)), ((), ()))
NT = (((1,), (1,)), ((), ()))


def dot(a, b, dims=NN, precision=None):
    return lax.dot_general(a, b, dims, precision=precision, preferred_element_type=f32)


def iota(shape, dim):
    return lax.broadcasted_iota(jnp.int32, shape, dim)


def docs_at(lens, positions):
    start = jnp.int32(0)
    count = jnp.zeros_like(positions)
    for k in range(lens.shape[0]):
        count = count + jnp.where(positions >= start, 1, 0)
        start = start + lens[k]
    return count - 1


def starts_at(lens):
    out = [jnp.int32(0)]
    for k in range(lens.shape[0] - 1):
        out.append(out[-1] + lens[k])
    return out


def doc_start(lens, positions):
    start = jnp.full_like(positions, 0)
    for s in starts_at(lens)[1:]:
        start = jnp.where(positions >= s, s, start)
    return start


def next_start(lens, positions):
    after = jnp.full_like(positions, jnp.iinfo(jnp.int32).max)
    for s in starts_at(lens)[:0:-1]:
        after = jnp.where(positions < s, s, after)
    return after


def one_minus_exp(x):
    series = x * (1 - x / 2 * (1 - x / 3 * (1 - x / 4 * (1 - x / 5 * (1 - x / 6 * (1 - x / 7))))))
    return jnp.where(x < 0.125, series, 1 - jnp.exp(-x))


def own_group(rows=LANES):
    return [iota((rows, LANES), 1) // GROUP == k for k in range(PER_TILE)]


def spread_rows(per_mode, masks):
    return jnp.concatenate([jnp.where(m, per_mode, 0.0) for m in masks], axis=0)


def pick_rows(full, masks):
    modes = full.shape[0] // PER_TILE
    total = jnp.where(masks[0], full[:modes], 0.0)
    for k in range(1, PER_TILE):
        total = jnp.where(masks[k], full[k * modes : (k + 1) * modes], total)
    return total


def column_of(ref, tile):
    modes = ref.shape[0]
    part = [ref[:, tile * PER_TILE + k : tile * PER_TILE + k + 1] for k in range(PER_TILE)]
    return jnp.concatenate([jnp.broadcast_to(p, (modes, LANES)) for p in part], axis=0)


def mode_gain(rate):
    return jnp.sqrt(one_minus_exp(2.0 * rate))


def each_tile(channels, width=LANES):
    return [slice(i, i + width) for i in range(0, channels, width)]


def vmem(shape, dtype):
    return jax.ShapeDtypeStruct(shape, dtype)


def call(body, outs, *args, smem=0, hbm=0, scratch=(), flops=0, name=None, limit=32):
    moved = sum(a.size * a.dtype.itemsize for a in args) + sum(
        math.prod(o.shape) * o.dtype.itemsize for o in outs
    )
    if hbm:
        args = (*args[:-hbm], *[pltpu.with_memory_space_constraint(a, pltpu.HBM) for a in args[-hbm:]])
        outs = [pltpu.VMEM(o.shape, o.dtype) for o in outs]
    return pl.pallas_call(
        body,
        out_shape=tuple(outs),
        in_specs=[pl.BlockSpec(memory_space=pltpu.SMEM)] * smem
        + [pl.BlockSpec(memory_space=pltpu.VMEM)] * (len(args) - smem - hbm)
        + [pl.BlockSpec(memory_space=pltpu.HBM)] * hbm,
        out_specs=tuple([pl.BlockSpec(memory_space=pltpu.VMEM)] * len(outs)),
        scratch_shapes=list(scratch),
        compiler_params=pltpu.CompilerParams(vmem_limit_bytes=limit << 20),
        cost_estimate=pl.CostEstimate(flops=flops, bytes_accessed=moved, transcendentals=0),
        name=name,
    )(*args)


def bring_in(arrays, *refs):
    sources, out, targets, sems = refs[:arrays], refs[arrays], refs[arrays + 1 : -1], refs[-1]
    copies = [pltpu.make_async_copy(a, b, sems.at[i]) for i, (a, b) in enumerate(zip(sources, targets))]
    for copy in copies:
        copy.start()
    for slot, (copy, ref) in enumerate(zip(copies, targets[:3])):
        copy.wait()
        rows = ref.shape[0]
        tail = ref[rows - 2 * HALO :, :].astype(f32)[HALO:]
        out[slot * HALO : (slot + 1) * HALO, :] = tail.astype(bf16)
    for copy in copies[3:]:
        copy.wait()


def shift_rows(table, lens, first, sign):
    shape = table.shape[1:]
    pos = first + iota((LANES, LANES), 0)
    limit = doc_start(lens, pos) if sign < 0 else next_start(lens, pos)
    limit = jnp.concatenate([limit, limit], axis=1)[:, : shape[1]]
    row, col = iota(shape, 0), iota(shape, 1)
    source = first + col - (2 * HALO if sign < 0 else 0)
    apart = col - row - (2 * HALO if sign < 0 else 0)
    apart = jnp.where(source >= limit if sign < 0 else source < limit, apart * sign, 0)
    for lag in range(1, TAPS):
        table[lag - 1] = jnp.where(apart == lag, 1.0, 0.0).astype(bf16)


def rounds_of(count):
    out, below = [], 0
    while count >> below > 1:
        meet = min(4, count >> below)
        out.append((below, meet))
        below += meet.bit_length() - 1
    return out


def pass_count(count):
    rounds = rounds_of(count)
    return sum(meet - 1 for _, meet in rounds) + sum(meet for _, meet in rounds[:-1])


def pass_factors(lens, me, count, forward):
    ends = lambda device: docs_at(lens, device * LANES + LANES - 1)
    out = []
    rounds = rounds_of(count)
    for place, (below, meet) in enumerate(rounds):
        size, mine = 1 << below, me >> below
        wide = size * meet
        start = (me // wide) * wide
        for m in range(1, meet):
            other = mine ^ m
            if forward:
                edge = other * size + size - 1
                lag, meets, valid = me - 1 - edge, ends(edge) == ends(me - 1), other < mine
            else:
                edge = other * size - 1
                lag, meets, valid = edge - me, ends(edge) == ends(me), other > mine
            out.append((lag, jnp.where(meets & valid, 1.0, 0.0)))
        if place + 1 == len(rounds):
            continue
        for m in range(meet):
            other = mine ^ m
            if forward:
                edge, far = other * size + size - 1, start + wide - 1
                lag = far - edge
            else:
                edge, far = other * size - 1, start - 1
                lag = edge - far
            out.append((lag, jnp.where(ends(edge) == ends(far), 1.0, 0.0)))
    return out


def first_tables(count, lens, res, rate, e_tab, before, after, start_row, start_col, edges, in_prev, in_sub, factors, weight, back_keep):
    me = lax.axis_index("ctx")
    first = me * LANES
    shift_rows(before, lens, first, -1)
    lane = iota((LANES, LANES), 1)
    last = first + LANES - 1
    in_last = jnp.where(docs_at(lens, first + lane) == docs_at(lens, last), 1.0, 0.0)
    lag = (LANES - 1 - lane).astype(f32)
    for tile in range(rate.shape[1] // PER_TILE):
        e = jnp.exp(-column_of(rate, tile) * lag) * in_last
        e_tab[tile * LANES : (tile + 1) * LANES, :] = e.astype(bf16)
    shift_rows(after, lens, first, 1)
    row = first + iota((LANES, LANES), 0)
    start = doc_start(lens, row)
    start_row[...] = start
    start_col[...] = doc_start(lens, first + lane)
    for lag in range(1, ROLLED + 1):
        back_keep[lag - 1] = jnp.where(row - lag >= start, 1.0, 0.0)
    weight[...] = res[...] * mode_gain(rate[...])
    row_in, lane_in = iota((LANES, LANES), 0) % SUB, lane % SUB
    same = doc_start(lens, row - row_in + lane_in) == start
    in_sub[0] = jnp.where(same & (lane_in <= row_in), 1.0, 0.0)
    in_sub[1] = jnp.where(same & (lane_in >= row_in), 1.0, 0.0)
    ends, here = doc_start(lens, first + lane - lane_in + (SUB - 1)), doc_start(lens, first + lane)
    in_sub[2] = jnp.where(ends == here, 1.0, 0.0)
    in_sub[3] = jnp.where((here < first + lane - lane_in) & (lane >= SUB), 1.0, 0.0)
    for lag, mask in enumerate(edge_masks(lens, first)):
        if lag:
            edges[lag] = mask
    doc_prev = docs_at(lens, first - 1)
    in_prev[...] = jnp.where(docs_at(lens, first + lane) == doc_prev, 1.0, 0.0)
    pairs = [(jnp.int32(1), jnp.where(docs_at(lens, last) == doc_prev, float(LANES), 0.0))]
    pairs += pass_factors(lens, me, count, True) + pass_factors(lens, me, count, False)
    ends = [docs_at(lens, first + SUB * block + SUB - 1) for block in range(BLOCKS)]
    blocks = [(jnp.int32(0), jnp.where(a == b, 1.0, 0.0)) for a, b in zip(ends[:-1], ends[1:])]
    pairs += blocks
    for place, (steps, mask) in enumerate(pairs):
        scale = -(jnp.maximum(steps, 0) * LANES).astype(f32)
        factors[2 * place : 2 * place + 1, :] = jnp.full((1, LANES), scale, f32)
        factors[2 * place + 1 : 2 * place + 2, :] = jnp.full((1, LANES), mask, f32)


def mode_tables(
    weight, rate, e_tab, in_prev, in_sub, factors, c_tab, c_tab_t, e_tab_t, to_end, to_end_t, on, on_t, w_out, sub_pass, *passes
):
    modes = rate.shape[0]
    lag = (iota((LANES, LANES), 1) + 1).astype(f32)
    masks = own_group(modes)
    mask, mask_end, mask_on = in_prev[...], in_sub[2], in_sub[3]
    lane_in = iota((LANES, LANES), 1) % SUB
    lag_end, lag_on = (SUB - 1 - lane_in).astype(f32), (lane_in + 1).astype(f32)
    for tile in range(rate.shape[1] // PER_TILE):
        at = slice(tile * LANES, (tile + 1) * LANES)
        r_col = column_of(rate, tile)
        c = jnp.exp(-r_col * lag) * mask
        c_tab_t[at, :] = c.astype(bf16)
        c_tab[at, :] = c.T.astype(bf16)
        e_tab_t[at, :] = e_tab[at, :].astype(f32).T.astype(bf16)
        end = jnp.exp(-r_col * lag_end) * mask_end
        to_end[at, :] = end.astype(bf16)
        to_end_t[at, :] = end.T.astype(bf16)
        on_block = jnp.exp(-r_col * lag_on) * mask_on
        on[at, :] = on_block.T.astype(bf16)
        on_t[at, :] = on_block.astype(bf16)
        r_tile = pick_rows(r_col, masks)
        sub_pass[:, at] = jnp.exp(-r_tile * float(SUB))
        w_out[:, at] = pick_rows(column_of(weight, tile), masks)
        for place, out in enumerate(passes):
            scale, keep = factors[2 * place : 2 * place + 1, :], factors[2 * place + 1 : 2 * place + 2, :]
            out[:, at] = jnp.exp(r_tile * scale) * keep


def split(x):
    high = x.astype(bf16)
    return high, (x - high.astype(f32)).astype(bf16)


def block_tables(transposed, weight, rate, in_sub, table, lines):
    modes, groups = rate.shape
    depth = PER_LINE * modes
    row, lane = iota((depth, LANES), 0) // modes, iota((depth, LANES), 1)
    inside = lane % SUB
    if transposed:
        own, lag = lane // SUB == row, inside
    else:
        back = jnp.where(inside > 0, 1, 0)
        own, lag = (lane // SUB + back) % PER_LINE == row, (SUB - inside) % SUB
    own, lag = jnp.where(own, 1.0, 0.0), lag.astype(f32)
    halves = PER_TILE // PER_LINE
    for tile in range(groups // PER_TILE):
        r_all = column_of(rate, tile)
        w_all = column_of(weight, tile)
        for half in range(halves):
            deep = slice(half * depth, (half + 1) * depth)
            place = tile * halves + half
            terms = w_all[deep] * jnp.exp(-r_all[deep] * lag) * own
            lines[place : place + 1, :] = jnp.sum(terms, axis=0, keepdims=True)
    keep = in_sub[1 if transposed else 0]
    for tile in range(groups // PER_TILE):
        for half in range(halves):
            place = tile * halves + half
            line = jnp.broadcast_to(lines[place : place + 1, :], (SUB, LANES))
            rolled = pltpu.roll(line, 0, 1, stride=1, stride_axis=0)
            full = jnp.concatenate([rolled] * BLOCKS, axis=0) * keep
            table[tile * LANES : (tile + 1) * LANES, half * LANES : (half + 1) * LANES] = full.astype(bf16)


def with_before(halo, slot, own, at):
    rows = halo[:, at].astype(f32)[slot * HALO : (slot + 1) * HALO]
    return jnp.concatenate([jnp.concatenate([jnp.zeros_like(rows), rows]).astype(bf16), own[:, at]])


def shifted(table, x):
    return dot(table[...].reshape(-1, table.shape[2])[:, : x.shape[0]], x)


def short_conv(moved_rows, here, taps, index, at):
    total = taps[index, 0:1, at] * here
    for lag in range(1, TAPS):
        total = total + taps[index, lag : lag + 1, at] * moved_rows[(lag - 1) * LANES : lag * LANES]
    return total


def back_conv(before, keep, halo, slot, own, taps, index, at):
    edge = halo[:, at].astype(f32)[slot * HALO : (slot + 1) * HALO]
    ext = jnp.concatenate([jnp.concatenate([jnp.zeros_like(edge), edge]).astype(bf16), own[:, at]])
    far = dot(before[...].reshape(-1, before.shape[2])[ROLLED * LANES :], ext)
    here = own[:, at].astype(f32)
    total = taps[index, 0:1, at] * here
    row = iota(edge.shape, 0)
    copies = here.shape[1] // LANES
    for lag in range(1, TAPS):
        if lag <= ROLLED:
            part = pltpu.roll(here, lag, 0)
            head = jnp.where(row < lag, pltpu.roll(edge, lag, 0), part[:HALO])
            part = jnp.concatenate([head, part[HALO:]]) * jnp.concatenate([keep[lag - 1]] * copies, axis=1)
        else:
            part = far[(lag - 1 - ROLLED) * LANES : (lag - ROLLED) * LANES]
        total = total + taps[index, lag : lag + 1, at] * part
    return total


def keys_values(k, v, halo, taps, before, keep, e_tab, mixed, ks_out, vs_out, s_out, s_msg):
    modes = s_out.shape[0]
    own = own_group(modes)
    for at in each_tile(k.shape[1], 2 * LANES):
        ks = back_conv(before, keep, halo, 0, k, taps, 1, at)
        vs = back_conv(before, keep, halo, 1, v, taps, 2, at)
        ks_out[:, at] = ks
        vs_out[:, at] = vs
        mixed[:, at] = (ks * vs).astype(bf16)
    for at in each_tile(k.shape[1]):
        state = pick_rows(dot(e_tab[at, :], mixed[:, at]), own)
        s_out[:, at] = state
        s_msg[:, at] = state.astype(bf16)


def queries_short(q, halo, taps, before, qs_out):
    for at in each_tile(q.shape[1], 2 * LANES):
        qs_out[:, at] = short_conv(shifted(before, with_before(halo, 2, q, at)), q[:, at].astype(f32), taps, 0, at)


def lane_masks_bf16():
    return [jnp.where(m, 1.0, 0.0).astype(bf16) for m in own_group()]


def across_blocks(x, gather, spread, w, carry, own, masks, forward):
    block_of = iota((1, LANES), 1) // SUB
    inner = range(BLOCKS - 1) if forward else range(1, BLOCKS)
    picks = [gather * jnp.where(block_of == b, 1.0, 0.0).astype(bf16) for b in inner]
    full = dot(jnp.concatenate(picks, axis=0), x)
    parts = [pick_rows(full[i * LANES : (i + 1) * LANES], own) for i in range(BLOCKS - 1)]
    zero = jnp.zeros((SUB, LANES), f32)
    out = [zero] * BLOCKS
    total = None
    for i in range(BLOCKS - 1) if forward else range(BLOCKS - 2, -1, -1):
        total = parts[i] if total is None else parts[i] + total * (carry * masks[i - forward])
        to = i + 1 if forward else i
        high, low = split(spread_rows(total * w, own))
        lhs = spread[to * SUB : (to + 1) * SUB]
        out[to] = dot(jnp.concatenate([lhs, lhs], axis=1), jnp.concatenate([high, low], axis=0))
    return jnp.concatenate(out, axis=0)


def apply_filter(forward, table, gather, spread, w, sub_pass, factors, x, out):
    modes = w.shape[0]
    own_b = [m[:SUB] for m in lane_masks_bf16()]
    own = own_group(modes)
    first = factors.shape[0] - 2 * (BLOCKS - 1)
    masks = [factors[first + 2 * b + 1 : first + 2 * b + 2, :] for b in range(BLOCKS - 1)]
    for at in each_tile(x.shape[1]):
        part = x[:, at]
        near = []
        for block in range(BLOCKS):
            rows = slice(block * SUB, (block + 1) * SUB)
            stacked = jnp.concatenate([part[rows] * m for m in own_b], axis=0)
            near.append(dot(table[at.start + block * SUB : at.start + (block + 1) * SUB, :], stacked))
        carry = sub_pass[:, at]
        far = across_blocks(part, gather[at, :], spread[at, :], w[:, at], carry, own, masks, forward)
        out[:, at] = jnp.concatenate(near, axis=0) + far


def joined(near, parts, at):
    total = near[:, at]
    for factor, message in zip(parts[0::2], parts[1::2]):
        total = total + factor[:, at] * message[: total.shape[0], at].astype(f32)
    return total


def gate(parts, within, near, *refs):
    links, (w, c_tab, qs, up, gain, conv_out, state_out, sums) = refs[:parts], refs[parts:]
    modes = near.shape[0]
    own = own_group(modes)
    squares = dots = jnp.zeros((LANES, LANES), f32)
    for at in each_tile(qs.shape[1]):
        state = joined(near, links, at)
        state_out[:, at] = state
        carried = spread_rows(state * w[:, at], own).astype(bf16)
        conv = within[:, at] + dot(c_tab[at, :], carried)
        conv_out[:, at] = conv
        gated = qs[:, at] * conv
        scaled = up[:, at].astype(f32) * gain[:, at]
        squares = squares + gated * gated
        dots = dots + scaled * gated
    line = lambda total: jnp.sum(total.T, axis=0, keepdims=True)
    sums[...] = jnp.where(iota((HALO, LANES), 0) < 4, line(squares), line(dots))


def norm_columns(sums, width):
    both = sums[...]
    inverse = lax.rsqrt(both[0:1] / width + epsilon)
    slope = inverse * inverse * inverse * both[4:5] / width
    wide = lambda line: jnp.broadcast_to(line, (LANES, LANES)).T
    return wide(inverse), wide(slope)


def grad_conv(width, sums, conv, qs, up, gain, w, c_tab_t, dconv, g_out, g_msg):
    modes = g_out.shape[0]
    own = own_group(modes)
    inverse, slope = norm_columns(sums, width)
    for at in each_tile(qs.shape[1]):
        q = qs[:, at]
        scaled = up[:, at].astype(f32) * gain[:, at]
        d_gated = inverse * scaled - (q * conv[:, at]) * slope
        d = (d_gated * q).astype(bf16)
        dconv[:, at] = d
        u = pick_rows(dot(c_tab_t[at, :], d), own)
        g = u * w[:, at]
        g_out[:, at] = g
        g_msg[:, at] = g.astype(bf16)


def edge_masks(lens, first):
    row = iota((HALO, LANES), 0)
    start = doc_start(lens, first + row)
    out = [None]
    for lag in range(1, TAPS):
        out.append(jnp.where((first + row - lag >= start) & (row < lag), 1.0, 0.0))
    return out


def tap_rows(rows_out, slot, d, x, edge, after, masks, at):
    back = shifted(after, d)
    head = d[:HALO].astype(f32) if d.dtype == f32 else d.astype(f32)[:HALO]
    rows_out[slot : slot + 1, at] = jnp.sum(d.astype(f32) * x, axis=0, keepdims=True)
    for lag in range(1, TAPS):
        prod = back[(lag - 1) * LANES : lag * LANES] * x
        total = prod[:HALO]
        for i in range(HALO, LANES, HALO):
            total = total + prod[i : i + HALO]
        mask = jnp.concatenate([masks[lag]] * (total.shape[1] // LANES), axis=1)
        total = total + head * (pltpu.roll(edge, lag, 0) * mask)
        rows_out[slot + lag : slot + lag + 1, at] = jnp.sum(total, axis=0, keepdims=True)


def query_side(width, sums, conv, qs, up, gain, q, halo, after, edges, out, dqs_out, rows_out):
    masks = edges
    inverse, slope = norm_columns(sums, width)
    for pair in each_tile(q.shape[1], 2 * LANES):
        for at in (slice(pair.start, pair.start + LANES), slice(pair.start + LANES, pair.stop)):
            c = conv[:, at]
            gated = qs[:, at] * c
            upstream = up[:, at].astype(f32)
            d_gated = inverse * (upstream * gain[:, at]) - gated * slope
            normed = gated * inverse
            out[:, at] = (normed * gain[:, at]).astype(bf16)
            dqs_out[:, at] = (d_gated * c).astype(bf16)
            rows_out[TAPS : TAPS + 1, at] = jnp.sum(upstream * normed, axis=0, keepdims=True)
        edge = halo[:, pair].astype(f32)[2 * HALO : 3 * HALO]
        tap_rows(rows_out, 0, dqs_out[:, pair], q[:, pair].astype(f32), edge, after, masks, pair)


def group_sums(parts):
    channels = parts.shape[1]
    high, low = split(parts)
    shape = (channels, channels // GROUP)
    belongs = jnp.where(iota(shape, 0) // GROUP == iota(shape, 1), 1.0, 0.0).astype(bf16)
    return dot(high, belongs) + dot(low, belongs)


def filter_tables(rate, mixed, state, own_pass, e_tab, late_out, both_out, x_out):
    modes, groups = rate.shape
    lane = iota((LANES, LANES), 1)
    centred = (lane - LANES // 2).astype(f32)
    lag_e = (LANES - 1 - lane).astype(f32)
    own = own_group(modes)
    for tile, at in enumerate(each_tile(mixed.shape[1])):
        r = column_of(rate, tile)
        early = jnp.exp(r * centred)
        late_out[at, :] = jnp.exp(-r * centred).T
        both_out[at, :] = jnp.concatenate([early.T, (early * centred).T], axis=1).astype(bf16)
        x = pick_rows(dot((e_tab[at, :].astype(f32) * lag_e).astype(bf16), mixed[:, at]), own)
        x_out[:, at] = x + own_pass[:, at] * state[:, at]


def filter_grads(start_row, start_col, dconv, mixed, state, late, both, c_tab, q0_out, q1_out, lines):
    modes, groups = q0_out.shape
    row, lane = iota((LANES, LANES), 0), iota((LANES, LANES), 1)
    keep = jnp.where((start_row[...] == start_col[...]) & (lane <= row), 1.0, 0.0)
    centred_row = (row - LANES // 2).astype(f32)
    later = (row + 1).astype(f32)
    own_b = lane_masks_bf16()
    wide = [jnp.concatenate([o, o], axis=1) for o in own_b]
    own = own_group(modes)
    for tile, at in enumerate(each_tile(dconv.shape[1])):
        d, m = dconv[:, at], mixed[:, at]
        stacked = jnp.concatenate([m * o for o in own_b], axis=0)
        outer = dot(d, stacked, NT)
        blocks = [outer[:, k * LANES : (k + 1) * LANES] * keep for k in range(PER_TILE)]
        outer = jnp.concatenate([b.astype(bf16) for b in blocks], axis=1)
        pair = both[at, :]
        met = dot(outer, jnp.concatenate([pair * o for o in wide], axis=0))
        near, near_lag = met[:, :LANES] * late[at, :], met[:, LANES:] * late[at, :]
        far = dot(d, spread_rows(state[:, at], own).astype(bf16), NT) * c_tab[at, :].astype(f32)
        q0 = jnp.sum(near + far, axis=0, keepdims=True)
        q1 = jnp.sum(near * centred_row - near_lag + far * later, axis=0, keepdims=True)
        lines[tile : tile + 1, :] = q0
        lines[groups // PER_TILE + tile : groups // PER_TILE + tile + 1, :] = q1
    pick = jnp.where(iota((modes, LANES), 1) % modes == iota((modes, LANES), 0), 1.0, 0.0).astype(bf16)
    mine = iota((PER_TILE, LANES), 1) // modes == iota((PER_TILE, LANES), 0)
    for begin, out in ((0, q0_out), (groups // PER_TILE, q1_out)):
        parts = [
            jnp.where(mine, jnp.broadcast_to(lines[begin + i : begin + i + 1, :], mine.shape), 0.0)
            for i in range(groups // PER_TILE)
        ]
        high, low = split(jnp.concatenate(parts, axis=0))
        out[...] = dot(pick, high, NT) + dot(pick, low, NT)


def first_grads(parts, near, *refs):
    links, (local, e_tab_t, ks, vs, dqs, later, rows_out) = refs[:parts], refs[parts:]
    own = own_group(near.shape[0])
    rows = 2 * HALO
    for tile, at in enumerate(each_tile(ks.shape[1])):
        g = joined(near, links, at)
        later[:, at] = g
        head = slice(tile * LANES, tile * LANES + rows)
        d_mixed = local[:rows, at] + dot(e_tab_t[head, :], spread_rows(g, own).astype(bf16))
        rows_out[:rows, at] = dqs[:rows, at]
        rows_out[rows : 2 * rows, at] = (d_mixed * vs[:rows, at]).astype(bf16)
        rows_out[2 * rows :, at] = (d_mixed * ks[:rows, at]).astype(bf16)


def grad_keys_values(
    res, rate, later, local, e_tab_t, ks, vs, k, v, halo, q0, q1, x, after, masks, dks_out, dvs_out, rows_out, flows
):
    modes = later.shape[0]
    own = own_group(modes)
    for at in each_tile(k.shape[1]):
        g = later[:, at]
        flows[:, at] = g * x[:, at]
        d_mixed = local[:, at] + dot(e_tab_t[at, :], spread_rows(g, own).astype(bf16))
        dks_out[:, at] = (d_mixed * vs[:, at]).astype(bf16)
        dvs_out[:, at] = (d_mixed * ks[:, at]).astype(bf16)
    for pair in each_tile(k.shape[1], 2 * LANES):
        edges = halo[:, pair].astype(f32)
        for slot, x_in, d_out in ((0, k, dks_out), (1, v, dvs_out)):
            edge = edges[slot * HALO : (slot + 1) * HALO]
            tap_rows(rows_out, slot * TAPS, d_out[:, pair], x_in[:, pair].astype(f32), edge, after, masks, pair)
    r = rate[...]
    gain = mode_gain(r)
    slope = jnp.exp(-2.0 * r) / gain
    q0_all = q0[...]
    d_res = gain * q0_all
    d_rate = res[...] * (slope * q0_all - gain * q1[...]) - group_sums(flows[...])
    groups = r.shape[1]
    for n in range(modes):
        at = slice(n * groups, (n + 1) * groups)
        rows_out[2 * TAPS : 2 * TAPS + 1, at] = d_res[n : n + 1]
        rows_out[2 * TAPS + 1 : 2 * TAPS + 2, at] = d_rate[n : n + 1]


def grad_inputs(filters, taps, after, edges, *refs):
    owns, outs = refs[: len(filters)], refs[len(filters) :]
    for index, own, out in zip(filters, owns, outs):
        begin = index * 2 * HALO
        for at in each_tile(own.shape[1], 2 * LANES):
            d = own[:, at]
            moved_rows = shifted(after, jnp.concatenate([d, edges[begin : begin + 2 * HALO, at]]))
            out[:, at] = short_conv(moved_rows, d.astype(f32), taps, index, at).astype(bf16)


def unpack(rows_q, rows, *refs):
    others, (taps_out, res_out, rate_out, gain_out) = refs[:-4], refs[-4:]
    modes, groups = res_out.shape
    total_q, total = rows_q[...], met(rows[...], [other[...] for other in others])
    taps_out[0] = total_q[0:TAPS]
    taps_out[1] = total[0:TAPS]
    taps_out[2] = total[TAPS : 2 * TAPS]
    gain_out[...] = total_q[TAPS : TAPS + 1]
    for slot, out in ((2 * TAPS, res_out), (2 * TAPS + 1, rate_out)):
        for n in range(modes):
            out[n : n + 1, :] = total[slot : slot + 1, n * groups : (n + 1) * groups]


def moved(value, axis, steps):
    count = lax.axis_size(axis)
    first, last = max(0, -steps), min(count, count - steps)
    return lax.ppermute(value, axis, [(i, i + steps) for i in range(first, last)])


def swapped(value, axis, bits):
    return lax.ppermute(value, axis, [(i, i ^ bits) for i in range(lax.axis_size(axis))])


def after_all(value, *others):
    return lax.optimization_barrier((value, *others))[0]


def met(own, got):
    own, got = own.astype(f32), [part.astype(f32) for part in got]
    return (own + got[0]) + (got[1] + got[2]) if len(got) == 3 else own + got[0]


def scanned(message, own, passes, beside=(), rows=None):
    rounds = rounds_of(lax.axis_size("ctx"))
    modes = own.shape[0]
    near, at = None, 0
    for place, (below, meet) in enumerate(rounds):
        last = place + 1 == len(rounds)
        if last and rows is not None:
            rows = rows.astype(bf16)
            message = jnp.concatenate([message, rows])
        got = [swapped(message, "ctx", m << below) for m in range(1, meet)]
        factors, at = passes[at : at + meet - 1], at + meet - 1
        if last:
            links = [part for pair in zip(factors, got) for part in pair]
            rows = None if rows is None else met(rows, [part[modes:] for part in got])
            return (jnp.zeros_like(own) if near is None else near), links, rows
        for factor, other in zip(factors, got):
            part = factor * other.astype(f32)
            near = part if near is None else near + part
        own = passes[at] * own
        for factor, other in zip(passes[at + 1 : at + meet], got):
            own = own + factor * other.astype(f32)
        at += meet
        message = after_all(own.astype(bf16), *beside) if beside and not place else own.astype(bf16)


def on_device(q, k, v, taps, res, rate, gain, lens, up):
    rows, channels = q.shape
    groups, modes = rate.shape
    count = lax.axis_size("ctx")
    width = channels * lax.axis_size("ch")
    res, rate = res.T, rate.T
    gain = gain.reshape(1, channels)
    wide = lambda dtype: vmem((rows, channels), dtype)
    state_shape = vmem((modes, channels), f32)
    msg_shape = vmem((modes, channels), bf16)
    table = vmem((channels, LANES), bf16)
    shifts = (TAPS - 1, LANES, LANES + 2 * HALO)

    brought = [k, v, q, up, taps, res, rate, gain]
    last, k, v, q, up, taps, res, rate, gain = call(
        functools.partial(bring_in, len(brought)),
        [vmem((3 * HALO, channels), bf16)] + [vmem(a.shape, a.dtype) for a in brought],
        *brought, hbm=len(brought), name="bring_in",
        scratch=[pltpu.SemaphoreType.DMA((len(brought),))],
    )
    halo = moved(last, "ctx", 1)
    passes_each = pass_count(count)
    square = lambda dtype: vmem((LANES, LANES), dtype)
    e_tab, before, after, start_row, start_col, edges, in_prev, in_sub, factors, weight, back_keep = call(
        functools.partial(first_tables, count),
        [table, vmem(shifts, bf16), vmem(shifts, bf16), square(jnp.int32), square(jnp.int32)]
        + [vmem((TAPS, HALO, LANES), f32), square(f32), vmem((4, LANES, LANES), f32)]
        + [vmem((2 * (1 + 2 * passes_each + BLOCKS - 1), LANES), f32), vmem(res.shape, f32)]
        + [vmem((ROLLED, LANES, LANES), f32)],
        lens, res, rate, smem=1, flops=4 << 20, name="first_tables",
    )
    blocked = [vmem((channels, PER_TILE * SUB), bf16)]
    lines = [pltpu.VMEM((groups // PER_LINE, LANES), f32)]
    near_tab = call(
        functools.partial(block_tables, False), blocked, weight, rate, in_sub, scratch=lines, flops=4 << 20, name="block_tables",
    )[0]
    halo, near_tab = lax.optimization_barrier((halo, near_tab))
    mixed, ks, vs, own_state, state_msg = call(
        keys_values, [wide(bf16), wide(f32), wide(f32), state_shape, msg_shape],
        k, v, halo, taps, before, back_keep, e_tab, flops=64 << 20, name="keys_values",
    )
    c_tab, c_tab_t, e_tab_t, to_end, to_end_t, on, on_t, w, sub_pass, own_pass, *passes = call(
        mode_tables, [table] * 7 + [state_shape] * (3 + 2 * passes_each),
        weight, rate, e_tab, in_prev, in_sub, factors, flops=4 << 20, name="mode_tables",
    )
    qs = call(queries_short, [wide(f32)], q, halo, taps, before, flops=8 << 20, name="queries_short")[0]
    near, links, _ = scanned(state_msg, own_state, passes[:passes_each], (qs,))
    within = call(
        functools.partial(apply_filter, True), [wide(f32)], near_tab, to_end, on, w, sub_pass, factors, mixed,
        flops=256 << 20, name="within",
    )[0]
    conv, state, sums = call(
        functools.partial(gate, len(links)), [wide(f32), state_shape, vmem((HALO, LANES), f32)],
        within, near, *links, w, c_tab, qs, up, gain, flops=64 << 20, name="gate",
    )
    rate_here = after_all(rate, sums)
    near_tab_t = call(
        functools.partial(block_tables, True), blocked, weight, rate_here, in_sub, scratch=lines, flops=4 << 20, name="block_tables_t",
    )[0]
    late, both, x = call(
        filter_tables, [vmem((channels, LANES), f32), vmem((channels, 2 * LANES), bf16), state_shape],
        rate_here, mixed, state, own_pass, e_tab, flops=64 << 20, name="filter_tables",
    )
    for below, meet in rounds_of(lax.axis_size("ch")):
        got = [swapped(sums, "ch", m << below) for m in range(1, meet)]
        got[0], near_tab_t, late = lax.optimization_barrier((got[0], near_tab_t, late))
        sums = (sums + got[0]) + (got[1] + got[2]) if meet == 4 else sums + got[0]
    dconv, own_grad, grad_msg = call(
        functools.partial(grad_conv, width), [wide(bf16), state_shape, msg_shape],
        sums, conv, qs, up, gain, w, c_tab_t, flops=64 << 20, name="grad_conv",
    )
    out, dqs, rows_q = call(
        functools.partial(query_side, width), [wide(bf16), wide(bf16), vmem((HALO, channels), f32)],
        sums, conv, qs, up, gain, q, halo, after, edges, flops=16 << 20, name="query_side",
    )
    local = call(
        functools.partial(apply_filter, False), [wide(f32)], near_tab_t, on_t, to_end_t, w, sub_pass, factors, dconv,
        flops=256 << 20, name="local_grad",
    )[0]
    near, links, rows_q = scanned(grad_msg, own_grad, passes[passes_each:], (local, rows_q), rows_q)
    q0, q1 = call(
        filter_grads, [vmem((modes, groups), f32)] * 2,
        start_row, start_col, dconv, mixed, state, late, both, c_tab,
        scratch=[pltpu.VMEM((2 * groups // PER_TILE, LANES), f32)], flops=512 << 20, name="filter_grads",
    )
    near, q0 = lax.optimization_barrier((near, q0))
    later, first_rows = call(
        functools.partial(first_grads, len(links)), [state_shape, vmem((6 * HALO, channels), bf16)],
        near, *links, local, e_tab_t, ks, vs, dqs, flops=8 << 20, name="first_grads",
    )
    next_rows = moved(first_rows, "ctx", -1)
    dks, dvs, rows_kv = call(
        grad_keys_values, [wide(bf16), wide(bf16), vmem((2 * HALO, channels), f32)],
        res, rate, later, local, e_tab_t, ks, vs, k, v, halo, q0, q1, x, after, edges,
        scratch=[pltpu.VMEM((modes, channels), f32)], flops=64 << 20, name="grad_keys_values",
    )
    d_q = call(
        functools.partial(grad_inputs, (0,)), [wide(bf16)], taps, after, next_rows, dqs,
        flops=24 << 20, name="grad_queries",
    )[0]
    d_k, d_v = call(
        functools.partial(grad_inputs, (1, 2)), [wide(bf16)] * 2, taps, after, next_rows, dks, dvs,
        flops=24 << 20, name="grad_inputs",
    )
    both = jnp.concatenate([rows_q, rows_kv])
    rounds = rounds_of(count)
    for below, meet in rounds[:-1]:
        both = both.astype(bf16)
        got = [swapped(both, "ctx", m << below) for m in range(1, meet)]
        if not below:
            got[0], d_q = lax.optimization_barrier((got[0], d_q))
        both = met(both, got)
    rows_q, rows_kv = both[:HALO], both[HALO:].astype(bf16)
    below, meet = rounds[-1]
    got = [swapped(rows_kv, "ctx", m << below) for m in range(1, meet)]
    d_taps, d_res, d_rate, d_gain = call(
        unpack,
        [vmem(taps.shape, f32), vmem(res.shape, f32), vmem(rate.shape, f32), vmem((1, channels), f32)],
        rows_q, rows_kv, *got, name="unpack",
    )
    return out, d_q, d_k, d_v, d_taps, d_res.T, d_rate.T, d_gain.reshape(channels)


def solution(mesh):
    wide = P("ctx", "ch")
    third, table, line = P(None, None, "ch"), P("ch", None), P("ch")
    return jax.shard_map(
        on_device,
        mesh=mesh,
        in_specs=(wide, wide, wide, third, table, table, line, P(), wide),
        out_specs=(wide, wide, wide, wide, third, table, table, line),
        check_vma=False,
    )
```

```python
import functools
import math

import jax
import jax.numpy as jnp
from jax import lax
from jax.experimental import pallas as pl
from jax.experimental.pallas import tpu as pltpu
from jax.sharding import PartitionSpec as P

GROUP = 16
TAPS = 7
HALO = 8
LANES = 128
PER_TILE = LANES // GROUP
SUB = 32
ROLLED = 1
BLOCKS = LANES // SUB
PER_LINE = LANES // SUB
epsilon = 1e-06
f32, bf16 = jnp.float32, jnp.bfloat16
highest = lax.Precision.HIGHEST
NN = (((1,), (0,)), ((), ()))
NT = (((1,), (1,)), ((), ()))


def dot(a, b, dims=NN, precision=None):
    return lax.dot_general(a, b, dims, precision=precision, preferred_element_type=f32)


def iota(shape, dim):
    return lax.broadcasted_iota(jnp.int32, shape, dim)


def docs_at(lens, positions):
    start = jnp.int32(0)
    count = jnp.zeros_like(positions)
    for k in range(lens.shape[0]):
        count = count + jnp.where(positions >= start, 1, 0)
        start = start + lens[k]
    return count - 1


def starts_at(lens):
    out = [jnp.int32(0)]
    for k in range(lens.shape[0] - 1):
        out.append(out[-1] + lens[k])
    return out


def doc_start(lens, positions):
    start = jnp.full_like(positions, 0)
    for s in starts_at(lens)[1:]:
        start = jnp.where(positions >= s, s, start)
    return start


def next_start(lens, positions):
    after = jnp.full_like(positions, jnp.iinfo(jnp.int32).max)
    for s in starts_at(lens)[:0:-1]:
        after = jnp.where(positions < s, s, after)
    return after


def one_minus_exp(x):
    series = x * (1 - x / 2 * (1 - x / 3 * (1 - x / 4 * (1 - x / 5 * (1 - x / 6 * (1 - x / 7))))))
    return jnp.where(x < 0.125, series, 1 - jnp.exp(-x))


def own_group(rows=LANES):
    return [iota((rows, LANES), 1) // GROUP == k for k in range(PER_TILE)]


def spread_rows(per_mode, masks):
    return jnp.concatenate([jnp.where(m, per_mode, 0.0) for m in masks], axis=0)


def pick_rows(full, masks):
    modes = full.shape[0] // PER_TILE
    total = jnp.where(masks[0], full[:modes], 0.0)
    for k in range(1, PER_TILE):
        total = jnp.where(masks[k], full[k * modes : (k + 1) * modes], total)
    return total


def column_of(ref, tile):
    modes = ref.shape[0]
    part = [ref[:, tile * PER_TILE + k : tile * PER_TILE + k + 1] for k in range(PER_TILE)]
    return jnp.concatenate([jnp.broadcast_to(p, (modes, LANES)) for p in part], axis=0)


def mode_gain(rate):
    return jnp.sqrt(one_minus_exp(2.0 * rate))


def each_tile(channels, width=LANES):
    return [slice(i, i + width) for i in range(0, channels, width)]


def vmem(shape, dtype):
    return jax.ShapeDtypeStruct(shape, dtype)


def call(body, outs, *args, smem=0, hbm=0, scratch=(), flops=0, name=None, limit=32):
    moved = sum(a.size * a.dtype.itemsize for a in args) + sum(
        math.prod(o.shape) * o.dtype.itemsize for o in outs
    )
    if hbm:
        args = (*args[:-hbm], *[pltpu.with_memory_space_constraint(a, pltpu.HBM) for a in args[-hbm:]])
        outs = [pltpu.VMEM(o.shape, o.dtype) for o in outs]
    return pl.pallas_call(
        body,
        out_shape=tuple(outs),
        in_specs=[pl.BlockSpec(memory_space=pltpu.SMEM)] * smem
        + [pl.BlockSpec(memory_space=pltpu.VMEM)] * (len(args) - smem - hbm)
        + [pl.BlockSpec(memory_space=pltpu.HBM)] * hbm,
        out_specs=tuple([pl.BlockSpec(memory_space=pltpu.VMEM)] * len(outs)),
        scratch_shapes=list(scratch),
        compiler_params=pltpu.CompilerParams(vmem_limit_bytes=limit << 20),
        cost_estimate=pl.CostEstimate(flops=flops, bytes_accessed=moved, transcendentals=0),
        name=name,
    )(*args)


def bring_in(arrays, *refs):
    sources, out, targets, sems = refs[:arrays], refs[arrays], refs[arrays + 1 : -1], refs[-1]
    copies = [pltpu.make_async_copy(a, b, sems.at[i]) for i, (a, b) in enumerate(zip(sources, targets))]
    for copy in copies:
        copy.start()
    for slot, (copy, ref) in enumerate(zip(copies, targets[:3])):
        copy.wait()
        rows = ref.shape[0]
        tail = ref[rows - 2 * HALO :, :].astype(f32)[HALO:]
        out[slot * HALO : (slot + 1) * HALO, :] = tail.astype(bf16)
    for copy in copies[3:]:
        copy.wait()


def shift_rows(table, lens, first, sign):
    shape = table.shape[1:]
    pos = first + iota((LANES, LANES), 0)
    limit = doc_start(lens, pos) if sign < 0 else next_start(lens, pos)
    limit = jnp.concatenate([limit, limit], axis=1)[:, : shape[1]]
    row, col = iota(shape, 0), iota(shape, 1)
    source = first + col - (2 * HALO if sign < 0 else 0)
    apart = col - row - (2 * HALO if sign < 0 else 0)
    apart = jnp.where(source >= limit if sign < 0 else source < limit, apart * sign, 0)
    for lag in range(1, TAPS):
        table[lag - 1] = jnp.where(apart == lag, 1.0, 0.0).astype(bf16)


def rounds_of(count):
    out, below = [], 0
    while count >> below > 1:
        meet = min(4, count >> below)
        out.append((below, meet))
        below += meet.bit_length() - 1
    return out


def pass_count(count):
    rounds = rounds_of(count)
    return sum(meet - 1 for _, meet in rounds) + sum(meet for _, meet in rounds[:-1])


def pass_factors(lens, me, count, forward):
    ends = lambda device: docs_at(lens, device * LANES + LANES - 1)
    out = []
    rounds = rounds_of(count)
    for place, (below, meet) in enumerate(rounds):
        size, mine = 1 << below, me >> below
        wide = size * meet
        start = (me // wide) * wide
        for m in range(1, meet):
            other = mine ^ m
            if forward:
                edge = other * size + size - 1
                lag, meets, valid = me - 1 - edge, ends(edge) == ends(me - 1), other < mine
            else:
                edge = other * size - 1
                lag, meets, valid = edge - me, ends(edge) == ends(me), other > mine
            out.append((lag, jnp.where(meets & valid, 1.0, 0.0)))
        if place + 1 == len(rounds):
            continue
        for m in range(meet):
            other = mine ^ m
            if forward:
                edge, far = other * size + size - 1, start + wide - 1
                lag = far - edge
            else:
                edge, far = other * size - 1, start - 1
                lag = edge - far
            out.append((lag, jnp.where(ends(edge) == ends(far), 1.0, 0.0)))
    return out


def first_tables(count, lens, res, rate, e_tab, before, after, start_row, start_col, edges, in_prev, in_sub, factors, weight, back_keep):
    me = lax.axis_index("ctx")
    first = me * LANES
    shift_rows(before, lens, first, -1)
    lane = iota((LANES, LANES), 1)
    last = first + LANES - 1
    in_last = jnp.where(docs_at(lens, first + lane) == docs_at(lens, last), 1.0, 0.0)
    lag = (LANES - 1 - lane).astype(f32)
    for tile in range(rate.shape[1] // PER_TILE):
        e = jnp.exp(-column_of(rate, tile) * lag) * in_last
        e_tab[tile * LANES : (tile + 1) * LANES, :] = e.astype(bf16)
    shift_rows(after, lens, first, 1)
    row = first + iota((LANES, LANES), 0)
    start = doc_start(lens, row)
    start_row[...] = start
    start_col[...] = doc_start(lens, first + lane)
    for lag in range(1, ROLLED + 1):
        back_keep[lag - 1] = jnp.where(row - lag >= start, 1.0, 0.0)
    weight[...] = res[...] * mode_gain(rate[...])
    row_in, lane_in = iota((LANES, LANES), 0) % SUB, lane % SUB
    same = doc_start(lens, row - row_in + lane_in) == start
    in_sub[0] = jnp.where(same & (lane_in <= row_in), 1.0, 0.0)
    in_sub[1] = jnp.where(same & (lane_in >= row_in), 1.0, 0.0)
    ends, here = doc_start(lens, first + lane - lane_in + (SUB - 1)), doc_start(lens, first + lane)
    in_sub[2] = jnp.where(ends == here, 1.0, 0.0)
    in_sub[3] = jnp.where((here < first + lane - lane_in) & (lane >= SUB), 1.0, 0.0)
    for lag, mask in enumerate(edge_masks(lens, first)):
        if lag:
            edges[lag] = mask
    doc_prev = docs_at(lens, first - 1)
    in_prev[...] = jnp.where(docs_at(lens, first + lane) == doc_prev, 1.0, 0.0)
    pairs = [(jnp.int32(1), jnp.where(docs_at(lens, last) == doc_prev, float(LANES), 0.0))]
    pairs += pass_factors(lens, me, count, True) + pass_factors(lens, me, count, False)
    ends = [docs_at(lens, first + SUB * block + SUB - 1) for block in range(BLOCKS)]
    blocks = [(jnp.int32(0), jnp.where(a == b, 1.0, 0.0)) for a, b in zip(ends[:-1], ends[1:])]
    pairs += blocks
    for place, (steps, mask) in enumerate(pairs):
        scale = -(jnp.maximum(steps, 0) * LANES).astype(f32)
        factors[2 * place : 2 * place + 1, :] = jnp.full((1, LANES), scale, f32)
        factors[2 * place + 1 : 2 * place + 2, :] = jnp.full((1, LANES), mask, f32)


def mode_tables(
    weight, rate, e_tab, in_prev, in_sub, factors, c_tab, c_tab_t, e_tab_t, to_end, to_end_t, on, on_t, w_out, sub_pass, *passes
):
    modes = rate.shape[0]
    lag = (iota((LANES, LANES), 1) + 1).astype(f32)
    masks = own_group(modes)
    mask, mask_end, mask_on = in_prev[...], in_sub[2], in_sub[3]
    lane_in = iota((LANES, LANES), 1) % SUB
    lag_end, lag_on = (SUB - 1 - lane_in).astype(f32), (lane_in + 1).astype(f32)
    for tile in range(rate.shape[1] // PER_TILE):
        at = slice(tile * LANES, (tile + 1) * LANES)
        r_col = column_of(rate, tile)
        c = jnp.exp(-r_col * lag) * mask
        c_tab_t[at, :] = c.astype(bf16)
        c_tab[at, :] = c.T.astype(bf16)
        e_tab_t[at, :] = e_tab[at, :].astype(f32).T.astype(bf16)
        end = jnp.exp(-r_col * lag_end) * mask_end
        to_end[at, :] = end.astype(bf16)
        to_end_t[at, :] = end.T.astype(bf16)
        on_block = jnp.exp(-r_col * lag_on) * mask_on
        on[at, :] = on_block.T.astype(bf16)
        on_t[at, :] = on_block.astype(bf16)
        r_tile = pick_rows(r_col, masks)
        sub_pass[:, at] = jnp.exp(-r_tile * float(SUB))
        w_out[:, at] = pick_rows(column_of(weight, tile), masks)
        for place, out in enumerate(passes):
            scale, keep = factors[2 * place : 2 * place + 1, :], factors[2 * place + 1 : 2 * place + 2, :]
            out[:, at] = jnp.exp(r_tile * scale) * keep


def split(x):
    high = x.astype(bf16)
    return high, (x - high.astype(f32)).astype(bf16)


def block_tables(transposed, weight, rate, in_sub, table, lines):
    modes, groups = rate.shape
    depth = PER_LINE * modes
    row, lane = iota((depth, LANES), 0) // modes, iota((depth, LANES), 1)
    inside = lane % SUB
    if transposed:
        own, lag = lane // SUB == row, inside
    else:
        back = jnp.where(inside > 0, 1, 0)
        own, lag = (lane // SUB + back) % PER_LINE == row, (SUB - inside) % SUB
    own, lag = jnp.where(own, 1.0, 0.0), lag.astype(f32)
    halves = PER_TILE // PER_LINE
    for tile in range(groups // PER_TILE):
        r_all = column_of(rate, tile)
        w_all = column_of(weight, tile)
        for half in range(halves):
            deep = slice(half * depth, (half + 1) * depth)
            place = tile * halves + half
            terms = w_all[deep] * jnp.exp(-r_all[deep] * lag) * own
            lines[place : place + 1, :] = jnp.sum(terms, axis=0, keepdims=True)
    keep = in_sub[1 if transposed else 0]
    for tile in range(groups // PER_TILE):
        for half in range(halves):
            place = tile * halves + half
            line = jnp.broadcast_to(lines[place : place + 1, :], (SUB, LANES))
            rolled = pltpu.roll(line, 0, 1, stride=1, stride_axis=0)
            full = jnp.concatenate([rolled] * BLOCKS, axis=0) * keep
            table[tile * LANES : (tile + 1) * LANES, half * LANES : (half + 1) * LANES] = full.astype(bf16)


def with_before(halo, slot, own, at):
    rows = halo[:, at].astype(f32)[slot * HALO : (slot + 1) * HALO]
    return jnp.concatenate([jnp.concatenate([jnp.zeros_like(rows), rows]).astype(bf16), own[:, at]])


def shifted(table, x):
    return dot(table[...].reshape(-1, table.shape[2])[:, : x.shape[0]], x)


def short_conv(moved_rows, here, taps, index, at):
    total = taps[index, 0:1, at] * here
    for lag in range(1, TAPS):
        total = total + taps[index, lag : lag + 1, at] * moved_rows[(lag - 1) * LANES : lag * LANES]
    return total


def back_conv(before, keep, halo, slot, own, taps, index, at):
    edge = halo[:, at].astype(f32)[slot * HALO : (slot + 1) * HALO]
    ext = jnp.concatenate([jnp.concatenate([jnp.zeros_like(edge), edge]).astype(bf16), own[:, at]])
    far = dot(before[...].reshape(-1, before.shape[2])[ROLLED * LANES :], ext)
    here = own[:, at].astype(f32)
    total = taps[index, 0:1, at] * here
    row = iota(edge.shape, 0)
    copies = here.shape[1] // LANES
    for lag in range(1, TAPS):
        if lag <= ROLLED:
            part = pltpu.roll(here, lag, 0)
            head = jnp.where(row < lag, pltpu.roll(edge, lag, 0), part[:HALO])
            part = jnp.concatenate([head, part[HALO:]]) * jnp.concatenate([keep[lag - 1]] * copies, axis=1)
        else:
            part = far[(lag - 1 - ROLLED) * LANES : (lag - ROLLED) * LANES]
        total = total + taps[index, lag : lag + 1, at] * part
    return total


def keys_values(k, v, halo, taps, before, keep, e_tab, mixed, ks_out, vs_out, s_out, s_msg):
    modes = s_out.shape[0]
    own = own_group(modes)
    for at in each_tile(k.shape[1], 2 * LANES):
        ks = back_conv(before, keep, halo, 0, k, taps, 1, at)
        vs = back_conv(before, keep, halo, 1, v, taps, 2, at)
        ks_out[:, at] = ks
        vs_out[:, at] = vs
        mixed[:, at] = (ks * vs).astype(bf16)
    for at in each_tile(k.shape[1]):
        state = pick_rows(dot(e_tab[at, :], mixed[:, at]), own)
        s_out[:, at] = state
        s_msg[:, at] = state.astype(bf16)


def queries_short(q, halo, taps, before, qs_out):
    for at in each_tile(q.shape[1], 2 * LANES):
        qs_out[:, at] = short_conv(shifted(before, with_before(halo, 2, q, at)), q[:, at].astype(f32), taps, 0, at)


def lane_masks_bf16():
    return [jnp.where(m, 1.0, 0.0).astype(bf16) for m in own_group()]


def across_blocks(x, gather, spread, w, carry, own, masks, forward):
    block_of = iota((1, LANES), 1) // SUB
    inner = range(BLOCKS - 1) if forward else range(1, BLOCKS)
    picks = [gather * jnp.where(block_of == b, 1.0, 0.0).astype(bf16) for b in inner]
    full = dot(jnp.concatenate(picks, axis=0), x)
    parts = [pick_rows(full[i * LANES : (i + 1) * LANES], own) for i in range(BLOCKS - 1)]
    zero = jnp.zeros((SUB, LANES), f32)
    out = [zero] * BLOCKS
    total = None
    for i in range(BLOCKS - 1) if forward else range(BLOCKS - 2, -1, -1):
        total = parts[i] if total is None else parts[i] + total * (carry * masks[i - forward])
        to = i + 1 if forward else i
        high, low = split(spread_rows(total * w, own))
        lhs = spread[to * SUB : (to + 1) * SUB]
        out[to] = dot(jnp.concatenate([lhs, lhs], axis=1), jnp.concatenate([high, low], axis=0))
    return jnp.concatenate(out, axis=0)


def apply_filter(forward, table, gather, spread, w, sub_pass, factors, x, out):
    modes = w.shape[0]
    own_b = [m[:SUB] for m in lane_masks_bf16()]
    own = own_group(modes)
    first = factors.shape[0] - 2 * (BLOCKS - 1)
    masks = [factors[first + 2 * b + 1 : first + 2 * b + 2, :] for b in range(BLOCKS - 1)]
    for at in each_tile(x.shape[1]):
        part = x[:, at]
        near = []
        for block in range(BLOCKS):
            rows = slice(block * SUB, (block + 1) * SUB)
            stacked = jnp.concatenate([part[rows] * m for m in own_b], axis=0)
            near.append(dot(table[at.start + block * SUB : at.start + (block + 1) * SUB, :], stacked))
        carry = sub_pass[:, at]
        far = across_blocks(part, gather[at, :], spread[at, :], w[:, at], carry, own, masks, forward)
        out[:, at] = jnp.concatenate(near, axis=0) + far


def joined(near, parts, at):
    total = near[:, at]
    for factor, message in zip(parts[0::2], parts[1::2]):
        total = total + factor[:, at] * message[:, at].astype(f32)
    return total


def gate(parts, within, near, *refs):
    links, (w, c_tab, qs, up, gain, conv_out, state_out, sums) = refs[:parts], refs[parts:]
    modes = near.shape[0]
    own = own_group(modes)
    squares = dots = jnp.zeros((LANES, LANES), f32)
    for at in each_tile(qs.shape[1]):
        state = joined(near, links, at)
        state_out[:, at] = state
        carried = spread_rows(state * w[:, at], own).astype(bf16)
        conv = within[:, at] + dot(c_tab[at, :], carried)
        conv_out[:, at] = conv
        gated = qs[:, at] * conv
        scaled = up[:, at].astype(f32) * gain[:, at]
        squares = squares + gated * gated
        dots = dots + scaled * gated
    line = lambda total: jnp.sum(total.T, axis=0, keepdims=True)
    sums[...] = jnp.where(iota((HALO, LANES), 0) < 4, line(squares), line(dots))


def norm_columns(sums, width):
    both = sums[...]
    inverse = lax.rsqrt(both[0:1] / width + epsilon)
    slope = inverse * inverse * inverse * both[4:5] / width
    wide = lambda line: jnp.broadcast_to(line, (LANES, LANES)).T
    return wide(inverse), wide(slope)


def grad_conv(width, sums, conv, qs, up, gain, w, c_tab_t, dconv, g_out, g_msg):
    modes = g_out.shape[0]
    own = own_group(modes)
    inverse, slope = norm_columns(sums, width)
    for at in each_tile(qs.shape[1]):
        q = qs[:, at]
        scaled = up[:, at].astype(f32) * gain[:, at]
        d_gated = inverse * scaled - (q * conv[:, at]) * slope
        d = (d_gated * q).astype(bf16)
        dconv[:, at] = d
        u = pick_rows(dot(c_tab_t[at, :], d), own)
        g = u * w[:, at]
        g_out[:, at] = g
        g_msg[:, at] = g.astype(bf16)


def edge_masks(lens, first):
    row = iota((HALO, LANES), 0)
    start = doc_start(lens, first + row)
    out = [None]
    for lag in range(1, TAPS):
        out.append(jnp.where((first + row - lag >= start) & (row < lag), 1.0, 0.0))
    return out


def tap_rows(rows_out, slot, d, x, edge, after, masks, at):
    back = shifted(after, d)
    head = d[:HALO].astype(f32) if d.dtype == f32 else d.astype(f32)[:HALO]
    rows_out[slot : slot + 1, at] = jnp.sum(d.astype(f32) * x, axis=0, keepdims=True)
    for lag in range(1, TAPS):
        prod = back[(lag - 1) * LANES : lag * LANES] * x
        total = prod[:HALO]
        for i in range(HALO, LANES, HALO):
            total = total + prod[i : i + HALO]
        mask = jnp.concatenate([masks[lag]] * (total.shape[1] // LANES), axis=1)
        total = total + head * (pltpu.roll(edge, lag, 0) * mask)
        rows_out[slot + lag : slot + lag + 1, at] = jnp.sum(total, axis=0, keepdims=True)


def query_side(width, sums, conv, qs, up, gain, q, halo, after, edges, out, dqs_out, rows_out):
    masks = edges
    inverse, slope = norm_columns(sums, width)
    for pair in each_tile(q.shape[1], 2 * LANES):
        for at in (slice(pair.start, pair.start + LANES), slice(pair.start + LANES, pair.stop)):
            c = conv[:, at]
            gated = qs[:, at] * c
            upstream = up[:, at].astype(f32)
            d_gated = inverse * (upstream * gain[:, at]) - gated * slope
            normed = gated * inverse
            out[:, at] = (normed * gain[:, at]).astype(bf16)
            dqs_out[:, at] = (d_gated * c).astype(bf16)
            rows_out[TAPS : TAPS + 1, at] = jnp.sum(upstream * normed, axis=0, keepdims=True)
        edge = halo[:, pair].astype(f32)[2 * HALO : 3 * HALO]
        d = dqs_out[:, pair]
        tap_rows(rows_out, 0, d, q[:, pair].astype(f32), edge, after, masks, pair)


def group_sums(parts):
    channels = parts.shape[1]
    high, low = split(parts)
    shape = (channels, channels // GROUP)
    belongs = jnp.where(iota(shape, 0) // GROUP == iota(shape, 1), 1.0, 0.0).astype(bf16)
    return dot(high, belongs) + dot(low, belongs)


def filter_tables(rate, mixed, state, own_pass, e_tab, late_out, both_out, x_out):
    modes, groups = rate.shape
    lane = iota((LANES, LANES), 1)
    centred = (lane - LANES // 2).astype(f32)
    lag_e = (LANES - 1 - lane).astype(f32)
    own = own_group(modes)
    for tile, at in enumerate(each_tile(mixed.shape[1])):
        r = column_of(rate, tile)
        early = jnp.exp(r * centred)
        late_out[at, :] = jnp.exp(-r * centred).T
        both_out[at, :] = jnp.concatenate([early.T, (early * centred).T], axis=1).astype(bf16)
        x = pick_rows(dot((e_tab[at, :].astype(f32) * lag_e).astype(bf16), mixed[:, at]), own)
        x_out[:, at] = x + own_pass[:, at] * state[:, at]


def filter_grads(start_row, start_col, dconv, mixed, state, late, both, c_tab, q0_out, q1_out, lines):
    modes, groups = q0_out.shape
    row, lane = iota((LANES, LANES), 0), iota((LANES, LANES), 1)
    keep = jnp.where((start_row[...] == start_col[...]) & (lane <= row), 1.0, 0.0)
    centred_row = (row - LANES // 2).astype(f32)
    later = (row + 1).astype(f32)
    own_b = lane_masks_bf16()
    wide = [jnp.concatenate([o, o], axis=1) for o in own_b]
    own = own_group(modes)
    for tile, at in enumerate(each_tile(dconv.shape[1])):
        d, m = dconv[:, at], mixed[:, at]
        stacked = jnp.concatenate([m * o for o in own_b], axis=0)
        outer = dot(d, stacked, NT)
        blocks = [outer[:, k * LANES : (k + 1) * LANES] * keep for k in range(PER_TILE)]
        outer = jnp.concatenate([b.astype(bf16) for b in blocks], axis=1)
        pair = both[at, :]
        met = dot(outer, jnp.concatenate([pair * o for o in wide], axis=0))
        near, near_lag = met[:, :LANES] * late[at, :], met[:, LANES:] * late[at, :]
        far = dot(d, spread_rows(state[:, at], own).astype(bf16), NT) * c_tab[at, :].astype(f32)
        q0 = jnp.sum(near + far, axis=0, keepdims=True)
        q1 = jnp.sum(near * centred_row - near_lag + far * later, axis=0, keepdims=True)
        lines[tile : tile + 1, :] = q0
        lines[groups // PER_TILE + tile : groups // PER_TILE + tile + 1, :] = q1
    pick = jnp.where(iota((modes, LANES), 1) % modes == iota((modes, LANES), 0), 1.0, 0.0).astype(bf16)
    mine = iota((PER_TILE, LANES), 1) // modes == iota((PER_TILE, LANES), 0)
    for begin, out in ((0, q0_out), (groups // PER_TILE, q1_out)):
        parts = [
            jnp.where(mine, jnp.broadcast_to(lines[begin + i : begin + i + 1, :], mine.shape), 0.0)
            for i in range(groups // PER_TILE)
        ]
        high, low = split(jnp.concatenate(parts, axis=0))
        out[...] = dot(pick, high, NT) + dot(pick, low, NT)


def first_grads(parts, near, *refs):
    links, (local, e_tab_t, ks, vs, dqs, later, rows_out) = refs[:parts], refs[parts:]
    own = own_group(near.shape[0])
    rows = 2 * HALO
    for tile, at in enumerate(each_tile(ks.shape[1])):
        g = joined(near, links, at)
        later[:, at] = g
        head = slice(tile * LANES, tile * LANES + rows)
        d_mixed = local[:rows, at] + dot(e_tab_t[head, :], spread_rows(g, own).astype(bf16))
        parts = (dqs[:rows, at].astype(f32), d_mixed * vs[:rows, at], d_mixed * ks[:rows, at])
        rows_out[:, at] = jnp.concatenate([part[:HALO] for part in parts]).astype(bf16)


def grad_keys_values(
    res, rate, later, local, e_tab_t, ks, vs, k, v, halo, q0, q1, x, after, masks, dks_out, dvs_out, rows_out, flows
):
    modes = later.shape[0]
    own = own_group(modes)
    for at in each_tile(k.shape[1]):
        g = later[:, at]
        flows[:, at] = g * x[:, at]
        d_mixed = local[:, at] + dot(e_tab_t[at, :], spread_rows(g, own).astype(bf16))
        dks_out[:, at] = (d_mixed * vs[:, at]).astype(bf16)
        dvs_out[:, at] = (d_mixed * ks[:, at]).astype(bf16)
    for pair in each_tile(k.shape[1], 2 * LANES):
        edges = halo[:, pair].astype(f32)
        for slot, x_in, d_out in ((0, k, dks_out), (1, v, dvs_out)):
            edge = edges[slot * HALO : (slot + 1) * HALO]
            tap_rows(rows_out, slot * TAPS, d_out[:, pair], x_in[:, pair].astype(f32), edge, after, masks, pair)
    r = rate[...]
    gain = mode_gain(r)
    slope = jnp.exp(-2.0 * r) / gain
    q0_all = q0[...]
    d_res = gain * q0_all
    d_rate = res[...] * (slope * q0_all - gain * q1[...]) - group_sums(flows[...])
    groups = r.shape[1]
    for n in range(modes):
        at = slice(n * groups, (n + 1) * groups)
        rows_out[2 * TAPS : 2 * TAPS + 1, at] = d_res[n : n + 1]
        rows_out[2 * TAPS + 1 : 2 * TAPS + 2, at] = d_rate[n : n + 1]


def grad_inputs(filters, taps, after, edges, *refs):
    owns, outs = refs[: len(filters)], refs[len(filters) :]
    for index, own, out in zip(filters, owns, outs):
        for at in each_tile(own.shape[1], 2 * LANES):
            d = own[:, at]
            edge = edges[:, at].astype(f32)[index * HALO : (index + 1) * HALO]
            edge = jnp.concatenate([edge, jnp.zeros_like(edge)]).astype(bf16)
            moved_rows = shifted(after, jnp.concatenate([d, edge]))
            out[:, at] = short_conv(moved_rows, d.astype(f32), taps, index, at).astype(bf16)


def unpack(rows, *refs):
    others, (taps_out, res_out, rate_out, gain_out) = refs[:-4], refs[-4:]
    modes, groups = res_out.shape
    everything = rows[...].astype(f32) + others[0][...].astype(f32)
    if len(others) > 1:
        everything = everything + (others[1][...].astype(f32) + others[2][...].astype(f32))
    total_q, total = everything[:HALO], everything[HALO:]
    taps_out[0] = total_q[0:TAPS]
    taps_out[1] = total[0:TAPS]
    taps_out[2] = total[TAPS : 2 * TAPS]
    gain_out[...] = total_q[TAPS : TAPS + 1]
    for slot, out in ((2 * TAPS, res_out), (2 * TAPS + 1, rate_out)):
        for n in range(modes):
            out[n : n + 1, :] = total[slot : slot + 1, n * groups : (n + 1) * groups]


def moved(value, axis, steps):
    count = lax.axis_size(axis)
    first, last = max(0, -steps), min(count, count - steps)
    return lax.ppermute(value, axis, [(i, i + steps) for i in range(first, last)])


def swapped(value, axis, bits):
    return lax.ppermute(value, axis, [(i, i ^ bits) for i in range(lax.axis_size(axis))])


def after_all(value, *others):
    return lax.optimization_barrier((value, *others))[0]


def scanned(message, own, passes, beside=()):
    rounds = rounds_of(lax.axis_size("ctx"))
    near, at = None, 0
    for place, (below, meet) in enumerate(rounds):
        got = [swapped(message, "ctx", m << below) for m in range(1, meet)]
        factors, at = passes[at : at + meet - 1], at + meet - 1
        if place + 1 == len(rounds):
            links = [part for pair in zip(factors, got) for part in pair]
            return (jnp.zeros_like(own) if near is None else near), links
        for factor, other in zip(factors, got):
            part = factor * other.astype(f32)
            near = part if near is None else near + part
        own = passes[at] * own
        for factor, other in zip(passes[at + 1 : at + meet], got):
            own = own + factor * other.astype(f32)
        at += meet
        message = after_all(own.astype(bf16), *beside) if beside and not place else own.astype(bf16)


def on_device(q, k, v, taps, res, rate, gain, lens, up):
    rows, channels = q.shape
    groups, modes = rate.shape
    count = lax.axis_size("ctx")
    width = channels * lax.axis_size("ch")
    res, rate = res.T, rate.T
    gain = gain.reshape(1, channels)
    wide = lambda dtype: vmem((rows, channels), dtype)
    state_shape = vmem((modes, channels), f32)
    msg_shape = vmem((modes, channels), bf16)
    table = vmem((channels, LANES), bf16)
    shifts = (TAPS - 1, LANES, LANES + 2 * HALO)

    brought = [k, v, q, up, taps, res, rate, gain]
    last, k, v, q, up, taps, res, rate, gain = call(
        functools.partial(bring_in, len(brought)),
        [vmem((3 * HALO, channels), bf16)] + [vmem(a.shape, a.dtype) for a in brought],
        *brought, hbm=len(brought), name="bring_in",
        scratch=[pltpu.SemaphoreType.DMA((len(brought),))],
    )
    halo = moved(last, "ctx", 1)
    passes_each = pass_count(count)
    square = lambda dtype: vmem((LANES, LANES), dtype)
    e_tab, before, after, start_row, start_col, edges, in_prev, in_sub, factors, weight, back_keep = call(
        functools.partial(first_tables, count),
        [table, vmem(shifts, bf16), vmem(shifts, bf16), square(jnp.int32), square(jnp.int32)]
        + [vmem((TAPS, HALO, LANES), f32), square(f32), vmem((4, LANES, LANES), f32)]
        + [vmem((2 * (1 + 2 * passes_each + BLOCKS - 1), LANES), f32), vmem(res.shape, f32)]
        + [vmem((ROLLED, LANES, LANES), f32)],
        lens, res, rate, smem=1, flops=4 << 20, name="first_tables",
    )
    blocked = [vmem((channels, PER_TILE * SUB), bf16)]
    lines = [pltpu.VMEM((groups // PER_LINE, LANES), f32)]
    near_tab = call(
        functools.partial(block_tables, False), blocked, weight, rate, in_sub, scratch=lines, flops=4 << 20, name="block_tables",
    )[0]
    halo, near_tab = lax.optimization_barrier((halo, near_tab))
    mixed, ks, vs, own_state, state_msg = call(
        keys_values, [wide(bf16), wide(f32), wide(f32), state_shape, msg_shape],
        k, v, halo, taps, before, back_keep, e_tab, flops=64 << 20, name="keys_values",
    )
    c_tab, c_tab_t, e_tab_t, to_end, to_end_t, on, on_t, w, sub_pass, own_pass, *passes = call(
        mode_tables, [table] * 7 + [state_shape] * (3 + 2 * passes_each),
        weight, rate, e_tab, in_prev, in_sub, factors, flops=4 << 20, name="mode_tables",
    )
    qs = call(queries_short, [wide(f32)], q, halo, taps, before, flops=8 << 20, name="queries_short")[0]
    near, links = scanned(state_msg, own_state, passes[:passes_each], (qs,))
    within = call(
        functools.partial(apply_filter, True), [wide(f32)], near_tab, to_end, on, w, sub_pass, factors, mixed,
        flops=256 << 20, name="within",
    )[0]
    conv, state, sums = call(
        functools.partial(gate, len(links)), [wide(f32), state_shape, vmem((HALO, LANES), f32)],
        within, near, *links, w, c_tab, qs, up, gain, flops=64 << 20, name="gate",
    )
    rate_here = after_all(rate, sums)
    near_tab_t = call(
        functools.partial(block_tables, True), blocked, weight, rate_here, in_sub, scratch=lines, flops=4 << 20, name="block_tables_t",
    )[0]
    late, both, x = call(
        filter_tables, [vmem((channels, LANES), f32), vmem((channels, 2 * LANES), bf16), state_shape],
        rate_here, mixed, state, own_pass, e_tab, flops=64 << 20, name="filter_tables",
    )
    for below, meet in rounds_of(lax.axis_size("ch")):
        got = [swapped(sums, "ch", m << below) for m in range(1, meet)]
        got[0], near_tab_t, late = lax.optimization_barrier((got[0], near_tab_t, late))
        sums = (sums + got[0]) + (got[1] + got[2]) if meet == 4 else sums + got[0]
    dconv, own_grad, grad_msg = call(
        functools.partial(grad_conv, width), [wide(bf16), state_shape, msg_shape],
        sums, conv, qs, up, gain, w, c_tab_t, flops=64 << 20, name="grad_conv",
    )
    out, dqs, rows_q = call(
        functools.partial(query_side, width), [wide(bf16), wide(bf16), vmem((HALO, channels), f32)],
        sums, conv, qs, up, gain, q, halo, after, edges, flops=16 << 20, name="query_side",
    )
    local = call(
        functools.partial(apply_filter, False), [wide(f32)], near_tab_t, on_t, to_end_t, w, sub_pass, factors, dconv,
        flops=256 << 20, name="local_grad",
    )[0]
    near, links = scanned(grad_msg, own_grad, passes[passes_each:], (local, rows_q))
    q0, q1 = call(
        filter_grads, [vmem((modes, groups), f32)] * 2,
        start_row, start_col, dconv, mixed, state, late, both, c_tab,
        scratch=[pltpu.VMEM((2 * groups // PER_TILE, LANES), f32)], flops=512 << 20, name="filter_grads",
    )
    near, q0 = lax.optimization_barrier((near, q0))
    later, first_rows = call(
        functools.partial(first_grads, len(links)), [state_shape, vmem((3 * HALO, channels), bf16)],
        near, *links, local, e_tab_t, ks, vs, dqs, flops=8 << 20, name="first_grads",
    )
    next_rows = moved(first_rows, "ctx", -1)
    dks, dvs, rows_kv = call(
        grad_keys_values, [wide(bf16), wide(bf16), vmem((2 * HALO, channels), f32)],
        res, rate, later, local, e_tab_t, ks, vs, k, v, halo, q0, q1, x, after, edges,
        scratch=[pltpu.VMEM((modes, channels), f32)], flops=64 << 20, name="grad_keys_values",
    )
    both = jnp.concatenate([rows_q, rows_kv]).astype(bf16)
    d_q = call(
        functools.partial(grad_inputs, (0,)), [wide(bf16)], taps, after, next_rows, dqs,
        flops=24 << 20, name="grad_queries",
    )[0]
    d_k, d_v = call(
        functools.partial(grad_inputs, (1, 2)), [wide(bf16)] * 2, taps, after, next_rows, dks, dvs,
        flops=24 << 20, name="grad_inputs",
    )
    rounds = rounds_of(count)
    for place, (below, meet) in enumerate(rounds):
        got = [swapped(both, "ctx", m << below) for m in range(1, meet)]
        if place + 1 < len(rounds):
            if place == 0:
                got[0], d_q = lax.optimization_barrier((got[0], d_q))
            both, got = both.astype(f32), [part.astype(f32) for part in got]
            both = ((both + got[0]) + (got[1] + got[2]) if meet == 4 else both + got[0]).astype(bf16)
    d_taps, d_res, d_rate, d_gain = call(
        unpack,
        [vmem(taps.shape, f32), vmem(res.shape, f32), vmem(rate.shape, f32), vmem((1, channels), f32)],
        both, *got, name="unpack",
    )
    return out, d_q, d_k, d_v, d_taps, d_res.T, d_rate.T, d_gain.reshape(channels)


def solution(mesh):
    wide = P("ctx", "ch")
    third, table, line = P(None, None, "ch"), P("ch", None), P("ch")
    return jax.shard_map(
        on_device,
        mesh=mesh,
        in_specs=(wide, wide, wide, third, table, table, line, P(), wide),
        out_specs=(wide, wide, wide, wide, third, table, table, line),
        check_vma=False,
    )
```

```python
import functools
import math

import jax
import jax.numpy as jnp
from jax import lax
from jax.experimental import pallas as pl
from jax.experimental.pallas import tpu as pltpu
from jax.sharding import PartitionSpec as P

GROUP = 16
TAPS = 7
HALO = 8
LANES = 128
PER_TILE = LANES // GROUP
SUB = 32
ROLLED = 1
BLOCKS = LANES // SUB
PER_LINE = LANES // SUB
epsilon = 1e-06
f32, bf16 = jnp.float32, jnp.bfloat16
highest = lax.Precision.HIGHEST
NN = (((1,), (0,)), ((), ()))
NT = (((1,), (1,)), ((), ()))


def dot(a, b, dims=NN, precision=None):
    return lax.dot_general(a, b, dims, precision=precision, preferred_element_type=f32)


def iota(shape, dim):
    return lax.broadcasted_iota(jnp.int32, shape, dim)


def docs_at(lens, positions):
    start = jnp.int32(0)
    count = jnp.zeros_like(positions)
    for k in range(lens.shape[0]):
        count = count + jnp.where(positions >= start, 1, 0)
        start = start + lens[k]
    return count - 1


def starts_at(lens):
    out = [jnp.int32(0)]
    for k in range(lens.shape[0] - 1):
        out.append(out[-1] + lens[k])
    return out


def doc_start(lens, positions):
    start = jnp.full_like(positions, 0)
    for s in starts_at(lens)[1:]:
        start = jnp.where(positions >= s, s, start)
    return start


def next_start(lens, positions):
    after = jnp.full_like(positions, jnp.iinfo(jnp.int32).max)
    for s in starts_at(lens)[:0:-1]:
        after = jnp.where(positions < s, s, after)
    return after


def one_minus_exp(x):
    series = x * (1 - x / 2 * (1 - x / 3 * (1 - x / 4 * (1 - x / 5 * (1 - x / 6 * (1 - x / 7))))))
    return jnp.where(x < 0.125, series, 1 - jnp.exp(-x))


def own_group(rows=LANES):
    return [iota((rows, LANES), 1) // GROUP == k for k in range(PER_TILE)]


def spread_rows(per_mode, masks):
    return jnp.concatenate([jnp.where(m, per_mode, 0.0) for m in masks], axis=0)


def pick_rows(full, masks):
    modes = full.shape[0] // PER_TILE
    total = jnp.where(masks[0], full[:modes], 0.0)
    for k in range(1, PER_TILE):
        total = jnp.where(masks[k], full[k * modes : (k + 1) * modes], total)
    return total


def column_of(ref, tile):
    modes = ref.shape[0]
    part = [ref[:, tile * PER_TILE + k : tile * PER_TILE + k + 1] for k in range(PER_TILE)]
    return jnp.concatenate([jnp.broadcast_to(p, (modes, LANES)) for p in part], axis=0)


def mode_gain(rate):
    return jnp.sqrt(one_minus_exp(2.0 * rate))


def each_tile(channels, width=LANES):
    return [slice(i, i + width) for i in range(0, channels, width)]


def vmem(shape, dtype):
    return jax.ShapeDtypeStruct(shape, dtype)


def call(body, outs, *args, smem=0, hbm=0, scratch=(), flops=0, name=None, limit=32):
    moved = sum(a.size * a.dtype.itemsize for a in args) + sum(
        math.prod(o.shape) * o.dtype.itemsize for o in outs
    )
    if hbm:
        args = (*args[:-hbm], *[pltpu.with_memory_space_constraint(a, pltpu.HBM) for a in args[-hbm:]])
        outs = [pltpu.VMEM(o.shape, o.dtype) for o in outs]
    return pl.pallas_call(
        body,
        out_shape=tuple(outs),
        in_specs=[pl.BlockSpec(memory_space=pltpu.SMEM)] * smem
        + [pl.BlockSpec(memory_space=pltpu.VMEM)] * (len(args) - smem - hbm)
        + [pl.BlockSpec(memory_space=pltpu.HBM)] * hbm,
        out_specs=tuple([pl.BlockSpec(memory_space=pltpu.VMEM)] * len(outs)),
        scratch_shapes=list(scratch),
        compiler_params=pltpu.CompilerParams(vmem_limit_bytes=limit << 20),
        cost_estimate=pl.CostEstimate(flops=flops, bytes_accessed=moved, transcendentals=0),
        name=name,
    )(*args)


def bring_in(arrays, *refs):
    sources, out, targets, sems = refs[:arrays], refs[arrays], refs[arrays + 1 : -1], refs[-1]
    copies = [pltpu.make_async_copy(a, b, sems.at[i]) for i, (a, b) in enumerate(zip(sources, targets))]
    for copy in copies:
        copy.start()
    for slot, (copy, ref) in enumerate(zip(copies, targets[:3])):
        copy.wait()
        rows = ref.shape[0]
        tail = ref[rows - 2 * HALO :, :].astype(f32)[HALO:]
        out[slot * HALO : (slot + 1) * HALO, :] = tail.astype(bf16)
    for copy in copies[3:]:
        copy.wait()


def shift_rows(table, lens, first, sign):
    shape = table.shape[1:]
    pos = first + iota((LANES, LANES), 0)
    limit = doc_start(lens, pos) if sign < 0 else next_start(lens, pos)
    limit = jnp.concatenate([limit, limit], axis=1)[:, : shape[1]]
    row, col = iota(shape, 0), iota(shape, 1)
    source = first + col - (2 * HALO if sign < 0 else 0)
    apart = col - row - (2 * HALO if sign < 0 else 0)
    apart = jnp.where(source >= limit if sign < 0 else source < limit, apart * sign, 0)
    for lag in range(1, TAPS):
        table[lag - 1] = jnp.where(apart == lag, 1.0, 0.0).astype(bf16)


def rounds_of(count):
    out, below = [], 0
    while count >> below > 1:
        meet = min(4, count >> below)
        out.append((below, meet))
        below += meet.bit_length() - 1
    return out


def pass_count(count):
    rounds = rounds_of(count)
    return sum(meet - 1 for _, meet in rounds) + sum(meet for _, meet in rounds[:-1])


def pass_factors(lens, me, count, forward):
    ends = lambda device: docs_at(lens, device * LANES + LANES - 1)
    out = []
    rounds = rounds_of(count)
    for place, (below, meet) in enumerate(rounds):
        size, mine = 1 << below, me >> below
        wide = size * meet
        start = (me // wide) * wide
        for m in range(1, meet):
            other = mine ^ m
            if forward:
                edge = other * size + size - 1
                lag, meets, valid = me - 1 - edge, ends(edge) == ends(me - 1), other < mine
            else:
                edge = other * size - 1
                lag, meets, valid = edge - me, ends(edge) == ends(me), other > mine
            out.append((lag, jnp.where(meets & valid, 1.0, 0.0)))
        if place + 1 == len(rounds):
            continue
        for m in range(meet):
            other = mine ^ m
            if forward:
                edge, far = other * size + size - 1, start + wide - 1
                lag = far - edge
            else:
                edge, far = other * size - 1, start - 1
                lag = edge - far
            out.append((lag, jnp.where(ends(edge) == ends(far), 1.0, 0.0)))
    return out


def first_tables(count, lens, res, rate, e_tab, before, after, start_row, start_col, edges, in_prev, in_sub, factors, weight, back_keep):
    me = lax.axis_index("ctx")
    first = me * LANES
    shift_rows(before, lens, first, -1)
    lane = iota((LANES, LANES), 1)
    last = first + LANES - 1
    in_last = jnp.where(docs_at(lens, first + lane) == docs_at(lens, last), 1.0, 0.0)
    lag = (LANES - 1 - lane).astype(f32)
    for tile in range(rate.shape[1] // PER_TILE):
        e = jnp.exp(-column_of(rate, tile) * lag) * in_last
        e_tab[tile * LANES : (tile + 1) * LANES, :] = e.astype(bf16)
    shift_rows(after, lens, first, 1)
    row = first + iota((LANES, LANES), 0)
    start = doc_start(lens, row)
    start_row[...] = start
    start_col[...] = doc_start(lens, first + lane)
    for lag in range(1, ROLLED + 1):
        back_keep[lag - 1] = jnp.where(row - lag >= start, 1.0, 0.0)
    weight[...] = res[...] * mode_gain(rate[...])
    row_in, lane_in = iota((LANES, LANES), 0) % SUB, lane % SUB
    same = doc_start(lens, row - row_in + lane_in) == start
    in_sub[0] = jnp.where(same & (lane_in <= row_in), 1.0, 0.0)
    in_sub[1] = jnp.where(same & (lane_in >= row_in), 1.0, 0.0)
    ends, here = doc_start(lens, first + lane - lane_in + (SUB - 1)), doc_start(lens, first + lane)
    in_sub[2] = jnp.where(ends == here, 1.0, 0.0)
    in_sub[3] = jnp.where((here < first + lane - lane_in) & (lane >= SUB), 1.0, 0.0)
    for lag, mask in enumerate(edge_masks(lens, first)):
        if lag:
            edges[lag] = mask
    doc_prev = docs_at(lens, first - 1)
    in_prev[...] = jnp.where(docs_at(lens, first + lane) == doc_prev, 1.0, 0.0)
    pairs = [(jnp.int32(1), jnp.where(docs_at(lens, last) == doc_prev, float(LANES), 0.0))]
    pairs += pass_factors(lens, me, count, True) + pass_factors(lens, me, count, False)
    ends = [docs_at(lens, first + SUB * block + SUB - 1) for block in range(BLOCKS)]
    blocks = [(jnp.int32(0), jnp.where(a == b, 1.0, 0.0)) for a, b in zip(ends[:-1], ends[1:])]
    pairs += blocks
    for place, (steps, mask) in enumerate(pairs):
        scale = -(jnp.maximum(steps, 0) * LANES).astype(f32)
        factors[2 * place : 2 * place + 1, :] = jnp.full((1, LANES), scale, f32)
        factors[2 * place + 1 : 2 * place + 2, :] = jnp.full((1, LANES), mask, f32)


def mode_tables(
    weight, rate, e_tab, in_prev, in_sub, factors, c_tab, c_tab_t, e_tab_t, to_end, to_end_t, on, on_t, w_out, sub_pass, *passes
):
    modes = rate.shape[0]
    lag = (iota((LANES, LANES), 1) + 1).astype(f32)
    masks = own_group(modes)
    mask, mask_end, mask_on = in_prev[...], in_sub[2], in_sub[3]
    lane_in = iota((LANES, LANES), 1) % SUB
    lag_end, lag_on = (SUB - 1 - lane_in).astype(f32), (lane_in + 1).astype(f32)
    for tile in range(rate.shape[1] // PER_TILE):
        at = slice(tile * LANES, (tile + 1) * LANES)
        r_col = column_of(rate, tile)
        c = jnp.exp(-r_col * lag) * mask
        c_tab_t[at, :] = c.astype(bf16)
        c_tab[at, :] = c.T.astype(bf16)
        e_tab_t[at, :] = e_tab[at, :].astype(f32).T.astype(bf16)
        end = jnp.exp(-r_col * lag_end) * mask_end
        to_end[at, :] = end.astype(bf16)
        to_end_t[at, :] = end.T.astype(bf16)
        on_block = jnp.exp(-r_col * lag_on) * mask_on
        on[at, :] = on_block.T.astype(bf16)
        on_t[at, :] = on_block.astype(bf16)
        r_tile = pick_rows(r_col, masks)
        sub_pass[:, at] = jnp.exp(-r_tile * float(SUB))
        w_out[:, at] = pick_rows(column_of(weight, tile), masks)
        for place, out in enumerate(passes):
            scale, keep = factors[2 * place : 2 * place + 1, :], factors[2 * place + 1 : 2 * place + 2, :]
            out[:, at] = jnp.exp(r_tile * scale) * keep


def split(x):
    high = x.astype(bf16)
    return high, (x - high.astype(f32)).astype(bf16)


def block_tables(transposed, weight, rate, in_sub, table, lines):
    modes, groups = rate.shape
    depth = PER_LINE * modes
    row, lane = iota((depth, LANES), 0) // modes, iota((depth, LANES), 1)
    inside = lane % SUB
    if transposed:
        own, lag = lane // SUB == row, inside
    else:
        back = jnp.where(inside > 0, 1, 0)
        own, lag = (lane // SUB + back) % PER_LINE == row, (SUB - inside) % SUB
    own, lag = jnp.where(own, 1.0, 0.0), lag.astype(f32)
    halves = PER_TILE // PER_LINE
    for tile in range(groups // PER_TILE):
        r_all = column_of(rate, tile)
        w_all = column_of(weight, tile)
        for half in range(halves):
            deep = slice(half * depth, (half + 1) * depth)
            place = tile * halves + half
            terms = w_all[deep] * jnp.exp(-r_all[deep] * lag) * own
            lines[place : place + 1, :] = jnp.sum(terms, axis=0, keepdims=True)
    keep = in_sub[1 if transposed else 0]
    for tile in range(groups // PER_TILE):
        for half in range(halves):
            place = tile * halves + half
            line = jnp.broadcast_to(lines[place : place + 1, :], (SUB, LANES))
            rolled = pltpu.roll(line, 0, 1, stride=1, stride_axis=0)
            full = jnp.concatenate([rolled] * BLOCKS, axis=0) * keep
            table[tile * LANES : (tile + 1) * LANES, half * LANES : (half + 1) * LANES] = full.astype(bf16)


def with_before(halo, slot, own, at):
    rows = halo[:, at].astype(f32)[slot * HALO : (slot + 1) * HALO]
    return jnp.concatenate([jnp.concatenate([jnp.zeros_like(rows), rows]).astype(bf16), own[:, at]])


def shifted(table, x):
    return dot(table[...].reshape(-1, table.shape[2])[:, : x.shape[0]], x)


def short_conv(moved_rows, here, taps, index, at):
    total = taps[index, 0:1, at] * here
    for lag in range(1, TAPS):
        total = total + taps[index, lag : lag + 1, at] * moved_rows[(lag - 1) * LANES : lag * LANES]
    return total


def back_conv(before, keep, halo, slot, own, taps, index, at):
    edge = halo[:, at].astype(f32)[slot * HALO : (slot + 1) * HALO]
    ext = jnp.concatenate([jnp.concatenate([jnp.zeros_like(edge), edge]).astype(bf16), own[:, at]])
    far = dot(before[...].reshape(-1, before.shape[2])[ROLLED * LANES :], ext)
    here = own[:, at].astype(f32)
    total = taps[index, 0:1, at] * here
    row = iota(edge.shape, 0)
    copies = here.shape[1] // LANES
    for lag in range(1, TAPS):
        if lag <= ROLLED:
            part = pltpu.roll(here, lag, 0)
            head = jnp.where(row < lag, pltpu.roll(edge, lag, 0), part[:HALO])
            part = jnp.concatenate([head, part[HALO:]]) * jnp.concatenate([keep[lag - 1]] * copies, axis=1)
        else:
            part = far[(lag - 1 - ROLLED) * LANES : (lag - ROLLED) * LANES]
        total = total + taps[index, lag : lag + 1, at] * part
    return total


def keys_values(k, v, halo, taps, before, keep, e_tab, mixed, ks_out, vs_out, s_out, s_msg):
    modes = s_out.shape[0]
    own = own_group(modes)
    for at in each_tile(k.shape[1], 2 * LANES):
        ks = back_conv(before, keep, halo, 0, k, taps, 1, at)
        vs = back_conv(before, keep, halo, 1, v, taps, 2, at)
        ks_out[:, at] = ks
        vs_out[:, at] = vs
        mixed[:, at] = (ks * vs).astype(bf16)
    for at in each_tile(k.shape[1]):
        state = pick_rows(dot(e_tab[at, :], mixed[:, at]), own)
        s_out[:, at] = state
        s_msg[:, at] = state.astype(bf16)


def queries_short(q, halo, taps, before, qs_out):
    for at in each_tile(q.shape[1], 2 * LANES):
        qs_out[:, at] = short_conv(shifted(before, with_before(halo, 2, q, at)), q[:, at].astype(f32), taps, 0, at)


def lane_masks_bf16():
    return [jnp.where(m, 1.0, 0.0).astype(bf16) for m in own_group()]


def across_blocks(x, gather, spread, w, carry, own, masks, forward):
    block_of = iota((1, LANES), 1) // SUB
    inner = range(BLOCKS - 1) if forward else range(1, BLOCKS)
    picks = [gather * jnp.where(block_of == b, 1.0, 0.0).astype(bf16) for b in inner]
    full = dot(jnp.concatenate(picks, axis=0), x)
    parts = [pick_rows(full[i * LANES : (i + 1) * LANES], own) for i in range(BLOCKS - 1)]
    zero = jnp.zeros((SUB, LANES), f32)
    out = [zero] * BLOCKS
    total = None
    for i in range(BLOCKS - 1) if forward else range(BLOCKS - 2, -1, -1):
        total = parts[i] if total is None else parts[i] + total * (carry * masks[i - forward])
        to = i + 1 if forward else i
        high, low = split(spread_rows(total * w, own))
        lhs = spread[to * SUB : (to + 1) * SUB]
        out[to] = dot(jnp.concatenate([lhs, lhs], axis=1), jnp.concatenate([high, low], axis=0))
    return jnp.concatenate(out, axis=0)


def apply_filter(forward, table, gather, spread, w, sub_pass, factors, x, out):
    modes = w.shape[0]
    own_b = [m[:SUB] for m in lane_masks_bf16()]
    own = own_group(modes)
    first = factors.shape[0] - 2 * (BLOCKS - 1)
    masks = [factors[first + 2 * b + 1 : first + 2 * b + 2, :] for b in range(BLOCKS - 1)]
    for at in each_tile(x.shape[1]):
        part = x[:, at]
        near = []
        for block in range(BLOCKS):
            rows = slice(block * SUB, (block + 1) * SUB)
            stacked = jnp.concatenate([part[rows] * m for m in own_b], axis=0)
            near.append(dot(table[at.start + block * SUB : at.start + (block + 1) * SUB, :], stacked))
        carry = sub_pass[:, at]
        far = across_blocks(part, gather[at, :], spread[at, :], w[:, at], carry, own, masks, forward)
        out[:, at] = jnp.concatenate(near, axis=0) + far


def joined(near, parts, at):
    total = near[:, at]
    for factor, message in zip(parts[0::2], parts[1::2]):
        total = total + factor[:, at] * message[:, at].astype(f32)
    return total


def gate(parts, within, near, *refs):
    links, (w, c_tab, qs, up, gain, conv_out, state_out, sums) = refs[:parts], refs[parts:]
    modes = near.shape[0]
    own = own_group(modes)
    squares = dots = jnp.zeros((LANES, LANES), f32)
    for at in each_tile(qs.shape[1]):
        state = joined(near, links, at)
        state_out[:, at] = state
        carried = spread_rows(state * w[:, at], own).astype(bf16)
        conv = within[:, at] + dot(c_tab[at, :], carried)
        conv_out[:, at] = conv
        gated = qs[:, at] * conv
        scaled = up[:, at].astype(f32) * gain[:, at]
        squares = squares + gated * gated
        dots = dots + scaled * gated
    line = lambda total: jnp.sum(total.T, axis=0, keepdims=True)
    sums[...] = jnp.where(iota((HALO, LANES), 0) < 4, line(squares), line(dots))


def norm_columns(sums, width):
    both = sums[...]
    inverse = lax.rsqrt(both[0:1] / width + epsilon)
    slope = inverse * inverse * inverse * both[4:5] / width
    wide = lambda line: jnp.broadcast_to(line, (LANES, LANES)).T
    return wide(inverse), wide(slope)


def grad_conv(width, sums, conv, qs, up, gain, w, c_tab_t, dconv, g_out, g_msg):
    modes = g_out.shape[0]
    own = own_group(modes)
    inverse, slope = norm_columns(sums, width)
    for at in each_tile(qs.shape[1]):
        q = qs[:, at]
        scaled = up[:, at].astype(f32) * gain[:, at]
        d_gated = inverse * scaled - (q * conv[:, at]) * slope
        d = (d_gated * q).astype(bf16)
        dconv[:, at] = d
        u = pick_rows(dot(c_tab_t[at, :], d), own)
        g = u * w[:, at]
        g_out[:, at] = g
        g_msg[:, at] = g.astype(bf16)


def edge_masks(lens, first):
    row = iota((HALO, LANES), 0)
    start = doc_start(lens, first + row)
    out = [None]
    for lag in range(1, TAPS):
        out.append(jnp.where((first + row - lag >= start) & (row < lag), 1.0, 0.0))
    return out


def tap_rows(rows_out, slot, d, x, edge, after, masks, at):
    back = shifted(after, d)
    head = d[:HALO].astype(f32) if d.dtype == f32 else d.astype(f32)[:HALO]
    rows_out[slot : slot + 1, at] = jnp.sum(d.astype(f32) * x, axis=0, keepdims=True)
    for lag in range(1, TAPS):
        prod = back[(lag - 1) * LANES : lag * LANES] * x
        total = prod[:HALO]
        for i in range(HALO, LANES, HALO):
            total = total + prod[i : i + HALO]
        mask = jnp.concatenate([masks[lag]] * (total.shape[1] // LANES), axis=1)
        total = total + head * (pltpu.roll(edge, lag, 0) * mask)
        rows_out[slot + lag : slot + lag + 1, at] = jnp.sum(total, axis=0, keepdims=True)


def query_side(width, sums, conv, qs, up, gain, q, halo, after, edges, out, dqs_out, rows_out):
    masks = edges
    inverse, slope = norm_columns(sums, width)
    for pair in each_tile(q.shape[1], 2 * LANES):
        for at in (slice(pair.start, pair.start + LANES), slice(pair.start + LANES, pair.stop)):
            c = conv[:, at]
            gated = qs[:, at] * c
            upstream = up[:, at].astype(f32)
            d_gated = inverse * (upstream * gain[:, at]) - gated * slope
            normed = gated * inverse
            out[:, at] = (normed * gain[:, at]).astype(bf16)
            dqs_out[:, at] = (d_gated * c).astype(bf16)
            rows_out[TAPS : TAPS + 1, at] = jnp.sum(upstream * normed, axis=0, keepdims=True)
        edge = halo[:, pair].astype(f32)[2 * HALO : 3 * HALO]
        d = dqs_out[:, pair]
        tap_rows(rows_out, 0, d, q[:, pair].astype(f32), edge, after, masks, pair)


def group_members(rate, belongs):
    shape = belongs.shape
    belongs[...] = jnp.where(iota(shape, 0) // GROUP == iota(shape, 1), 1.0, 0.0).astype(bf16)


def group_sums(parts, belongs):
    high, low = split(parts)
    return dot(high, belongs) + dot(low, belongs)


def filter_tables(rate, mixed, state, own_pass, e_tab, late_out, both_out, x_out):
    modes, groups = rate.shape
    lane = iota((LANES, LANES), 1)
    centred = (lane - LANES // 2).astype(f32)
    lag_e = (LANES - 1 - lane).astype(f32)
    own = own_group(modes)
    for tile, at in enumerate(each_tile(mixed.shape[1])):
        r = column_of(rate, tile)
        early = jnp.exp(r * centred)
        late_out[at, :] = jnp.exp(-r * centred).T
        both_out[at, :] = jnp.concatenate([early.T, (early * centred).T], axis=1).astype(bf16)
        x = pick_rows(dot((e_tab[at, :].astype(f32) * lag_e).astype(bf16), mixed[:, at]), own)
        x_out[:, at] = x + own_pass[:, at] * state[:, at]


def filter_grads(start_row, start_col, dconv, mixed, state, late, both, c_tab, q0_out, q1_out, lines):
    modes, groups = q0_out.shape
    row, lane = iota((LANES, LANES), 0), iota((LANES, LANES), 1)
    keep = jnp.where((start_row[...] == start_col[...]) & (lane <= row), 1.0, 0.0)
    centred_row = (row - LANES // 2).astype(f32)
    later = (row + 1).astype(f32)
    own_b = lane_masks_bf16()
    wide = [jnp.concatenate([o, o], axis=1) for o in own_b]
    own = own_group(modes)
    for tile, at in enumerate(each_tile(dconv.shape[1])):
        d, m = dconv[:, at], mixed[:, at]
        stacked = jnp.concatenate([m * o for o in own_b], axis=0)
        outer = dot(d, stacked, NT)
        blocks = [outer[:, k * LANES : (k + 1) * LANES] * keep for k in range(PER_TILE)]
        outer = jnp.concatenate([b.astype(bf16) for b in blocks], axis=1)
        pair = both[at, :]
        met = dot(outer, jnp.concatenate([pair * o for o in wide], axis=0))
        near, near_lag = met[:, :LANES] * late[at, :], met[:, LANES:] * late[at, :]
        far = dot(d, spread_rows(state[:, at], own).astype(bf16), NT) * c_tab[at, :].astype(f32)
        q0 = jnp.sum(near + far, axis=0, keepdims=True)
        q1 = jnp.sum(near * centred_row - near_lag + far * later, axis=0, keepdims=True)
        lines[tile : tile + 1, :] = q0
        lines[groups // PER_TILE + tile : groups // PER_TILE + tile + 1, :] = q1
    pick = jnp.where(iota((modes, LANES), 1) % modes == iota((modes, LANES), 0), 1.0, 0.0).astype(bf16)
    mine = iota((PER_TILE, LANES), 1) // modes == iota((PER_TILE, LANES), 0)
    for begin, out in ((0, q0_out), (groups // PER_TILE, q1_out)):
        parts = [
            jnp.where(mine, jnp.broadcast_to(lines[begin + i : begin + i + 1, :], mine.shape), 0.0)
            for i in range(groups // PER_TILE)
        ]
        high, low = split(jnp.concatenate(parts, axis=0))
        out[...] = dot(pick, high, NT) + dot(pick, low, NT)


def first_grads(parts, near, *refs):
    links, (local, e_tab_t, ks, vs, dqs, later, rows_out) = refs[:parts], refs[parts:]
    own = own_group(near.shape[0])
    rows = 2 * HALO
    for tile, at in enumerate(each_tile(ks.shape[1])):
        g = joined(near, links, at)
        later[:, at] = g
        head = slice(tile * LANES, tile * LANES + rows)
        d_mixed = local[:rows, at] + dot(e_tab_t[head, :], spread_rows(g, own).astype(bf16))
        parts = (dqs[:rows, at].astype(f32), d_mixed * vs[:rows, at], d_mixed * ks[:rows, at])
        rows_out[:, at] = jnp.concatenate([part[:HALO] for part in parts]).astype(bf16)


def grad_keys_values(
    res, rate, later, local, e_tab_t, ks, vs, k, v, halo, q0, q1, x, after, masks, belongs, dks_out, dvs_out, rows_out, flows
):
    modes = later.shape[0]
    own = own_group(modes)
    for at in each_tile(k.shape[1]):
        g = later[:, at]
        flows[:, at] = g * x[:, at]
        d_mixed = local[:, at] + dot(e_tab_t[at, :], spread_rows(g, own).astype(bf16))
        dks_out[:, at] = (d_mixed * vs[:, at]).astype(bf16)
        dvs_out[:, at] = (d_mixed * ks[:, at]).astype(bf16)
    for pair in each_tile(k.shape[1], 2 * LANES):
        edges = halo[:, pair].astype(f32)
        for slot, x_in, d_out in ((0, k, dks_out), (1, v, dvs_out)):
            edge = edges[slot * HALO : (slot + 1) * HALO]
            tap_rows(rows_out, slot * TAPS, d_out[:, pair], x_in[:, pair].astype(f32), edge, after, masks, pair)
    r = rate[...]
    gain = mode_gain(r)
    slope = jnp.exp(-2.0 * r) / gain
    q0_all = q0[...]
    d_res = gain * q0_all
    d_rate = res[...] * (slope * q0_all - gain * q1[...]) - group_sums(flows[...], belongs[...])
    groups = r.shape[1]
    for n in range(modes):
        at = slice(n * groups, (n + 1) * groups)
        rows_out[2 * TAPS : 2 * TAPS + 1, at] = d_res[n : n + 1]
        rows_out[2 * TAPS + 1 : 2 * TAPS + 2, at] = d_rate[n : n + 1]


def grad_inputs(filters, taps, after, edges, *refs):
    owns, outs = refs[: len(filters)], refs[len(filters) :]
    for index, own, out in zip(filters, owns, outs):
        for at in each_tile(own.shape[1], 2 * LANES):
            d = own[:, at]
            edge = edges[:, at].astype(f32)[index * HALO : (index + 1) * HALO]
            edge = jnp.concatenate([edge, jnp.zeros_like(edge)]).astype(bf16)
            moved_rows = shifted(after, jnp.concatenate([d, edge]))
            out[:, at] = short_conv(moved_rows, d.astype(f32), taps, index, at).astype(bf16)


def unpack(rows, *refs):
    others, (taps_out, res_out, rate_out, gain_out) = refs[:-4], refs[-4:]
    modes, groups = res_out.shape
    everything = rows[...].astype(f32) + others[0][...].astype(f32)
    if len(others) > 1:
        everything = everything + (others[1][...].astype(f32) + others[2][...].astype(f32))
    total_q, total = everything[:HALO], everything[HALO:]
    taps_out[0] = total_q[0:TAPS]
    taps_out[1] = total[0:TAPS]
    taps_out[2] = total[TAPS : 2 * TAPS]
    gain_out[...] = total_q[TAPS : TAPS + 1]
    for slot, out in ((2 * TAPS, res_out), (2 * TAPS + 1, rate_out)):
        for n in range(modes):
            out[n : n + 1, :] = total[slot : slot + 1, n * groups : (n + 1) * groups]


def moved(value, axis, steps):
    count = lax.axis_size(axis)
    first, last = max(0, -steps), min(count, count - steps)
    return lax.ppermute(value, axis, [(i, i + steps) for i in range(first, last)])


def swapped(value, axis, bits):
    return lax.ppermute(value, axis, [(i, i ^ bits) for i in range(lax.axis_size(axis))])


def after_all(value, *others):
    return lax.optimization_barrier((value, *others))[0]


def scanned(message, own, passes, beside=()):
    rounds = rounds_of(lax.axis_size("ctx"))
    near, at = None, 0
    for place, (below, meet) in enumerate(rounds):
        got = [swapped(message, "ctx", m << below) for m in range(1, meet)]
        factors, at = passes[at : at + meet - 1], at + meet - 1
        if place + 1 == len(rounds):
            links = [part for pair in zip(factors, got) for part in pair]
            return (jnp.zeros_like(own) if near is None else near), links
        for factor, other in zip(factors, got):
            part = factor * other.astype(f32)
            near = part if near is None else near + part
        own = passes[at] * own
        for factor, other in zip(passes[at + 1 : at + meet], got):
            own = own + factor * other.astype(f32)
        at += meet
        message = after_all(own.astype(bf16), *beside) if beside and not place else own.astype(bf16)


def on_device(q, k, v, taps, res, rate, gain, lens, up):
    rows, channels = q.shape
    groups, modes = rate.shape
    count = lax.axis_size("ctx")
    width = channels * lax.axis_size("ch")
    res, rate = res.T, rate.T
    gain = gain.reshape(1, channels)
    wide = lambda dtype: vmem((rows, channels), dtype)
    state_shape = vmem((modes, channels), f32)
    msg_shape = vmem((modes, channels), bf16)
    table = vmem((channels, LANES), bf16)
    shifts = (TAPS - 1, LANES, LANES + 2 * HALO)

    brought = [k, v, q, up, taps, res, rate, gain]
    last, k, v, q, up, taps, res, rate, gain = call(
        functools.partial(bring_in, len(brought)),
        [vmem((3 * HALO, channels), bf16)] + [vmem(a.shape, a.dtype) for a in brought],
        *brought, hbm=len(brought), name="bring_in",
        scratch=[pltpu.SemaphoreType.DMA((len(brought),))],
    )
    halo = moved(last, "ctx", 1)
    passes_each = pass_count(count)
    square = lambda dtype: vmem((LANES, LANES), dtype)
    e_tab, before, after, start_row, start_col, edges, in_prev, in_sub, factors, weight, back_keep = call(
        functools.partial(first_tables, count),
        [table, vmem(shifts, bf16), vmem(shifts, bf16), square(jnp.int32), square(jnp.int32)]
        + [vmem((TAPS, HALO, LANES), f32), square(f32), vmem((4, LANES, LANES), f32)]
        + [vmem((2 * (1 + 2 * passes_each + BLOCKS - 1), LANES), f32), vmem(res.shape, f32)]
        + [vmem((ROLLED, LANES, LANES), f32)],
        lens, res, rate, smem=1, flops=4 << 20, name="first_tables",
    )
    blocked = [vmem((channels, PER_TILE * SUB), bf16)]
    lines = [pltpu.VMEM((groups // PER_LINE, LANES), f32)]
    near_tab = call(
        functools.partial(block_tables, False), blocked, weight, rate, in_sub, scratch=lines, flops=4 << 20, name="block_tables",
    )[0]
    halo, near_tab = lax.optimization_barrier((halo, near_tab))
    mixed, ks, vs, own_state, state_msg = call(
        keys_values, [wide(bf16), wide(f32), wide(f32), state_shape, msg_shape],
        k, v, halo, taps, before, back_keep, e_tab, flops=64 << 20, name="keys_values",
    )
    c_tab, c_tab_t, e_tab_t, to_end, to_end_t, on, on_t, w, sub_pass, own_pass, *passes = call(
        mode_tables, [table] * 7 + [state_shape] * (3 + 2 * passes_each),
        weight, rate, e_tab, in_prev, in_sub, factors, flops=4 << 20, name="mode_tables",
    )
    qs = call(queries_short, [wide(f32)], q, halo, taps, before, flops=8 << 20, name="queries_short")[0]
    near, links = scanned(state_msg, own_state, passes[:passes_each], (qs,))
    within = call(
        functools.partial(apply_filter, True), [wide(f32)], near_tab, to_end, on, w, sub_pass, factors, mixed,
        flops=256 << 20, name="within",
    )[0]
    belongs = call(
        group_members, [vmem((channels, groups), bf16)], after_all(rate, near), flops=1 << 20, name="group_members",
    )[0]
    within, belongs = lax.optimization_barrier((within, belongs))
    conv, state, sums = call(
        functools.partial(gate, len(links)), [wide(f32), state_shape, vmem((HALO, LANES), f32)],
        within, near, *links, w, c_tab, qs, up, gain, flops=64 << 20, name="gate",
    )
    rate_here = after_all(rate, sums)
    near_tab_t = call(
        functools.partial(block_tables, True), blocked, weight, rate_here, in_sub, scratch=lines, flops=4 << 20, name="block_tables_t",
    )[0]
    late, both, x = call(
        filter_tables, [vmem((channels, LANES), f32), vmem((channels, 2 * LANES), bf16), state_shape],
        rate_here, mixed, state, own_pass, e_tab, flops=64 << 20, name="filter_tables",
    )
    for below, meet in rounds_of(lax.axis_size("ch")):
        got = [swapped(sums, "ch", m << below) for m in range(1, meet)]
        got[0], near_tab_t, late = lax.optimization_barrier((got[0], near_tab_t, late))
        sums = (sums + got[0]) + (got[1] + got[2]) if meet == 4 else sums + got[0]
    dconv, own_grad, grad_msg = call(
        functools.partial(grad_conv, width), [wide(bf16), state_shape, msg_shape],
        sums, conv, qs, up, gain, w, c_tab_t, flops=64 << 20, name="grad_conv",
    )
    out, dqs, rows_q = call(
        functools.partial(query_side, width), [wide(bf16), wide(bf16), vmem((HALO, channels), f32)],
        sums, conv, qs, up, gain, q, halo, after, edges, flops=16 << 20, name="query_side",
    )
    local = call(
        functools.partial(apply_filter, False), [wide(f32)], near_tab_t, on_t, to_end_t, w, sub_pass, factors, dconv,
        flops=256 << 20, name="local_grad",
    )[0]
    near, links = scanned(grad_msg, own_grad, passes[passes_each:], (local, rows_q))
    q0, q1 = call(
        filter_grads, [vmem((modes, groups), f32)] * 2,
        start_row, start_col, dconv, mixed, state, late, both, c_tab,
        scratch=[pltpu.VMEM((2 * groups // PER_TILE, LANES), f32)], flops=512 << 20, name="filter_grads",
    )
    near, q0 = lax.optimization_barrier((near, q0))
    later, first_rows = call(
        functools.partial(first_grads, len(links)), [state_shape, vmem((3 * HALO, channels), bf16)],
        near, *links, local, e_tab_t, ks, vs, dqs, flops=8 << 20, name="first_grads",
    )
    next_rows = moved(first_rows, "ctx", -1)
    dks, dvs, rows_kv = call(
        grad_keys_values, [wide(bf16), wide(bf16), vmem((2 * HALO, channels), f32)],
        res, rate, later, local, e_tab_t, ks, vs, k, v, halo, q0, q1, x, after, edges, belongs,
        scratch=[pltpu.VMEM((modes, channels), f32)], flops=64 << 20, name="grad_keys_values",
    )
    both = jnp.concatenate([rows_q, rows_kv]).astype(bf16)
    d_q = call(
        functools.partial(grad_inputs, (0,)), [wide(bf16)], taps, after, next_rows, dqs,
        flops=24 << 20, name="grad_queries",
    )[0]
    d_k, d_v = call(
        functools.partial(grad_inputs, (1, 2)), [wide(bf16)] * 2, taps, after, next_rows, dks, dvs,
        flops=24 << 20, name="grad_inputs",
    )
    rounds = rounds_of(count)
    for place, (below, meet) in enumerate(rounds):
        got = [swapped(both, "ctx", m << below) for m in range(1, meet)]
        if place + 1 < len(rounds):
            if place == 0:
                got[0], d_q = lax.optimization_barrier((got[0], d_q))
            both, got = both.astype(f32), [part.astype(f32) for part in got]
            both = ((both + got[0]) + (got[1] + got[2]) if meet == 4 else both + got[0]).astype(bf16)
    d_taps, d_res, d_rate, d_gain = call(
        unpack,
        [vmem(taps.shape, f32), vmem(res.shape, f32), vmem(rate.shape, f32), vmem((1, channels), f32)],
        both, *got, name="unpack",
    )
    return out, d_q, d_k, d_v, d_taps, d_res.T, d_rate.T, d_gain.reshape(channels)


def solution(mesh):
    wide = P("ctx", "ch")
    third, table, line = P(None, None, "ch"), P("ch", None), P("ch")
    return jax.shard_map(
        on_device,
        mesh=mesh,
        in_specs=(wide, wide, wide, third, table, table, line, P(), wide),
        out_specs=(wide, wide, wide, wide, third, table, table, line),
        check_vma=False,
    )
```

```python
import functools
import math

import jax
import jax.numpy as jnp
from jax import lax
from jax.experimental import pallas as pl
from jax.experimental.pallas import tpu as pltpu
from jax.sharding import PartitionSpec as P

GROUP = 16
TAPS = 7
HALO = 8
LANES = 128
PER_TILE = LANES // GROUP
SUB = 32
ROLLED = 1
BLOCKS = LANES // SUB
PER_LINE = LANES // SUB
epsilon = 1e-06
f32, bf16 = jnp.float32, jnp.bfloat16
highest = lax.Precision.HIGHEST
NN = (((1,), (0,)), ((), ()))
NT = (((1,), (1,)), ((), ()))


def dot(a, b, dims=NN, precision=None):
    return lax.dot_general(a, b, dims, precision=precision, preferred_element_type=f32)


def iota(shape, dim):
    return lax.broadcasted_iota(jnp.int32, shape, dim)


def docs_at(lens, positions):
    start = jnp.int32(0)
    count = jnp.zeros_like(positions)
    for k in range(lens.shape[0]):
        count = count + jnp.where(positions >= start, 1, 0)
        start = start + lens[k]
    return count - 1


def starts_at(lens):
    out = [jnp.int32(0)]
    for k in range(lens.shape[0] - 1):
        out.append(out[-1] + lens[k])
    return out


def doc_start(lens, positions):
    start = jnp.full_like(positions, 0)
    for s in starts_at(lens)[1:]:
        start = jnp.where(positions >= s, s, start)
    return start


def next_start(lens, positions):
    after = jnp.full_like(positions, jnp.iinfo(jnp.int32).max)
    for s in starts_at(lens)[:0:-1]:
        after = jnp.where(positions < s, s, after)
    return after


def one_minus_exp(x):
    series = x * (1 - x / 2 * (1 - x / 3 * (1 - x / 4 * (1 - x / 5 * (1 - x / 6 * (1 - x / 7))))))
    return jnp.where(x < 0.125, series, 1 - jnp.exp(-x))


def own_group(rows=LANES):
    return [iota((rows, LANES), 1) // GROUP == k for k in range(PER_TILE)]


def spread_rows(per_mode, masks):
    return jnp.concatenate([jnp.where(m, per_mode, 0.0) for m in masks], axis=0)


def pick_rows(full, masks):
    modes = full.shape[0] // PER_TILE
    total = jnp.where(masks[0], full[:modes], 0.0)
    for k in range(1, PER_TILE):
        total = jnp.where(masks[k], full[k * modes : (k + 1) * modes], total)
    return total


def column_of(ref, tile):
    modes = ref.shape[0]
    part = [ref[:, tile * PER_TILE + k : tile * PER_TILE + k + 1] for k in range(PER_TILE)]
    return jnp.concatenate([jnp.broadcast_to(p, (modes, LANES)) for p in part], axis=0)


def mode_gain(rate):
    return jnp.sqrt(one_minus_exp(2.0 * rate))


def each_tile(channels, width=LANES):
    return [slice(i, i + width) for i in range(0, channels, width)]


def vmem(shape, dtype):
    return jax.ShapeDtypeStruct(shape, dtype)


def call(body, outs, *args, smem=0, hbm=0, scratch=(), flops=0, name=None, limit=32):
    moved = sum(a.size * a.dtype.itemsize for a in args) + sum(
        math.prod(o.shape) * o.dtype.itemsize for o in outs
    )
    if hbm:
        args = (*args[:-hbm], *[pltpu.with_memory_space_constraint(a, pltpu.HBM) for a in args[-hbm:]])
        outs = [pltpu.VMEM(o.shape, o.dtype) for o in outs]
    return pl.pallas_call(
        body,
        out_shape=tuple(outs),
        in_specs=[pl.BlockSpec(memory_space=pltpu.SMEM)] * smem
        + [pl.BlockSpec(memory_space=pltpu.VMEM)] * (len(args) - smem - hbm)
        + [pl.BlockSpec(memory_space=pltpu.HBM)] * hbm,
        out_specs=tuple([pl.BlockSpec(memory_space=pltpu.VMEM)] * len(outs)),
        scratch_shapes=list(scratch),
        compiler_params=pltpu.CompilerParams(vmem_limit_bytes=limit << 20),
        cost_estimate=pl.CostEstimate(flops=flops, bytes_accessed=moved, transcendentals=0),
        name=name,
    )(*args)


def bring_in(arrays, *refs):
    sources, out, targets, sems = refs[:arrays], refs[arrays], refs[arrays + 1 : -1], refs[-1]
    copies = [pltpu.make_async_copy(a, b, sems.at[i]) for i, (a, b) in enumerate(zip(sources, targets))]
    for copy in copies:
        copy.start()
    for slot, (copy, ref) in enumerate(zip(copies, targets[:3])):
        copy.wait()
        rows = ref.shape[0]
        tail = ref[rows - 2 * HALO :, :].astype(f32)[HALO:]
        out[slot * HALO : (slot + 1) * HALO, :] = tail.astype(bf16)
    for copy in copies[3:]:
        copy.wait()


def shift_rows(table, lens, first, sign):
    shape = table.shape[1:]
    pos = first + iota((LANES, LANES), 0)
    limit = doc_start(lens, pos) if sign < 0 else next_start(lens, pos)
    limit = jnp.concatenate([limit, limit], axis=1)[:, : shape[1]]
    row, col = iota(shape, 0), iota(shape, 1)
    source = first + col - (2 * HALO if sign < 0 else 0)
    apart = col - row - (2 * HALO if sign < 0 else 0)
    apart = jnp.where(source >= limit if sign < 0 else source < limit, apart * sign, 0)
    for lag in range(1, TAPS):
        table[lag - 1] = jnp.where(apart == lag, 1.0, 0.0).astype(bf16)


def rounds_of(count):
    out, below = [], 0
    while count >> below > 1:
        meet = min(4, count >> below)
        out.append((below, meet))
        below += meet.bit_length() - 1
    return out


def pass_count(count):
    rounds = rounds_of(count)
    return sum(meet - 1 for _, meet in rounds) + sum(meet for _, meet in rounds[:-1])


def pass_factors(lens, me, count, forward):
    ends = lambda device: docs_at(lens, device * LANES + LANES - 1)
    out = []
    rounds = rounds_of(count)
    for place, (below, meet) in enumerate(rounds):
        size, mine = 1 << below, me >> below
        wide = size * meet
        start = (me // wide) * wide
        for m in range(1, meet):
            other = mine ^ m
            if forward:
                edge = other * size + size - 1
                lag, meets, valid = me - 1 - edge, ends(edge) == ends(me - 1), other < mine
            else:
                edge = other * size - 1
                lag, meets, valid = edge - me, ends(edge) == ends(me), other > mine
            out.append((lag, jnp.where(meets & valid, 1.0, 0.0)))
        if place + 1 == len(rounds):
            continue
        for m in range(meet):
            other = mine ^ m
            if forward:
                edge, far = other * size + size - 1, start + wide - 1
                lag = far - edge
            else:
                edge, far = other * size - 1, start - 1
                lag = edge - far
            out.append((lag, jnp.where(ends(edge) == ends(far), 1.0, 0.0)))
    return out


def first_tables(count, lens, res, rate, e_tab, before, after, start_row, start_col, edges, in_prev, in_sub, factors, weight, back_keep):
    me = lax.axis_index("ctx")
    first = me * LANES
    shift_rows(before, lens, first, -1)
    lane = iota((LANES, LANES), 1)
    last = first + LANES - 1
    in_last = jnp.where(docs_at(lens, first + lane) == docs_at(lens, last), 1.0, 0.0)
    lag = (LANES - 1 - lane).astype(f32)
    for tile in range(rate.shape[1] // PER_TILE):
        e = jnp.exp(-column_of(rate, tile) * lag) * in_last
        e_tab[tile * LANES : (tile + 1) * LANES, :] = e.astype(bf16)
    shift_rows(after, lens, first, 1)
    row = first + iota((LANES, LANES), 0)
    start = doc_start(lens, row)
    start_row[...] = start
    start_col[...] = doc_start(lens, first + lane)
    for lag in range(1, ROLLED + 1):
        back_keep[lag - 1] = jnp.where(row - lag >= start, 1.0, 0.0)
    weight[...] = res[...] * mode_gain(rate[...])
    row_in, lane_in = iota((LANES, LANES), 0) % SUB, lane % SUB
    same = doc_start(lens, row - row_in + lane_in) == start
    in_sub[0] = jnp.where(same & (lane_in <= row_in), 1.0, 0.0)
    in_sub[1] = jnp.where(same & (lane_in >= row_in), 1.0, 0.0)
    ends, here = doc_start(lens, first + lane - lane_in + (SUB - 1)), doc_start(lens, first + lane)
    in_sub[2] = jnp.where(ends == here, 1.0, 0.0)
    in_sub[3] = jnp.where((here < first + lane - lane_in) & (lane >= SUB), 1.0, 0.0)
    for lag, mask in enumerate(edge_masks(lens, first)):
        if lag:
            edges[lag] = mask
    doc_prev = docs_at(lens, first - 1)
    in_prev[...] = jnp.where(docs_at(lens, first + lane) == doc_prev, 1.0, 0.0)
    pairs = [(jnp.int32(1), jnp.where(docs_at(lens, last) == doc_prev, float(LANES), 0.0))]
    pairs += pass_factors(lens, me, count, True) + pass_factors(lens, me, count, False)
    ends = [docs_at(lens, first + SUB * block + SUB - 1) for block in range(BLOCKS)]
    blocks = [(jnp.int32(0), jnp.where(a == b, 1.0, 0.0)) for a, b in zip(ends[:-1], ends[1:])]
    pairs += blocks
    for place, (steps, mask) in enumerate(pairs):
        scale = -(jnp.maximum(steps, 0) * LANES).astype(f32)
        factors[2 * place : 2 * place + 1, :] = jnp.full((1, LANES), scale, f32)
        factors[2 * place + 1 : 2 * place + 2, :] = jnp.full((1, LANES), mask, f32)


def mode_tables(
    weight, rate, e_tab, in_prev, in_sub, factors, c_tab, c_tab_t, e_tab_t, to_end, to_end_t, on, on_t, w_out, sub_pass, *passes
):
    modes = rate.shape[0]
    lag = (iota((LANES, LANES), 1) + 1).astype(f32)
    masks = own_group(modes)
    mask, mask_end, mask_on = in_prev[...], in_sub[2], in_sub[3]
    lane_in = iota((LANES, LANES), 1) % SUB
    lag_end, lag_on = (SUB - 1 - lane_in).astype(f32), (lane_in + 1).astype(f32)
    for tile in range(rate.shape[1] // PER_TILE):
        at = slice(tile * LANES, (tile + 1) * LANES)
        r_col = column_of(rate, tile)
        c = jnp.exp(-r_col * lag) * mask
        c_tab_t[at, :] = c.astype(bf16)
        c_tab[at, :] = c.T.astype(bf16)
        e_tab_t[at, :] = e_tab[at, :].astype(f32).T.astype(bf16)
        end = jnp.exp(-r_col * lag_end) * mask_end
        to_end[at, :] = end.astype(bf16)
        to_end_t[at, :] = end.T.astype(bf16)
        on_block = jnp.exp(-r_col * lag_on) * mask_on
        on[at, :] = on_block.T.astype(bf16)
        on_t[at, :] = on_block.astype(bf16)
        r_tile = pick_rows(r_col, masks)
        sub_pass[:, at] = jnp.exp(-r_tile * float(SUB))
        w_out[:, at] = pick_rows(column_of(weight, tile), masks)
        for place, out in enumerate(passes):
            scale, keep = factors[2 * place : 2 * place + 1, :], factors[2 * place + 1 : 2 * place + 2, :]
            out[:, at] = jnp.exp(r_tile * scale) * keep


def split(x):
    high = x.astype(bf16)
    return high, (x - high.astype(f32)).astype(bf16)


def block_tables(transposed, weight, rate, in_sub, table, lines):
    modes, groups = rate.shape
    depth = PER_LINE * modes
    row, lane = iota((depth, LANES), 0) // modes, iota((depth, LANES), 1)
    inside = lane % SUB
    if transposed:
        own, lag = lane // SUB == row, inside
    else:
        back = jnp.where(inside > 0, 1, 0)
        own, lag = (lane // SUB + back) % PER_LINE == row, (SUB - inside) % SUB
    own, lag = jnp.where(own, 1.0, 0.0), lag.astype(f32)
    halves = PER_TILE // PER_LINE
    for tile in range(groups // PER_TILE):
        r_all = column_of(rate, tile)
        w_all = column_of(weight, tile)
        for half in range(halves):
            deep = slice(half * depth, (half + 1) * depth)
            place = tile * halves + half
            terms = w_all[deep] * jnp.exp(-r_all[deep] * lag) * own
            lines[place : place + 1, :] = jnp.sum(terms, axis=0, keepdims=True)
    keep = in_sub[1 if transposed else 0]
    for tile in range(groups // PER_TILE):
        for half in range(halves):
            place = tile * halves + half
            line = jnp.broadcast_to(lines[place : place + 1, :], (SUB, LANES))
            rolled = pltpu.roll(line, 0, 1, stride=1, stride_axis=0)
            full = jnp.concatenate([rolled] * BLOCKS, axis=0) * keep
            table[tile * LANES : (tile + 1) * LANES, half * LANES : (half + 1) * LANES] = full.astype(bf16)


def with_before(halo, slot, own, at):
    rows = halo[:, at].astype(f32)[slot * HALO : (slot + 1) * HALO]
    return jnp.concatenate([jnp.concatenate([jnp.zeros_like(rows), rows]).astype(bf16), own[:, at]])


def shifted(table, x):
    return dot(table[...].reshape(-1, table.shape[2])[:, : x.shape[0]], x)


def short_conv(moved_rows, here, taps, index, at):
    total = taps[index, 0:1, at] * here
    for lag in range(1, TAPS):
        total = total + taps[index, lag : lag + 1, at] * moved_rows[(lag - 1) * LANES : lag * LANES]
    return total


def back_conv(before, keep, halo, slot, own, taps, index, at):
    edge = halo[:, at].astype(f32)[slot * HALO : (slot + 1) * HALO]
    ext = jnp.concatenate([jnp.concatenate([jnp.zeros_like(edge), edge]).astype(bf16), own[:, at]])
    far = dot(before[...].reshape(-1, before.shape[2])[ROLLED * LANES :], ext)
    here = own[:, at].astype(f32)
    total = taps[index, 0:1, at] * here
    row = iota(edge.shape, 0)
    copies = here.shape[1] // LANES
    for lag in range(1, TAPS):
        if lag <= ROLLED:
            part = pltpu.roll(here, lag, 0)
            head = jnp.where(row < lag, pltpu.roll(edge, lag, 0), part[:HALO])
            part = jnp.concatenate([head, part[HALO:]]) * jnp.concatenate([keep[lag - 1]] * copies, axis=1)
        else:
            part = far[(lag - 1 - ROLLED) * LANES : (lag - ROLLED) * LANES]
        total = total + taps[index, lag : lag + 1, at] * part
    return total


def keys_values(k, v, halo, taps, before, keep, e_tab, mixed, ks_out, vs_out, s_out, s_msg):
    modes = s_out.shape[0]
    own = own_group(modes)
    for at in each_tile(k.shape[1], 2 * LANES):
        ks = back_conv(before, keep, halo, 0, k, taps, 1, at)
        vs = back_conv(before, keep, halo, 1, v, taps, 2, at)
        ks_out[:, at] = ks
        vs_out[:, at] = vs
        mixed[:, at] = (ks * vs).astype(bf16)
    for at in each_tile(k.shape[1]):
        state = pick_rows(dot(e_tab[at, :], mixed[:, at]), own)
        s_out[:, at] = state
        s_msg[:, at] = state.astype(bf16)


def queries_short(q, halo, taps, before, qs_out):
    for at in each_tile(q.shape[1], 2 * LANES):
        qs_out[:, at] = short_conv(shifted(before, with_before(halo, 2, q, at)), q[:, at].astype(f32), taps, 0, at)


def lane_masks_bf16():
    return [jnp.where(m, 1.0, 0.0).astype(bf16) for m in own_group()]


def across_blocks(x, gather, spread, w, carry, own, masks, forward):
    block_of = iota((1, LANES), 1) // SUB
    inner = range(BLOCKS - 1) if forward else range(1, BLOCKS)
    picks = [gather * jnp.where(block_of == b, 1.0, 0.0).astype(bf16) for b in inner]
    full = dot(jnp.concatenate(picks, axis=0), x)
    parts = [pick_rows(full[i * LANES : (i + 1) * LANES], own) for i in range(BLOCKS - 1)]
    zero = jnp.zeros((SUB, LANES), f32)
    out = [zero] * BLOCKS
    total = None
    for i in range(BLOCKS - 1) if forward else range(BLOCKS - 2, -1, -1):
        total = parts[i] if total is None else parts[i] + total * (carry * masks[i - forward])
        to = i + 1 if forward else i
        high, low = split(spread_rows(total * w, own))
        lhs = spread[to * SUB : (to + 1) * SUB]
        out[to] = dot(jnp.concatenate([lhs, lhs], axis=1), jnp.concatenate([high, low], axis=0))
    return jnp.concatenate(out, axis=0)


def apply_filter(forward, table, gather, spread, w, sub_pass, factors, x, out):
    modes = w.shape[0]
    own_b = [m[:SUB] for m in lane_masks_bf16()]
    own = own_group(modes)
    first = factors.shape[0] - 2 * (BLOCKS - 1)
    masks = [factors[first + 2 * b + 1 : first + 2 * b + 2, :] for b in range(BLOCKS - 1)]
    for at in each_tile(x.shape[1]):
        part = x[:, at]
        near = []
        for block in range(BLOCKS):
            rows = slice(block * SUB, (block + 1) * SUB)
            stacked = jnp.concatenate([part[rows] * m for m in own_b], axis=0)
            near.append(dot(table[at.start + block * SUB : at.start + (block + 1) * SUB, :], stacked))
        carry = sub_pass[:, at]
        far = across_blocks(part, gather[at, :], spread[at, :], w[:, at], carry, own, masks, forward)
        out[:, at] = jnp.concatenate(near, axis=0) + far


def joined(near, parts, at):
    total = near[:, at]
    for factor, message in zip(parts[0::2], parts[1::2]):
        total = total + factor[:, at] * message[:, at].astype(f32)
    return total


def gate(parts, within, near, *refs):
    links, (w, c_tab, qs, up, gain, conv_out, state_out, sums) = refs[:parts], refs[parts:]
    modes = near.shape[0]
    own = own_group(modes)
    squares = dots = jnp.zeros((LANES, LANES), f32)
    for at in each_tile(qs.shape[1]):
        state = joined(near, links, at)
        state_out[:, at] = state
        carried = spread_rows(state * w[:, at], own).astype(bf16)
        conv = within[:, at] + dot(c_tab[at, :], carried)
        conv_out[:, at] = conv
        gated = qs[:, at] * conv
        scaled = up[:, at].astype(f32) * gain[:, at]
        squares = squares + gated * gated
        dots = dots + scaled * gated
    line = lambda total: jnp.sum(total.T, axis=0, keepdims=True)
    sums[...] = jnp.where(iota((HALO, LANES), 0) < 4, line(squares), line(dots))


def norm_columns(sums, width):
    both = sums[...]
    inverse = lax.rsqrt(both[0:1] / width + epsilon)
    slope = inverse * inverse * inverse * both[4:5] / width
    wide = lambda line: jnp.broadcast_to(line, (LANES, LANES)).T
    return wide(inverse), wide(slope)


def grad_conv(width, sums, conv, qs, up, gain, w, c_tab_t, dconv, g_out, g_msg):
    modes = g_out.shape[0]
    own = own_group(modes)
    inverse, slope = norm_columns(sums, width)
    for at in each_tile(qs.shape[1]):
        q = qs[:, at]
        scaled = up[:, at].astype(f32) * gain[:, at]
        d_gated = inverse * scaled - (q * conv[:, at]) * slope
        d = (d_gated * q).astype(bf16)
        dconv[:, at] = d
        u = pick_rows(dot(c_tab_t[at, :], d), own)
        g = u * w[:, at]
        g_out[:, at] = g
        g_msg[:, at] = g.astype(bf16)


def edge_masks(lens, first):
    row = iota((HALO, LANES), 0)
    start = doc_start(lens, first + row)
    out = [None]
    for lag in range(1, TAPS):
        out.append(jnp.where((first + row - lag >= start) & (row < lag), 1.0, 0.0))
    return out


def tap_rows(rows_out, slot, d, x, edge, after, masks, at):
    back = shifted(after, d)
    head = d[:HALO].astype(f32) if d.dtype == f32 else d.astype(f32)[:HALO]
    rows_out[slot : slot + 1, at] = jnp.sum(d.astype(f32) * x, axis=0, keepdims=True)
    for lag in range(1, TAPS):
        prod = back[(lag - 1) * LANES : lag * LANES] * x
        total = prod[:HALO]
        for i in range(HALO, LANES, HALO):
            total = total + prod[i : i + HALO]
        mask = jnp.concatenate([masks[lag]] * (total.shape[1] // LANES), axis=1)
        total = total + head * (pltpu.roll(edge, lag, 0) * mask)
        rows_out[slot + lag : slot + lag + 1, at] = jnp.sum(total, axis=0, keepdims=True)


def query_side(width, sums, conv, qs, up, gain, q, halo, after, edges, out, dqs_out, rows_out):
    masks = edges
    inverse, slope = norm_columns(sums, width)
    for pair in each_tile(q.shape[1], 2 * LANES):
        for at in (slice(pair.start, pair.start + LANES), slice(pair.start + LANES, pair.stop)):
            c = conv[:, at]
            gated = qs[:, at] * c
            upstream = up[:, at].astype(f32)
            d_gated = inverse * (upstream * gain[:, at]) - gated * slope
            normed = gated * inverse
            out[:, at] = (normed * gain[:, at]).astype(bf16)
            dqs_out[:, at] = (d_gated * c).astype(bf16)
            rows_out[TAPS : TAPS + 1, at] = jnp.sum(upstream * normed, axis=0, keepdims=True)
        edge = halo[:, pair].astype(f32)[2 * HALO : 3 * HALO]
        d = dqs_out[:, pair]
        tap_rows(rows_out, 0, d, q[:, pair].astype(f32), edge, after, masks, pair)


def group_members(rate, belongs):
    shape = belongs.shape
    belongs[...] = jnp.where(iota(shape, 0) // GROUP == iota(shape, 1), 1.0, 0.0).astype(bf16)


def group_sums(parts, belongs):
    high, low = split(parts)
    return dot(high, belongs) + dot(low, belongs)


def filter_tables(rate, mixed, state, own_pass, e_tab, late_out, both_out, x_out):
    modes, groups = rate.shape
    lane = iota((LANES, LANES), 1)
    centred = (lane - LANES // 2).astype(f32)
    lag_e = (LANES - 1 - lane).astype(f32)
    own = own_group(modes)
    for tile, at in enumerate(each_tile(mixed.shape[1])):
        r = column_of(rate, tile)
        early = jnp.exp(r * centred)
        late_out[at, :] = jnp.exp(-r * centred).T
        both_out[at, :] = jnp.concatenate([early.T, (early * centred).T], axis=1).astype(bf16)
        x = pick_rows(dot((e_tab[at, :].astype(f32) * lag_e).astype(bf16), mixed[:, at]), own)
        x_out[:, at] = x + own_pass[:, at] * state[:, at]


def filter_grads(start_row, start_col, dconv, mixed, state, late, both, c_tab, q0_out, q1_out, lines):
    modes, groups = q0_out.shape
    row, lane = iota((LANES, LANES), 0), iota((LANES, LANES), 1)
    keep = jnp.where((start_row[...] == start_col[...]) & (lane <= row), 1.0, 0.0)
    centred_row = (row - LANES // 2).astype(f32)
    later = (row + 1).astype(f32)
    own_b = lane_masks_bf16()
    wide = [jnp.concatenate([o, o], axis=1) for o in own_b]
    own = own_group(modes)
    for tile, at in enumerate(each_tile(dconv.shape[1])):
        d, m = dconv[:, at], mixed[:, at]
        stacked = jnp.concatenate([m * o for o in own_b], axis=0)
        outer = dot(d, stacked, NT)
        blocks = [outer[:, k * LANES : (k + 1) * LANES] * keep for k in range(PER_TILE)]
        outer = jnp.concatenate([b.astype(bf16) for b in blocks], axis=1)
        pair = both[at, :]
        met = dot(outer, jnp.concatenate([pair * o for o in wide], axis=0))
        near, near_lag = met[:, :LANES] * late[at, :], met[:, LANES:] * late[at, :]
        far = dot(d, spread_rows(state[:, at], own).astype(bf16), NT) * c_tab[at, :].astype(f32)
        q0 = jnp.sum(near + far, axis=0, keepdims=True)
        q1 = jnp.sum(near * centred_row - near_lag + far * later, axis=0, keepdims=True)
        lines[tile : tile + 1, :] = q0
        lines[groups // PER_TILE + tile : groups // PER_TILE + tile + 1, :] = q1
    pick = jnp.where(iota((modes, LANES), 1) % modes == iota((modes, LANES), 0), 1.0, 0.0).astype(bf16)
    mine = iota((PER_TILE, LANES), 1) // modes == iota((PER_TILE, LANES), 0)
    for begin, out in ((0, q0_out), (groups // PER_TILE, q1_out)):
        parts = [
            jnp.where(mine, jnp.broadcast_to(lines[begin + i : begin + i + 1, :], mine.shape), 0.0)
            for i in range(groups // PER_TILE)
        ]
        high, low = split(jnp.concatenate(parts, axis=0))
        out[...] = dot(pick, high, NT) + dot(pick, low, NT)


def first_grads(parts, near, *refs):
    links, (local, e_tab_t, ks, vs, dqs, later, rows_out) = refs[:parts], refs[parts:]
    own = own_group(near.shape[0])
    rows = 2 * HALO
    for tile, at in enumerate(each_tile(ks.shape[1])):
        g = joined(near, links, at)
        later[:, at] = g
        head = slice(tile * LANES, tile * LANES + rows)
        d_mixed = local[:rows, at] + dot(e_tab_t[head, :], spread_rows(g, own).astype(bf16))
        parts = (dqs[:rows, at].astype(f32), d_mixed * vs[:rows, at], d_mixed * ks[:rows, at])
        rows_out[:, at] = jnp.concatenate([part[:HALO] for part in parts]).astype(bf16)


def grad_keys_values(
    res, rate, later, local, e_tab_t, ks, vs, k, v, halo, q0, q1, x, after, masks, belongs, dks_out, dvs_out, rows_out, flows
):
    modes = later.shape[0]
    own = own_group(modes)
    for at in each_tile(k.shape[1]):
        g = later[:, at]
        flows[:, at] = g * x[:, at]
        d_mixed = local[:, at] + dot(e_tab_t[at, :], spread_rows(g, own).astype(bf16))
        dks_out[:, at] = (d_mixed * vs[:, at]).astype(bf16)
        dvs_out[:, at] = (d_mixed * ks[:, at]).astype(bf16)
    for pair in each_tile(k.shape[1], 2 * LANES):
        edges = halo[:, pair].astype(f32)
        for slot, x_in, d_out in ((0, k, dks_out), (1, v, dvs_out)):
            edge = edges[slot * HALO : (slot + 1) * HALO]
            tap_rows(rows_out, slot * TAPS, d_out[:, pair], x_in[:, pair].astype(f32), edge, after, masks, pair)
    r = rate[...]
    gain = mode_gain(r)
    slope = jnp.exp(-2.0 * r) / gain
    q0_all = q0[...]
    d_res = gain * q0_all
    d_rate = res[...] * (slope * q0_all - gain * q1[...]) - group_sums(flows[...], belongs[...])
    groups = r.shape[1]
    for n in range(modes):
        at = slice(n * groups, (n + 1) * groups)
        rows_out[2 * TAPS : 2 * TAPS + 1, at] = d_res[n : n + 1]
        rows_out[2 * TAPS + 1 : 2 * TAPS + 2, at] = d_rate[n : n + 1]


def grad_inputs(filters, taps, after, edges, *refs):
    owns, outs = refs[: len(filters)], refs[len(filters) :]
    for index, own, out in zip(filters, owns, outs):
        for at in each_tile(own.shape[1], 2 * LANES):
            d = own[:, at]
            edge = edges[:, at].astype(f32)[index * HALO : (index + 1) * HALO]
            edge = jnp.concatenate([edge, jnp.zeros_like(edge)]).astype(bf16)
            moved_rows = shifted(after, jnp.concatenate([d, edge]))
            out[:, at] = short_conv(moved_rows, d.astype(f32), taps, index, at).astype(bf16)


def unpack(rows, *refs):
    others, (taps_out, res_out, rate_out, gain_out) = refs[:-4], refs[-4:]
    modes, groups = res_out.shape
    everything = rows[...].astype(f32) + others[0][...].astype(f32)
    if len(others) > 1:
        everything = everything + (others[1][...].astype(f32) + others[2][...].astype(f32))
    total_q, total = everything[:HALO], everything[HALO:]
    taps_out[0] = total_q[0:TAPS]
    taps_out[1] = total[0:TAPS]
    taps_out[2] = total[TAPS : 2 * TAPS]
    gain_out[...] = total_q[TAPS : TAPS + 1]
    for slot, out in ((2 * TAPS, res_out), (2 * TAPS + 1, rate_out)):
        for n in range(modes):
            out[n : n + 1, :] = total[slot : slot + 1, n * groups : (n + 1) * groups]


def moved(value, axis, steps):
    count = lax.axis_size(axis)
    first, last = max(0, -steps), min(count, count - steps)
    return lax.ppermute(value, axis, [(i, i + steps) for i in range(first, last)])


def swapped(value, axis, bits):
    return lax.ppermute(value, axis, [(i, i ^ bits) for i in range(lax.axis_size(axis))])


def after_all(value, *others):
    return lax.optimization_barrier((value, *others))[0]


def scanned(message, own, passes, beside=()):
    rounds = rounds_of(lax.axis_size("ctx"))
    near, at = None, 0
    for place, (below, meet) in enumerate(rounds):
        got = [swapped(message, "ctx", m << below) for m in range(1, meet)]
        factors, at = passes[at : at + meet - 1], at + meet - 1
        if place + 1 == len(rounds):
            links = [part for pair in zip(factors, got) for part in pair]
            return (jnp.zeros_like(own) if near is None else near), links
        for factor, other in zip(factors, got):
            part = factor * other.astype(f32)
            near = part if near is None else near + part
        own = passes[at] * own
        for factor, other in zip(passes[at + 1 : at + meet], got):
            own = own + factor * other.astype(f32)
        at += meet
        message = after_all(own.astype(bf16), *beside) if beside and not place else own.astype(bf16)


def on_device(q, k, v, taps, res, rate, gain, lens, up):
    rows, channels = q.shape
    groups, modes = rate.shape
    count = lax.axis_size("ctx")
    width = channels * lax.axis_size("ch")
    res, rate = res.T, rate.T
    gain = gain.reshape(1, channels)
    wide = lambda dtype: vmem((rows, channels), dtype)
    state_shape = vmem((modes, channels), f32)
    msg_shape = vmem((modes, channels), bf16)
    table = vmem((channels, LANES), bf16)
    shifts = (TAPS - 1, LANES, LANES + 2 * HALO)

    brought = [k, v, q, up, taps, res, rate, gain]
    last, k, v, q, up, taps, res, rate, gain = call(
        functools.partial(bring_in, len(brought)),
        [vmem((3 * HALO, channels), bf16)] + [vmem(a.shape, a.dtype) for a in brought],
        *brought, hbm=len(brought), name="bring_in",
        scratch=[pltpu.SemaphoreType.DMA((len(brought),))],
    )
    halo = moved(last, "ctx", 1)
    passes_each = pass_count(count)
    square = lambda dtype: vmem((LANES, LANES), dtype)
    e_tab, before, after, start_row, start_col, edges, in_prev, in_sub, factors, weight, back_keep = call(
        functools.partial(first_tables, count),
        [table, vmem(shifts, bf16), vmem(shifts, bf16), square(jnp.int32), square(jnp.int32)]
        + [vmem((TAPS, HALO, LANES), f32), square(f32), vmem((4, LANES, LANES), f32)]
        + [vmem((2 * (1 + 2 * passes_each + BLOCKS - 1), LANES), f32), vmem(res.shape, f32)]
        + [vmem((ROLLED, LANES, LANES), f32)],
        lens, res, rate, smem=1, flops=4 << 20, name="first_tables",
    )
    blocked = [vmem((channels, PER_TILE * SUB), bf16)]
    lines = [pltpu.VMEM((groups // PER_LINE, LANES), f32)]
    near_tab = call(
        functools.partial(block_tables, False), blocked, weight, rate, in_sub, scratch=lines, flops=4 << 20, name="block_tables",
    )[0]
    halo, near_tab = lax.optimization_barrier((halo, near_tab))
    mixed, ks, vs, own_state, state_msg = call(
        keys_values, [wide(bf16), wide(f32), wide(f32), state_shape, msg_shape],
        k, v, halo, taps, before, back_keep, e_tab, flops=64 << 20, name="keys_values",
    )
    c_tab, c_tab_t, e_tab_t, to_end, to_end_t, on, on_t, w, sub_pass, own_pass, *passes = call(
        mode_tables, [table] * 7 + [state_shape] * (3 + 2 * passes_each),
        weight, rate, e_tab, in_prev, in_sub, factors, flops=4 << 20, name="mode_tables",
    )
    qs = call(queries_short, [wide(f32)], q, halo, taps, before, flops=8 << 20, name="queries_short")[0]
    near, links = scanned(state_msg, own_state, passes[:passes_each], (qs,))
    within = call(
        functools.partial(apply_filter, True), [wide(f32)], near_tab, to_end, on, w, sub_pass, factors, mixed,
        flops=256 << 20, name="within",
    )[0]
    belongs = call(
        group_members, [vmem((channels, groups), bf16)], after_all(rate, near), flops=1 << 20, name="group_members",
    )[0]
    within, belongs = lax.optimization_barrier((within, belongs))
    conv, state, sums = call(
        functools.partial(gate, len(links)), [wide(f32), state_shape, vmem((HALO, LANES), f32)],
        within, near, *links, w, c_tab, qs, up, gain, flops=64 << 20, name="gate",
    )
    rate_here = after_all(rate, sums)
    near_tab_t = call(
        functools.partial(block_tables, True), blocked, weight, rate_here, in_sub, scratch=lines, flops=4 << 20, name="block_tables_t",
    )[0]
    late, both, x = call(
        filter_tables, [vmem((channels, LANES), f32), vmem((channels, 2 * LANES), bf16), state_shape],
        rate_here, mixed, state, own_pass, e_tab, flops=64 << 20, name="filter_tables",
    )
    for below, meet in [(bit, 2) for bit in range(lax.axis_size("ch").bit_length() - 1)]:
        got = [swapped(sums, "ch", m << below) for m in range(1, meet)]
        if below:
            got[0], late = lax.optimization_barrier((got[0], late))
        else:
            got[0], near_tab_t = lax.optimization_barrier((got[0], near_tab_t))
        sums = (sums + got[0]) + (got[1] + got[2]) if meet == 4 else sums + got[0]
    dconv, own_grad, grad_msg = call(
        functools.partial(grad_conv, width), [wide(bf16), state_shape, msg_shape],
        sums, conv, qs, up, gain, w, c_tab_t, flops=64 << 20, name="grad_conv",
    )
    out, dqs, rows_q = call(
        functools.partial(query_side, width), [wide(bf16), wide(bf16), vmem((HALO, channels), f32)],
        sums, conv, qs, up, gain, q, halo, after, edges, flops=16 << 20, name="query_side",
    )
    local = call(
        functools.partial(apply_filter, False), [wide(f32)], near_tab_t, on_t, to_end_t, w, sub_pass, factors, dconv,
        flops=256 << 20, name="local_grad",
    )[0]
    near, links = scanned(grad_msg, own_grad, passes[passes_each:], (local, rows_q))
    q0, q1 = call(
        filter_grads, [vmem((modes, groups), f32)] * 2,
        start_row, start_col, dconv, mixed, state, late, both, c_tab,
        scratch=[pltpu.VMEM((2 * groups // PER_TILE, LANES), f32)], flops=512 << 20, name="filter_grads",
    )
    near, q0 = lax.optimization_barrier((near, q0))
    later, first_rows = call(
        functools.partial(first_grads, len(links)), [state_shape, vmem((3 * HALO, channels), bf16)],
        near, *links, local, e_tab_t, ks, vs, dqs, flops=8 << 20, name="first_grads",
    )
    next_rows = moved(first_rows, "ctx", -1)
    dks, dvs, rows_kv = call(
        grad_keys_values, [wide(bf16), wide(bf16), vmem((2 * HALO, channels), f32)],
        res, rate, later, local, e_tab_t, ks, vs, k, v, halo, q0, q1, x, after, edges, belongs,
        scratch=[pltpu.VMEM((modes, channels), f32)], flops=64 << 20, name="grad_keys_values",
    )
    both = jnp.concatenate([rows_q, rows_kv]).astype(bf16)
    d_q = call(
        functools.partial(grad_inputs, (0,)), [wide(bf16)], taps, after, next_rows, dqs,
        flops=24 << 20, name="grad_queries",
    )[0]
    d_k, d_v = call(
        functools.partial(grad_inputs, (1, 2)), [wide(bf16)] * 2, taps, after, next_rows, dks, dvs,
        flops=24 << 20, name="grad_inputs",
    )
    rounds = rounds_of(count)
    for place, (below, meet) in enumerate(rounds):
        got = [swapped(both, "ctx", m << below) for m in range(1, meet)]
        if place + 1 < len(rounds):
            if place == 0:
                got[0], d_q = lax.optimization_barrier((got[0], d_q))
            both, got = both.astype(f32), [part.astype(f32) for part in got]
            both = ((both + got[0]) + (got[1] + got[2]) if meet == 4 else both + got[0]).astype(bf16)
    d_taps, d_res, d_rate, d_gain = call(
        unpack,
        [vmem(taps.shape, f32), vmem(res.shape, f32), vmem(rate.shape, f32), vmem((1, channels), f32)],
        both, *got, name="unpack",
    )
    return out, d_q, d_k, d_v, d_taps, d_res.T, d_rate.T, d_gain.reshape(channels)


def solution(mesh):
    wide = P("ctx", "ch")
    third, table, line = P(None, None, "ch"), P("ch", None), P("ch")
    return jax.shard_map(
        on_device,
        mesh=mesh,
        in_specs=(wide, wide, wide, third, table, table, line, P(), wide),
        out_specs=(wide, wide, wide, wide, third, table, table, line),
        check_vma=False,
    )
```
